256 devices in a mesh: ctx: 32 (over z, y), head: 8 (over x, core).
Axes of the slice: x: 4, y: 4, z: 8, core: 2. Of those that a mesh axis runs over, the one named last changes fastest.
Arguments:
- queries: bfloat16 [16384, 2048], P('ctx', 'head'), may hold values from -6 to 6
- key_vec: bfloat16 [16384, 2048], P('ctx', 'head'), may hold values from -6 to 6
- values: bfloat16 [16384, 4096], P('ctx', 'head'), may hold values from -6 to 6
- out_gate: bfloat16 [16384, 4096], P('ctx', 'head'), may hold values from -6 to 6
- beta_logit: float32 [32, 16384], P('head', 'ctx'), may hold values from -6 to 6
- decay_gate: float32 [32, 16384], P('head', 'ctx'), may hold values from 0 to 196608, as said below
- decay_exp: int32 [32], P('head'), may hold values from -4 to 9, as said below
- norm_gain: float32 [128], replicated, may hold values from 0.25 to 1.75
- out_weight: bfloat16 [4096, 2048], P('head'), may hold values from -0.09375 to 0.09375
- router_weight: bfloat16 [2048, 512], replicated, may hold values from -0.75 to 0.75
- old_scores: int32 [16384, 512], P(('ctx', 'head')), may hold values from -8192 to 8192
Outputs:
- layer_out: bfloat16 [16384, 2048], P(('ctx', 'head'))
- divergence: float32 [16384], P(('ctx', 'head'))
The draws below stay inside these ranges and needn't reach their ends.
Inputs may be any that keep to these rules, and one draw needn't show every extreme that they name: `decay_exp`: every whole number from min to max is the exponent of some head. `decay_gate`: positive.
All inputs are finite; a program needn't handle non-finite values.
Results may differ from the reference program's by a relative error of at most 0.005.
Values may be sent and summed in bfloat16 or wider, within the bound.
A program may use at most 128 MiB of HBM per device.

```python
import jax
import jax.numpy as jnp
from jax import lax

DMODEL = 2048
KEY_HEADS = 16
VALUE_HEADS = 32
KEY_DIM = 128
VALUE_DIM = 128
EXPERTS = 512
BLOCK_LEN = 64
TOKENS = 16384


def shared_exponents(key):
    order = jax.random.permutation(key, VALUE_HEADS)
    return (order % 14 - 4).astype(jnp.int32)


def draw_decay_exp(key, part):
    exponents = shared_exponents(key)
    return exponents


def draw_beta_logit(key, part):
    exponents = shared_exponents(key)
    key = jax.random.fold_in(key, 31)
    first_key, second_key = jax.random.split(key)
    drawn = jnp.clip(1.5 * jax.random.normal(first_key, (VALUE_HEADS, TOKENS)), -6.0, 6.0)
    faint = jax.random.uniform(second_key, (VALUE_HEADS, TOKENS), minval=-5.5, maxval=-4.0)
    chosen = (exponents <= 1)[:, None]
    return jnp.where(chosen, faint, drawn)


def draw_decay_gate(key, part):
    exponents = shared_exponents(key).astype(jnp.float32)
    key = jax.random.fold_in(key, 23)
    first_key, second_key, third_key = jax.random.split(key, 3)
    base = jnp.exp(jax.random.uniform(first_key, (VALUE_HEADS, TOKENS), minval=-1.0, maxval=1.0))
    places = jax.random.randint(second_key, (VALUE_HEADS, 4), 0, TOKENS)
    losses = jax.random.uniform(third_key, (VALUE_HEADS, 4), minval=0.2, maxval=0.5)
    strength = -jnp.log(1.0 - losses) * TOKENS * jnp.exp2(-exponents)[:, None]
    hits = jnp.arange(TOKENS)[None, None, :] == places[:, :, None]
    extra = jnp.sum(jnp.where(hits, strength[:, :, None], 0.0), axis=1)
    return base + extra


def plant(result, own_key, smallest, largest):
    spot = [jax.random.randint(jax.random.fold_in(own_key, axis), (), 0, length) for axis, length in enumerate(result.shape)]
    widest = result.shape.index(max(result.shape))
    neighbour = spot[:widest] + [(spot[widest] + 1) % result.shape[widest]] + spot[widest + 1:]
    return result.at[tuple(spot)].set(smallest).at[tuple(neighbour)].set(largest)


def block_scale(key, extent, pieces, smallest, top_value):
    factor_of, own = 1.0, jax.random.fold_in(key, 6)
    for dim, shards_of in pieces:
        steps = jnp.exp(jax.random.uniform(jax.random.fold_in(own, dim), (shards_of,), jnp.float32, smallest / len(pieces), top_value / len(pieces)))
        factor_of = factor_of * jnp.repeat(steps, extent[dim] // shards_of).reshape([-1 if axis == dim else 1 for axis in range(len(extent))])
    return factor_of


def scatter_about(rng, shape, deviation, limit, shards=(), kind=jnp.bfloat16):
    loudness = block_scale(rng, shape, shards, -0.22, 0.18) if shards else 1.0
    drawn = jax.random.normal(rng, shape, jnp.float32) * deviation * loudness
    return jnp.minimum(jnp.maximum(drawn, -limit), limit).astype(kind)


def setup_inputs(seed: int = 0) -> dict:
    arg_keys = jax.random.split(jax.random.key(seed), 12)
    queries = scatter_about(arg_keys[0], (TOKENS, KEY_HEADS * KEY_DIM), 1.0, 6.0, ((0, 32), (1, 8)))
    key_vec = scatter_about(arg_keys[1], (TOKENS, KEY_HEADS * KEY_DIM), 1.0, 6.0, ((0, 32), (1, 8)))
    values = scatter_about(arg_keys[2], (TOKENS, VALUE_HEADS * VALUE_DIM), 1.0, 6.0, ((0, 32), (1, 8)))
    out_gate = scatter_about(arg_keys[3], (TOKENS, VALUE_HEADS * VALUE_DIM), 1.0, 6.0, ((0, 32), (1, 8)))
    beta_logit = draw_beta_logit(jax.random.fold_in(arg_keys[11], 71), 0)
    decay_gate = draw_decay_gate(jax.random.fold_in(arg_keys[11], 71), 0)
    decay_exp = draw_decay_exp(jax.random.fold_in(arg_keys[11], 71), 0)
    norm_gain = jnp.clip(1.0 + 0.15 * jax.random.normal(arg_keys[7], (VALUE_DIM,), jnp.float32), 0.25, 1.75)
    out_weight = scatter_about(arg_keys[8], (VALUE_HEADS * VALUE_DIM, DMODEL), (VALUE_HEADS * VALUE_DIM) ** -0.5, 0.09375, ((0, 8),))
    router_weight = scatter_about(arg_keys[9], (DMODEL, EXPERTS), (DMODEL // 36) ** -0.5, 0.75)
    old_scores = plant(jax.random.randint(arg_keys[10], (TOKENS, EXPERTS), -8192, 8193), jax.random.fold_in(arg_keys[10], 1), -8192, 8192).astype(jnp.int32)
    return dict(queries=queries, key_vec=key_vec, values=values, out_gate=out_gate, beta_logit=beta_logit, decay_gate=decay_gate, decay_exp=decay_exp, norm_gain=norm_gain, out_weight=out_weight, router_weight=router_weight, old_scores=old_scores)


epsilon = 1e-06
highest = lax.Precision.HIGHEST

def product_matrix(pattern, first_op, second_op):
    return jnp.einsum(pattern, first_op, second_op, precision=highest)

def prepare(queries, key_vec, values, beta_logit, decay_gate, decay_exp, chain_length):
    token_count = queries.shape[0]
    query_heads = queries.astype(jnp.float32).reshape(token_count, -1, KEY_DIM)
    key_heads = key_vec.astype(jnp.float32).reshape(token_count, -1, KEY_DIM)
    unit_query = query_heads / jnp.sqrt(lax.optimization_barrier(jnp.sum(query_heads * query_heads, -1, keepdims=True)) + epsilon) / KEY_DIM ** 0.5
    unit_key = key_heads / jnp.sqrt(lax.optimization_barrier(jnp.sum(key_heads * key_heads, -1, keepdims=True)) + epsilon)
    unit_query = jnp.repeat(unit_query, 2, axis=1)
    unit_key = jnp.repeat(unit_key, 2, axis=1)
    head_count = unit_query.shape[1]
    blocks = token_count // BLOCK_LEN
    value_heads = values.astype(jnp.float32).reshape(token_count, head_count, VALUE_DIM)

    def arrange(tensor):
        return tensor.reshape(blocks, BLOCK_LEN, head_count, -1).transpose(2, 0, 1, 3)
    beta = jax.nn.sigmoid(beta_logit).reshape(head_count, blocks, BLOCK_LEN)
    rate = jnp.exp2(decay_exp.astype(jnp.float32)) / chain_length
    log_decay = (-rate[:, None] * decay_gate).reshape(head_count, blocks, BLOCK_LEN)
    return (arrange(unit_query), arrange(unit_key), arrange(value_heads), beta, log_decay)

def block_pass(query_blocks, key_blocks, value_blocks, beta, log_decay, keep_map):
    head_count = query_blocks.shape[0]
    block_len = query_blocks.shape[2]
    value_width = value_blocks.shape[-1]
    key_width = key_blocks.shape[-1]
    position = jnp.arange(block_len)
    strict = position[:, None] > position[None, :]
    inclusive = position[:, None] >= position[None, :]

    def advance(carry, inputs):
        memory_state, propagator = carry
        current_query, key_now, value_now, beta_now, decay_now = inputs
        cumulative = jnp.cumsum(decay_now, axis=-1)
        growth_factor = jnp.exp(cumulative)
        fade = jnp.exp(jnp.minimum(cumulative[:, :, None] - cumulative[:, None, :], 0.0))
        key_gram = product_matrix('hid,hjd->hij', key_now, key_now)
        system = jnp.eye(block_len, dtype=jnp.float32) + beta_now[:, :, None] * jnp.where(strict, key_gram * fade, 0.0)
        right_side = jnp.concatenate([beta_now[..., None] * value_now, (beta_now * growth_factor)[..., None] * key_now], axis=-1)
        solved = jax.scipy.linalg.solve_triangular(system, right_side, lower=True, unit_diagonal=True)
        written_values = solved[..., :value_width]
        widened_keys = solved[..., value_width:]
        score_matrix = jnp.where(inclusive, product_matrix('hid,hjd->hij', current_query, key_now) * fade, 0.0)
        key_remainder = jnp.exp(cumulative[:, -1:] - cumulative)[..., None] * key_now
        final_growth = growth_factor[:, -1][:, None, None]
        fresh_values = written_values - product_matrix('pjz,pzw->pjw', widened_keys, memory_state)
        current_output = growth_factor[..., None] * product_matrix('pjz,pzw->pjw', current_query, memory_state) + product_matrix('gxd,gdk->gxk', score_matrix, fresh_values)
        updated_memory = final_growth * memory_state + product_matrix('pgy,pgq->pyq', key_remainder, fresh_values)
        if keep_map:
            leading = growth_factor[..., None] * current_query - product_matrix('hij,hjk->hik', score_matrix, widened_keys)
            carried_state = product_matrix('hck,hkm->hcm', leading, propagator)
            new_propagator = final_growth * propagator - product_matrix('hck,hcm->hkm', key_remainder, product_matrix('hck,hkm->hcm', widened_keys, propagator))
            return ((updated_memory, new_propagator), (current_output, carried_state))
        return ((updated_memory, propagator), current_output)
    start_memory = jnp.zeros((head_count, key_width, value_width), jnp.float32)
    start_map = jnp.broadcast_to(jnp.eye(key_width, dtype=jnp.float32), (head_count, key_width, key_width))
    sequence = tuple((jnp.moveaxis(tensor, 1, 0) for tensor in (query_blocks, key_blocks, value_blocks, beta, log_decay)))
    return lax.scan(advance, (start_memory, start_map), sequence)

def finish(attended, out_gate, norm_gain):
    token_count, head_count = (attended.shape[0], attended.shape[1])
    gate_heads = out_gate.astype(jnp.float32).reshape(token_count, head_count, VALUE_DIM)
    scale = lax.rsqrt(lax.optimization_barrier(jnp.mean(attended * attended, -1, keepdims=True)) + epsilon)
    normed = attended * scale * norm_gain * jax.nn.silu(gate_heads)
    return normed.astype(jnp.bfloat16).reshape(token_count, head_count * VALUE_DIM)

def router_divergence(layer_out, router_weight, old_scores):
    new_logit = jnp.dot(layer_out.astype(jnp.float32), router_weight.astype(jnp.float32), preferred_element_type=jnp.float32)
    new_logp = new_logit - jnp.log(lax.optimization_barrier(jnp.sum(jnp.exp(new_logit), -1, keepdims=True)))
    old_logit = old_scores.astype(jnp.float32) / 1024.0
    old_logp = old_logit - jnp.log(lax.optimization_barrier(jnp.sum(jnp.exp(old_logit), -1, keepdims=True)))
    return lax.optimization_barrier(jnp.sum(jnp.exp(old_logp) * (old_logp - new_logp), -1))

def reference(queries, key_vec, values, out_gate, beta_logit, decay_gate, decay_exp, norm_gain, out_weight, router_weight, old_scores):
    prepared = prepare(queries, key_vec, values, beta_logit, decay_gate, decay_exp, TOKENS)
    final_carry, output_rows = block_pass(*prepared, False)
    head_count = output_rows.shape[1]
    attended = output_rows.transpose(0, 2, 1, 3).reshape(TOKENS, head_count, VALUE_DIM)
    normed = finish(attended, out_gate, norm_gain)
    layer_out = jnp.dot(normed.astype(jnp.float32), out_weight.astype(jnp.float32), preferred_element_type=jnp.float32).astype(jnp.bfloat16)
    return (layer_out, router_divergence(layer_out, router_weight, old_scores))
```

```python
import functools

import jax
import jax.numpy as jnp
from jax import lax
from jax.experimental import pallas as pl
from jax.experimental.pallas import tpu as pltpu
from jax.sharding import PartitionSpec as P

F32 = jnp.float32
BF16 = jnp.bfloat16
L = 128
EPS = 1e-6


def mm(a, b):
    return jnp.dot(a, b, preferred_element_type=F32)


def split(x):
    hi = x.astype(BF16)
    return hi, (x - hi.astype(F32)).astype(BF16)


def mm_wide(a, b):
    ah, al = split(a)
    bh, bl = split(b)
    row = jnp.concatenate([bh, bl], axis=1)
    r = mm(jnp.concatenate([ah, al], axis=1), jnp.concatenate([row, row], axis=0))
    n = b.shape[1]
    return r[:, :n] + r[:, n:]


def mm_three(a, b):
    ah, al = split(a)
    bh, bl = split(b)
    return mm(jnp.concatenate([ah, al, ah], axis=1), jnp.concatenate([bh, bh, bl], axis=0))


def mm_exact_right(a, b16):
    ah, al = split(a)
    return mm(jnp.concatenate([ah, al], axis=1), jnp.concatenate([b16, b16], axis=0))


def odd_rows(x, s):
    if s == 64:
        return x[64:]
    return jnp.concatenate([x[i : i + s] for i in range(s, L, 2 * s)], axis=0)


def weave(even, odd, s):
    parts = []
    for n, i in enumerate(range(0, L, 2 * s)):
        parts += [even[i : i + s], odd[n * s : (n + 1) * s]]
    return jnp.concatenate(parts, axis=0)


def unit_lower_inverse(systems):
    lane16 = lax.broadcasted_iota(jnp.int32, (16, L), 1)
    row16 = lax.broadcasted_iota(jnp.int32, (16, L), 0)
    place = lane16 // 16
    bands = []
    for a in systems:
        band = jnp.zeros((16, L), F32)
        for b in range(L // 16):
            band = jnp.where(place == b, a[16 * b : 16 * b + 16], band)
        bands.append(band)
    start = jnp.where(lane16 % 16 == row16, 1.0, 0.0).astype(F32)
    solved = [start for _ in systems]
    for m in range(15):
        index = place * 16 + m
        spread = [jnp.take_along_axis(band, index, axis=1) for band in bands]
        solved = [r - s * r[m : m + 1] for r, s in zip(solved, spread)]
    row = lax.broadcasted_iota(jnp.int32, (L, L), 0)
    lane = lax.broadcasted_iota(jnp.int32, (L, L), 1)
    same = row // 16 == lane // 16
    inverses = [jnp.where(same, jnp.concatenate([r] * (L // 16), axis=0), 0.0) for r in solved]
    for s in (16, 32, 64):
        below = odd_rows(row // s, s) == odd_rows(lane // s, s) + 1
        zeros = jnp.zeros((L, L), F32)
        lower = [mm_wide(jnp.where(below, odd_rows(a, s), 0.0), t) for a, t in zip(systems, inverses)]
        full = [weave(zeros, y, s) for y in lower]
        odd = [odd_rows(t, s) for t in inverses]
        change = [mm_wide(o, f) for o, f in zip(odd, full)]
        inverses = [weave(t, o - c, s) for t, o, c in zip(inverses, odd, change)]
    return inverses


def decay_columns(de_ref, bl_ref, dg_ref):
    row = lax.broadcasted_iota(jnp.int32, (8, 512), 0)
    lane = lax.broadcasted_iota(jnp.int32, (8, 512), 1) % L
    exponent = jnp.zeros((8, 512), jnp.int32)
    for h in range(4):
        exponent = jnp.where(row % 4 == h, de_ref[h], exponent)
    rate = jnp.exp2(exponent.astype(F32)) / 16384.0
    gate = jnp.concatenate([dg_ref[...]] * 2, axis=0)
    logit = jnp.concatenate([bl_ref[...]] * 2, axis=0)
    beta = jax.nn.sigmoid(logit)
    cum = -rate * gate
    for s in (1, 2, 4, 8, 16, 32, 64):
        cum = cum + jnp.where(lane >= s, pltpu.roll(cum, s, 1), 0.0)
    last = jnp.concatenate(
        [jnp.broadcast_to(cum[:, L * b + L - 1 : L * b + L], (8, L)) for b in range(4)], axis=1
    )
    growth = jnp.exp(cum)
    remain = jnp.exp(last - cum)
    final = jnp.exp(last)
    pieces = []
    for quantity in (cum, beta, growth, remain):
        pieces += [quantity[:, L * b : L * b + L] for b in range(4)]
    columns = jnp.concatenate(pieces, axis=0).T
    return cum, beta, growth, final, columns


def local_kernel(de_ref, q_ref, k_ref, v_ref, bl_ref, dg_ref, x_ref, out_ref, lead_s, pu_s, b_s, d_s):
    cum, beta, growth, final, columns = decay_columns(de_ref, bl_ref, dg_ref)

    def column(quantity, b, h):
        i = quantity * 32 + b * 8 + h
        return columns[:, i : i + 1]

    row = lax.broadcasted_iota(jnp.int32, (L, L), 0)
    lane = lax.broadcasted_iota(jnp.int32, (L, L), 1)
    strict = row > lane
    inclusive = row >= lane
    eye = jnp.where(row == lane, 1.0, 0.0).astype(F32)

    key_norm, query_norm = {}, {}
    table = jnp.zeros((L, L), F32)
    for b in range(4):
        for kh in range(2):
            key = k_ref[L * b : L * b + L, L * kh : L * kh + L].astype(F32)
            query = q_ref[L * b : L * b + L, L * kh : L * kh + L].astype(F32)
            rk = lax.rsqrt(jnp.sum(key * key, axis=1, keepdims=True) + EPS)
            rq = lax.rsqrt(jnp.sum(query * query, axis=1, keepdims=True) + EPS) * (L**-0.5)
            key_norm[b, kh], query_norm[b, kh] = rk, rq
            table = jnp.where(lane == 2 * b + kh, rk, table)
    key_rows = table.T

    for b in range(4):
        tokens = slice(L * b, L * b + L)
        systems, scores, keys, keys_t, queries, vals = [], [], [], [], [], []
        for kh in range(2):
            key = k_ref[tokens, L * kh : L * kh + L]
            query = q_ref[tokens, L * kh : L * kh + L]
            key_t = key.T
            gram = mm(jnp.concatenate([query, key], axis=0), key_t)
            rk, rq = key_norm[b, kh], query_norm[b, kh]
            rk_row = key_rows[2 * b + kh : 2 * b + kh + 1]
            qk = gram[:L] * rk_row
            kk = gram[L:] * rk_row
            for h in (2 * kh, 2 * kh + 1):
                cum_row = cum[h : h + 1, tokens]
                fade = jnp.exp(jnp.minimum(column(0, b, h) - cum_row, 0.0))
                systems.append(jnp.where(strict, kk * (rk * column(1, b, h)) * fade, 0.0))
                scores.append(jnp.where(inclusive, qk * rq * fade, 0.0))
                keys.append(key)
                keys_t.append(key_t)
                queries.append(query)
                vals.append(v_ref[tokens, L * h : L * h + L])
        inverses = unit_lower_inverse(systems)
        for h in range(4):
            rk_row = key_rows[2 * b + h // 2 : 2 * b + h // 2 + 1]
            rk, rq = key_norm[b, h // 2], query_norm[b, h // 2]
            t1 = inverses[h] * beta[h : h + 1, tokens]
            r1 = mm_wide(scores[h], t1)
            both = jnp.concatenate([t1, r1], axis=0)
            written = mm_exact_right(both, vals[h])
            widened = mm_exact_right(both * (growth[h : h + 1, tokens] * rk_row), keys[h])
            pu_s[4 * b + h] = written[L:]
            lead_s[4 * b + h] = queries[h].astype(F32) * (column(2, b, h) * rq) - widened[L:]
            rem = column(3, b, h) * rk
            wu = jnp.concatenate([written[:L] * rem, widened[:L] * rem], axis=1)
            wh, wl = split(wu)
            kt = keys_t[h]
            change = mm(jnp.concatenate([kt, kt], axis=1), jnp.concatenate([wh, wl], axis=0))
            d_s[4 * b + h] = change[:, :L]
            b_s[4 * b + h] = eye * final[h : h + 1, tokens] - change[:, L:]

    zero = jnp.zeros((L, L), F32)
    state = [jnp.concatenate([d_s[h], b_s[h]], axis=1) for h in range(4)]
    for h in range(4):
        out_ref[h, 0:L, :] = jnp.concatenate([pu_s[h], lead_s[h]], axis=1)
    for b in range(1, 4):
        for h in range(4):
            out_ref[h, L * b : L * b + L, :] = mm_three(lead_s[4 * b + h], state[h]) + jnp.concatenate(
                [pu_s[4 * b + h], zero], axis=1
            )
        state = [
            mm_three(b_s[4 * b + h], state[h]) + jnp.concatenate([d_s[4 * b + h], zero], axis=1)
            for h in range(4)
        ]
    for h in range(4):
        x_ref[h] = state[h]


def local_part(queries, key_vec, values, beta_logit, decay_gate, decay_exp):
    vm = pl.BlockSpec(memory_space=pltpu.VMEM)
    return pl.pallas_call(
        local_kernel,
        out_shape=(
            jax.ShapeDtypeStruct((4, L, 2 * L), F32),
            jax.ShapeDtypeStruct((4, 512, 2 * L), F32),
        ),
        in_specs=[pl.BlockSpec(memory_space=pltpu.SMEM)] + [vm] * 5,
        out_specs=(vm, vm),
        scratch_shapes=[pltpu.VMEM((16, L, L), F32)] * 4,
        compiler_params=pltpu.CompilerParams(vmem_limit_bytes=48 * 1024 * 1024),
    )(decay_exp, queries, key_vec, values, beta_logit, decay_gate)


MESH_Y = 4


def to_ctx(ctx):
    return {"ctx": ctx}


def to_head(head):
    return {"head": head}


def exchange_kernel(nz, x_ref, sin_ref, gath, zbox, total, prefix, acc, outbox, landed, s1, r1, s2, r2, s3, r3):
    me = lax.axis_index("ctx")
    z, y = me // MESH_Y, lax.rem(me, MESH_Y)
    in_group = [z * MESH_Y + lax.rem(y + d, MESH_Y) for d in range(1, MESH_Y)]

    barrier = pltpu.get_barrier_semaphore()
    for other in in_group:
        pl.semaphore_signal(barrier, inc=1, device_id=to_ctx(other), device_id_type=pl.DeviceIdType.MESH)
    for d in range(1, nz):
        other = lax.rem(z + d, nz) * MESH_Y + y
        pl.semaphore_signal(barrier, inc=1, device_id=to_ctx(other), device_id_type=pl.DeviceIdType.MESH)
    pl.semaphore_wait(barrier, MESH_Y - 1 + nz - 1)

    firsts = []
    for d in range(1, MESH_Y):
        copy = pltpu.make_async_remote_copy(
            src_ref=x_ref.at[lax.rem(y + d, MESH_Y)],
            dst_ref=gath.at[y],
            send_sem=s1.at[d - 1],
            recv_sem=r1.at[d - 1],
            device_id=to_ctx(in_group[d - 1]),
            device_id_type=pl.DeviceIdType.MESH,
        )
        copy.start()
        firsts.append(copy)
    gath[y] = x_ref[y]
    for copy in firsts:
        copy.wait_recv()

    zero = jnp.zeros((L, L), F32)
    state = gath[0]
    for j in range(1, MESH_Y):
        prefix[j - 1] = state
        now = gath[j]
        state = mm_three(now[:, L:], state) + jnp.concatenate([now[:, :L], zero], axis=1)
    total[...] = state

    def z_copy(d):
        return pltpu.make_async_remote_copy(
            src_ref=total,
            dst_ref=zbox.at[z],
            send_sem=s2.at[d - 1],
            recv_sem=r2.at[d - 1],
            device_id=to_ctx(lax.rem(z + d, nz) * MESH_Y + y),
            device_id_type=pl.DeviceIdType.MESH,
        )

    for d in range(1, nz):

        @pl.when(z + d < nz)
        def _():
            z_copy(d).start()

    acc[...] = jnp.zeros((L, 2 * L), F32)
    for d in range(1, nz):

        @pl.when(z - d >= 0)
        def _():
            z_copy(d).wait_recv()
            if d == 1:
                acc[...] = zbox[z - d]
            else:
                so_far = acc[...]
                acc[...] = mm_three(so_far[:, L:], zbox[z - d]) + jnp.concatenate([so_far[:, :L], zero], axis=1)

    incoming = acc[:, :L]
    outbox[0] = incoming
    for j in range(1, MESH_Y):
        before = prefix[j - 1]
        outbox[j] = before[:, :L] + mm_three(before[:, L:], incoming)
    lasts = []
    for d in range(1, MESH_Y):
        copy = pltpu.make_async_remote_copy(
            src_ref=outbox.at[lax.rem(y + d, MESH_Y)],
            dst_ref=landed.at[y],
            send_sem=s3.at[d - 1],
            recv_sem=r3.at[d - 1],
            device_id=to_ctx(in_group[d - 1]),
            device_id_type=pl.DeviceIdType.MESH,
        )
        copy.start()
        lasts.append(copy)
    landed[y] = outbox[y]
    for copy in lasts:
        copy.wait_recv()
    sin_ref[...] = landed[...]
    for copy in firsts + lasts:
        copy.wait_send()
    for d in range(1, nz):

        @pl.when(z + d < nz)
        def _():
            z_copy(d).wait_send()


def exchange(x, nz):
    vm = pl.BlockSpec(memory_space=pltpu.VMEM)
    square = (MESH_Y, L, L)
    return pl.pallas_call(
        functools.partial(exchange_kernel, nz),
        out_shape=jax.ShapeDtypeStruct(square, F32),
        in_specs=[vm],
        out_specs=vm,
        scratch_shapes=[
            pltpu.VMEM((MESH_Y, L, 2 * L), F32),
            pltpu.VMEM((nz, L, 2 * L), F32),
            pltpu.VMEM((L, 2 * L), F32),
            pltpu.VMEM((MESH_Y - 1, L, 2 * L), F32),
            pltpu.VMEM((L, 2 * L), F32),
            pltpu.VMEM(square, F32),
            pltpu.VMEM(square, F32),
        ]
        + [pltpu.SemaphoreType.DMA((MESH_Y - 1,))] * 2
        + [pltpu.SemaphoreType.DMA((nz - 1,))] * 2
        + [pltpu.SemaphoreType.DMA((MESH_Y - 1,))] * 2,
        compiler_params=pltpu.CompilerParams(
            collective_id=0, has_side_effects=True, vmem_limit_bytes=24 * 1024 * 1024
        ),
    )(x)


MESH_X = 4
ROWS = 64
WIDE = 2048
HALF = WIDE // 2


def project_kernel(
    out_ref, sin_ref, gate_ref, gain_ref, w_ref, router_ref, old_ref, lo_ref, div_ref,
    normed, own, cores, corebox, ring1, box1, ring2, box2, sc, rc, s1, r1, s2, r2,
):
    me = lax.axis_index("head")
    x, c = me // 2, lax.rem(me, 2)
    right = lax.rem(x + 1, MESH_X) * 2 + c
    left = lax.rem(x + MESH_X - 1, MESH_X) * 2 + c
    twin = x * 2 + 1 - c

    barrier = pltpu.get_barrier_semaphore()
    for other in (right, left, twin):
        pl.semaphore_signal(barrier, inc=1, device_id=to_head(other), device_id_type=pl.DeviceIdType.MESH)
    pl.semaphore_wait(barrier, 3)

    def send(src, dst, ssem, rsem, head):
        copy = pltpu.make_async_remote_copy(
            src_ref=src, dst_ref=dst, send_sem=ssem, recv_sem=rsem,
            device_id=to_head(head), device_id_type=pl.DeviceIdType.MESH,
        )
        copy.start()
        return copy

    order = [lax.rem(x + d, MESH_X) for d in (2, 1, 3, 0)]
    core_copies = []

    def block(i):
        rows = pl.ds(pl.multiple_of(order[i] * L, L), L)
        parts = []
        for h in range(4):
            o = out_ref[h, rows, :]
            attended = o[:, :L] + mm_three(o[:, L:], sin_ref[h])
            scale = lax.rsqrt(jnp.mean(attended * attended, axis=1, keepdims=True) + EPS)
            gate = gate_ref[rows, L * h : L * h + L].astype(F32)
            parts.append((attended * scale * gain_ref[...] * (gate / (1.0 + jnp.exp(-gate)))).astype(BF16))
        normed[...] = jnp.concatenate(parts, axis=1)
        mine = normed[pl.ds(pl.multiple_of(c * ROWS, ROWS), ROWS), :]
        other = normed[pl.ds(pl.multiple_of((1 - c) * ROWS, ROWS), ROWS), :]
        both = jnp.concatenate([mine, other], axis=0)
        for n in range(4):
            cols = slice(512 * n, 512 * n + 512)
            partial = mm(both, w_ref[:, cols])
            own[i, :, cols] = partial[:ROWS]
            cores[i, :, cols] = partial[ROWS:].astype(BF16)
        core_copies.append(send(cores.at[i], corebox.at[i], sc.at[i], rc.at[i], twin))

    def pair_sum(i):
        core_copies[i].wait_recv()
        return own[i] + corebox[i].astype(F32)

    block(0)
    block(1)
    total = pair_sum(0)
    ring1[0] = total[:, :HALF].astype(BF16)
    ring1[1] = total[:, HALF:].astype(BF16)
    first = [
        send(ring1.at[0], box1.at[0], s1.at[0], r1.at[0], right),
        send(ring1.at[1], box1.at[1], s1.at[1], r1.at[1], left),
    ]
    block(2)
    block(3)
    total = pair_sum(1)
    first[0].wait_recv()
    ring2[0, :, :HALF] = (total[:, :HALF] + box1[0].astype(F32)).astype(BF16)
    ring2[0, :, HALF:] = total[:, HALF:].astype(BF16)
    second = [send(ring2.at[0], box2.at[0], s2.at[0], r2.at[0], right)]
    total = pair_sum(2)
    first[1].wait_recv()
    ring2[1, :, :HALF] = total[:, :HALF].astype(BF16)
    ring2[1, :, HALF:] = (total[:, HALF:] + box1[1].astype(F32)).astype(BF16)
    second.append(send(ring2.at[1], box2.at[1], s2.at[1], r2.at[1], left))

    old_logit = old_ref[...].astype(F32) / 1024.0
    old_logp = old_logit - jnp.log(jnp.sum(jnp.exp(old_logit), axis=1, keepdims=True))
    old_prob = jnp.exp(old_logp)

    total = pair_sum(3)
    for copy in second:
        copy.wait_recv()
    layer_out = (total + box2[0].astype(F32) + box2[1].astype(F32)).astype(BF16)
    lo_ref[...] = layer_out
    new_logit = mm(layer_out, router_ref[...])
    new_logp = new_logit - jnp.log(jnp.sum(jnp.exp(new_logit), axis=1, keepdims=True))
    div = jnp.sum(old_prob * (old_logp - new_logp), axis=1, keepdims=True)
    div_ref[...] = jnp.broadcast_to(div, (ROWS, L)).T[0:1, :]
    for copy in core_copies + first + second:
        copy.wait_send()


def project(outs, sin, gate, gain, w, router, old):
    vm = pl.BlockSpec(memory_space=pltpu.VMEM)
    return pl.pallas_call(
        project_kernel,
        out_shape=(
            jax.ShapeDtypeStruct((ROWS, WIDE), BF16),
            jax.ShapeDtypeStruct((1, ROWS), F32),
        ),
        in_specs=[vm] * 7,
        out_specs=(vm, vm),
        scratch_shapes=[
            pltpu.VMEM((L, 512), BF16),
            pltpu.VMEM((4, ROWS, WIDE), F32),
            pltpu.VMEM((4, ROWS, WIDE), BF16),
            pltpu.VMEM((4, ROWS, WIDE), BF16),
            pltpu.VMEM((2, ROWS, HALF), BF16),
            pltpu.VMEM((2, ROWS, HALF), BF16),
            pltpu.VMEM((2, ROWS, WIDE), BF16),
            pltpu.VMEM((2, ROWS, WIDE), BF16),
            pltpu.SemaphoreType.DMA((4,)),
            pltpu.SemaphoreType.DMA((4,)),
            pltpu.SemaphoreType.DMA((2,)),
            pltpu.SemaphoreType.DMA((2,)),
            pltpu.SemaphoreType.DMA((2,)),
            pltpu.SemaphoreType.DMA((2,)),
        ],
        compiler_params=pltpu.CompilerParams(
            collective_id=1, has_side_effects=True, vmem_limit_bytes=40 * 1024 * 1024
        ),
    )(outs, sin, gate, gain, w, router, old)


def solution(mesh):
    nz = mesh.shape["ctx"] // MESH_Y

    def local(
        queries, key_vec, values, out_gate, beta_logit, decay_gate, decay_exp,
        norm_gain, out_weight, router_weight, old_scores,
    ):
        x, outs = local_part(queries, key_vec, values, beta_logit, decay_gate, decay_exp)
        sin = exchange(x, nz)
        layer_out, div = project(
            outs, sin, out_gate, norm_gain.reshape(1, L), out_weight, router_weight, old_scores
        )
        return layer_out, div.reshape(ROWS)

    placed = (
        P("ctx", "head"), P("ctx", "head"), P("ctx", "head"), P("ctx", "head"), P("head", "ctx"),
        P("head", "ctx"), P("head"), P(), P("head", None), P(), P(("ctx", "head"), None),
    )
    return jax.shard_map(
        local,
        mesh=mesh,
        in_specs=placed,
        out_specs=(P(("ctx", "head"), None), P(("ctx", "head"))),
        check_vma=False,
    )
```

```python
import functools

import jax
import jax.numpy as jnp
from jax import lax
from jax.experimental import pallas as pl
from jax.experimental.pallas import tpu as pltpu
from jax.sharding import PartitionSpec as P

F32 = jnp.float32
BF16 = jnp.bfloat16
L = 128
EPS = 1e-6


def mm(a, b):
    return jnp.dot(a, b, preferred_element_type=F32)


def split(x):
    hi = x.astype(BF16)
    return hi, (x - hi.astype(F32)).astype(BF16)


def mm_wide(a, b):
    ah, al = split(a)
    bh, bl = split(b)
    row = jnp.concatenate([bh, bl], axis=1)
    r = mm(jnp.concatenate([ah, al], axis=1), jnp.concatenate([row, row], axis=0))
    n = b.shape[1]
    return r[:, :n] + r[:, n:]


def mm_three(a, b):
    ah, al = split(a)
    bh, bl = split(b)
    return mm(jnp.concatenate([ah, al, ah], axis=1), jnp.concatenate([bh, bh, bl], axis=0))


def mm_exact_right(a, b16):
    ah, al = split(a)
    return mm(jnp.concatenate([ah, al], axis=1), jnp.concatenate([b16, b16], axis=0))


def odd_rows(x, s):
    if s == 64:
        return x[64:]
    return jnp.concatenate([x[i : i + s] for i in range(s, L, 2 * s)], axis=0)


def weave(even, odd, s):
    parts = []
    for n, i in enumerate(range(0, L, 2 * s)):
        parts += [even[i : i + s], odd[n * s : (n + 1) * s]]
    return jnp.concatenate(parts, axis=0)


def unit_lower_inverse(systems):
    lane16 = lax.broadcasted_iota(jnp.int32, (16, L), 1)
    row16 = lax.broadcasted_iota(jnp.int32, (16, L), 0)
    place = lane16 // 16
    bands = []
    for a in systems:
        band = jnp.zeros((16, L), F32)
        for b in range(L // 16):
            band = jnp.where(place == b, a[16 * b : 16 * b + 16], band)
        bands.append(band)
    start = jnp.where(lane16 % 16 == row16, 1.0, 0.0).astype(F32)
    solved = [start for _ in systems]
    for m in range(15):
        index = place * 16 + m
        spread = [jnp.take_along_axis(band, index, axis=1) for band in bands]
        solved = [r - s * r[m : m + 1] for r, s in zip(solved, spread)]
    row = lax.broadcasted_iota(jnp.int32, (L, L), 0)
    lane = lax.broadcasted_iota(jnp.int32, (L, L), 1)
    same = row // 16 == lane // 16
    inverses = [jnp.where(same, jnp.concatenate([r] * (L // 16), axis=0), 0.0) for r in solved]
    for s in (16, 32, 64):
        below = odd_rows(row // s, s) == odd_rows(lane // s, s) + 1
        zeros = jnp.zeros((L, L), F32)
        lower = [mm_wide(jnp.where(below, odd_rows(a, s), 0.0), t) for a, t in zip(systems, inverses)]
        full = [weave(zeros, y, s) for y in lower]
        odd = [odd_rows(t, s) for t in inverses]
        change = [mm_wide(o, f) for o, f in zip(odd, full)]
        inverses = [weave(t, o - c, s) for t, o, c in zip(inverses, odd, change)]
    return inverses


ROWS = 64
WIDE = 2048
HALF = WIDE // 2
MESH_X = 4
MESH_Y = 4
QUAD = 4
PACK = L + 16


def to_ctx(ctx):
    return {"ctx": ctx}


def to_head(head):
    return {"head": head}


def signal(semaphore, device):
    pl.semaphore_signal(semaphore, inc=1, device_id=device, device_id_type=pl.DeviceIdType.MESH)


def remote(src, dst, send_sem, recv_sem, device):
    return pltpu.make_async_remote_copy(
        src_ref=src, dst_ref=dst, send_sem=send_sem, recv_sem=recv_sem,
        device_id=device, device_id_type=pl.DeviceIdType.MESH,
    )


def iotas():
    return lax.broadcasted_iota(jnp.int32, (L, L), 0), lax.broadcasted_iota(jnp.int32, (L, L), 1)


def decay_tables(de_ref, bl_ref, dg_ref, rows_s, cols_s):
    row = lax.broadcasted_iota(jnp.int32, (8, 512), 0)
    lane = lax.broadcasted_iota(jnp.int32, (8, 512), 1) % L
    exponent = jnp.zeros((8, 512), jnp.int32)
    for h in range(4):
        exponent = jnp.where(row % 4 == h, de_ref[h], exponent)
    rate = jnp.exp2(exponent.astype(F32)) / 16384.0
    gate = jnp.concatenate([dg_ref[...]] * 2, axis=0)
    beta = jax.nn.sigmoid(jnp.concatenate([bl_ref[...]] * 2, axis=0))
    cum = -rate * gate
    for s in (1, 2, 4, 8, 16, 32, 64):
        cum = cum + jnp.where(lane >= s, pltpu.roll(cum, s, 1), 0.0)
    growth = jnp.exp(cum)
    for b in range(4):
        tokens = slice(L * b, L * b + L)
        now = cum[:, tokens]
        last = jnp.broadcast_to(now[:, L - 1 : L], (8, L))
        parts = [now, beta[:, tokens], growth[:, tokens]]
        rows_s[b] = jnp.concatenate(parts + [jnp.exp(last)], axis=0)
        padding = [jnp.zeros((L - 32, L), F32)]
        cols_s[b] = jnp.concatenate(parts + [jnp.exp(last - now)] + padding, axis=0).T


def solve_block(b, q_ref, k_ref, v_ref, rows_s, cols_s, t1_s, score_s, b_s, d_s):
    row, lane = iotas()
    tokens = pl.ds(pl.multiple_of(b * L, L), L)
    rows, columns = rows_s[b], cols_s[b]
    systems, keys, norms = [], [], []
    table = jnp.zeros((L, L), F32)
    for kh in range(2):
        key = k_ref[tokens, L * kh : L * kh + L]
        query = q_ref[tokens, L * kh : L * kh + L]
        key32, query32 = key.astype(F32), query.astype(F32)
        rk = lax.rsqrt(jnp.sum(key32 * key32, axis=1, keepdims=True) + EPS)
        rq = lax.rsqrt(jnp.sum(query32 * query32, axis=1, keepdims=True) + EPS) * (L**-0.5)
        table = jnp.where(lane == kh, rk, table)
        columns = jnp.where(lane == 32 + kh, rq, columns)
        norms.append((rk, rq))
        keys.append((key, query))
    cols_s[b] = columns
    key_rows = table.T
    for kh in range(2):
        key, query = keys[kh]
        rk, rq = norms[kh]
        rk_row = key_rows[kh : kh + 1]
        key_t = key.T
        gram = mm(jnp.concatenate([query, key], axis=0), key_t)
        qk, kk = gram[:L] * rk_row, gram[L:] * rk_row
        keys[kh] = (key, key_t)
        for h in (2 * kh, 2 * kh + 1):
            fade = jnp.exp(jnp.minimum(columns[:, h : h + 1] - rows[h : h + 1], 0.0))
            systems.append(jnp.where(row > lane, kk * (rk * columns[:, 8 + h : 9 + h]) * fade, 0.0))
            score_s[4 * b + h] = jnp.where(row >= lane, qk * rq * fade, 0.0)
    inverses = unit_lower_inverse(systems)
    eye = jnp.where(row == lane, 1.0, 0.0).astype(F32)
    for h in range(4):
        kh = h // 2
        key, key_t = keys[kh]
        t1 = inverses[h] * rows[8 + h : 9 + h]
        t1_s[4 * b + h] = t1
        reach = rows[16 + h : 17 + h] * key_rows[kh : kh + 1]
        rows_s[b, 4 + h : 5 + h] = reach
        written = mm_exact_right(t1, v_ref[tokens, L * h : L * h + L])
        widened = mm_exact_right(t1 * reach, key)
        rem = columns[:, 24 + h : 25 + h] * norms[kh][0]
        wh, wl = split(jnp.concatenate([written * rem, widened * rem], axis=1))
        change = mm(jnp.concatenate([key_t, key_t], axis=1), jnp.concatenate([wh, wl], axis=0))
        d_s[4 * b + h] = change[:, :L]
        b_s[4 * b + h] = eye * rows[24 + h : 25 + h] - change[:, L:]


def output_block(b, q_ref, k_ref, v_ref, rows_s, cols_s, t1_s, score_s, state_s, out_s):
    tokens = pl.ds(pl.multiple_of(b * L, L), L)
    rows, columns = rows_s[b], cols_s[b]
    zero = jnp.zeros((L, L), F32)
    for h in range(4):
        kh = h // 2
        r1 = mm_wide(score_s[4 * b + h], t1_s[4 * b + h])
        from_values = mm_exact_right(r1, v_ref[tokens, L * h : L * h + L])
        from_keys = mm_exact_right(r1 * rows[4 + h : 5 + h], k_ref[tokens, L * kh : L * kh + L])
        query = q_ref[tokens, L * kh : L * kh + L].astype(F32)
        lead = query * (columns[:, 16 + h : 17 + h] * columns[:, 32 + kh : 33 + kh]) - from_keys
        out_s[4 * b + h] = mm_three(lead, state_s[4 * b + h]) + jnp.concatenate([from_values, zero], axis=1)


def pack(state):
    row, lane = iotas()
    kept = state.astype(BF16)
    lost = state[:, L:] - kept[:, L:].astype(F32)
    lost = jnp.sum(jnp.where(row == lane, lost, 0.0), axis=0, keepdims=True)
    lost = jnp.broadcast_to(jnp.concatenate([jnp.zeros((1, L), F32), lost], axis=1), (PACK - L, 2 * L))
    return jnp.concatenate([kept, lost.astype(BF16)], axis=0)


def lost_diagonal(packed):
    row, lane = iotas()
    return jnp.where(row == lane, packed[L : L + 1, L:].astype(F32), 0.0)


def unpack(packed):
    state = packed[:L].astype(F32)
    return jnp.concatenate([state[:, :L], state[:, L:] + lost_diagonal(packed)], axis=1)


def after(packed, state):
    m = packed[:L, L:]
    hi, lo = split(state)
    lhs = jnp.concatenate([m, lost_diagonal(packed).astype(BF16), m], axis=1)
    moved = mm(lhs, jnp.concatenate([hi, hi, lo], axis=0))
    return moved + jnp.concatenate([packed[:L, :L].astype(F32), jnp.zeros((L, L), F32)], axis=1)


def before(state, packed):
    hi, lo = split(state[:, L:])
    lost = jnp.concatenate([jnp.zeros((L, L), F32), lost_diagonal(packed)], axis=1).astype(BF16)
    moved = mm(
        jnp.concatenate([hi, lo, hi], axis=1), jnp.concatenate([packed[:L], packed[:L], lost], axis=0)
    )
    return moved + jnp.concatenate([state[:, :L], jnp.zeros((L, L), F32)], axis=1)


def layer_kernel(
    nz,
    de_ref, gain_ref, q_hbm, k_hbm, v_hbm, bl_hbm, dg_hbm, gate_hbm, w_hbm, router_hbm, old_hbm,
    lo_ref, div_ref,
    q_ref, k_ref, v_ref, bl_ref, dg_ref, gate_ref, w_ref, router_ref, old_ref,
    rows_s, cols_s, t1_s, score_s, b_s, d_s, state_s, out_s,
    packs, gath, prefix, total, zbox, acc, first_half, start, outbox, landed,
    normed, own, cores, corebox, ring1, box1, ring2, box2,
    load, ys, yr, zs, zr, hs, hr, ls, lr, sc, rc, s1, r1, s2, r2,
):
    ctx = lax.axis_index("ctx")
    z, y = ctx // MESH_Y, lax.rem(ctx, MESH_Y)
    quad, zq = z // QUAD, lax.rem(z, QUAD)
    head = lax.axis_index("head")
    x, c = head // 2, lax.rem(head, 2)
    in_group = [to_ctx(z * MESH_Y + lax.rem(y + d, MESH_Y)) for d in range(1, MESH_Y)]
    right = to_head(lax.rem(x + 1, MESH_X) * 2 + c)
    left = to_head(lax.rem(x + MESH_X - 1, MESH_X) * 2 + c)
    twin = to_head(x * 2 + 1 - c)

    loads = [
        pltpu.make_async_copy(src, dst, load.at[i])
        for i, (src, dst) in enumerate(
            (
                (bl_hbm, bl_ref), (dg_hbm, dg_ref), (k_hbm, k_ref), (q_hbm, q_ref), (v_hbm, v_ref),
                (gate_hbm, gate_ref), (w_hbm, w_ref), (router_hbm, router_ref), (old_hbm, old_ref),
            )
        )
    ]
    for copy in loads:
        copy.start()

    barrier = pltpu.get_barrier_semaphore()
    for device in in_group + [right, left, twin]:
        signal(barrier, device)
    for d in range(1, QUAD):
        signal(barrier, to_ctx((quad * QUAD + lax.rem(zq + d, QUAD)) * MESH_Y + y))

    @pl.when(z == QUAD - 1)
    def _():
        for other in range(QUAD, nz):
            signal(barrier, to_ctx(other * MESH_Y + y))

    @pl.when(z >= QUAD)
    def _():
        signal(barrier, to_ctx((QUAD - 1) * MESH_Y + y))

    for copy in loads[:2]:
        copy.wait()
    decay_tables(de_ref, bl_ref, dg_ref, rows_s, cols_s)
    for copy in loads[2:5]:
        copy.wait()

    def solve(b, carry):
        solve_block(b, q_ref, k_ref, v_ref, rows_s, cols_s, t1_s, score_s, b_s, d_s)
        return carry

    lax.fori_loop(0, 4, solve, 0)

    row, lane = iotas()
    zero = jnp.zeros((L, L), F32)
    eye = jnp.where(row == lane, 1.0, 0.0).astype(F32)
    states = []
    for h in range(4):
        state_s[h] = jnp.concatenate([zero, eye], axis=1)
        states.append(jnp.concatenate([d_s[h], b_s[h]], axis=1))
    for b in range(1, 4):
        for h in range(4):
            state_s[4 * b + h] = states[h]
        states = [
            mm_three(b_s[4 * b + h], states[h]) + jnp.concatenate([d_s[4 * b + h], zero], axis=1)
            for h in range(4)
        ]
    for h in range(4):
        packs[h] = pack(states[h])

    peers = MESH_Y - 1 + 3 + QUAD - 1

    @pl.when(z < QUAD - 1)
    def _():
        pl.semaphore_wait(barrier, peers)

    @pl.when(z == QUAD - 1)
    def _():
        pl.semaphore_wait(barrier, peers + nz - QUAD)

    @pl.when(z >= QUAD)
    def _():
        pl.semaphore_wait(barrier, peers + 1)

    firsts = [
        remote(packs.at[lax.rem(y + d, MESH_Y)], gath.at[y], ys.at[d - 1], yr.at[d - 1], in_group[d - 1])
        for d in range(1, MESH_Y)
    ]
    for copy in firsts:
        copy.start()
    gath[y] = packs[y]

    def output(b, carry):
        output_block(b, q_ref, k_ref, v_ref, rows_s, cols_s, t1_s, score_s, state_s, out_s)
        return carry

    lax.fori_loop(0, 3, output, 0)

    for copy in firsts:
        copy.wait_recv()
    state = unpack(gath[0])
    for j in range(1, MESH_Y):
        prefix[j - 1] = state
        state = after(gath[j], state)
    total[...] = pack(state)

    def quad_copy(d):
        device = to_ctx((quad * QUAD + lax.rem(zq + d, QUAD)) * MESH_Y + y)
        return remote(total, zbox.at[zq], zs.at[d - 1], zr.at[d - 1], device)

    for d in range(1, QUAD):

        @pl.when(zq + d < QUAD)
        def _():
            quad_copy(d).start()

    output(3, 0)
    acc[...] = jnp.concatenate([zero, eye], axis=1)
    for d in range(1, QUAD):

        @pl.when(zq - d >= 0)
        def _():
            quad_copy(d).wait_recv()
            acc[...] = unpack(zbox[zq - 1]) if d == 1 else before(acc[...], zbox[zq - d])

    def half_copy(other):
        device = to_ctx(other * MESH_Y + y)
        return remote(first_half.at[0], first_half.at[1], hs.at[other - QUAD], hr.at[0], device)

    @pl.when(z == QUAD - 1)
    def _():
        ended = state[:, :L] + mm_three(state[:, L:], acc[:, :L])
        first_half[0] = ended.astype(BF16)
        for other in range(QUAD, nz):
            half_copy(other).start()

    start[...] = acc[:, :L]

    @pl.when(z >= QUAD)
    def _():
        half_copy(QUAD).wait_recv()
        start[...] = acc[:, :L] + mm_exact_right(acc[:, L:], first_half[1])

    incoming = start[...]
    outbox[0] = incoming.astype(BF16)
    for j in range(1, MESH_Y):
        outbox[j] = (prefix[j - 1, :, :L] + mm_three(prefix[j - 1, :, L:], incoming)).astype(BF16)
    lasts = [
        remote(outbox.at[lax.rem(y + d, MESH_Y)], landed.at[y], ls.at[d - 1], lr.at[d - 1], in_group[d - 1])
        for d in range(1, MESH_Y)
    ]
    for copy in lasts:
        copy.start()
    landed[y] = outbox[y]

    for copy in loads[5:]:
        copy.wait()
    old_logit = old_ref[...].astype(F32) / 1024.0
    old_logp = old_logit - jnp.log(jnp.sum(jnp.exp(old_logit), axis=1, keepdims=True))
    old_prob = jnp.exp(old_logp)
    old_part = jnp.sum(old_prob * old_logp, axis=1, keepdims=True)

    for copy in lasts:
        copy.wait_recv()

    order = [lax.rem(x + d, MESH_X) for d in (2, 1, 3, 0)]

    def send(src, dst, ssem, rsem, device):
        copy = remote(src, dst, ssem, rsem, device)
        copy.start()
        return copy

    core_copies = []

    def project(i):
        rows = pl.ds(pl.multiple_of(order[i] * L, L), L)
        parts = []
        for h in range(4):
            o = out_s[4 * order[i] + h]
            attended = o[:, :L] + mm_exact_right(o[:, L:], landed[h])
            scale = lax.rsqrt(jnp.mean(attended * attended, axis=1, keepdims=True) + EPS)
            gate = gate_ref[rows, L * h : L * h + L].astype(F32)
            parts.append((attended * scale * gain_ref[...] * (gate / (1.0 + jnp.exp(-gate)))).astype(BF16))
        normed[...] = jnp.concatenate(parts, axis=1)
        mine = normed[pl.ds(pl.multiple_of(c * ROWS, ROWS), ROWS), :]
        other = normed[pl.ds(pl.multiple_of((1 - c) * ROWS, ROWS), ROWS), :]
        both = jnp.concatenate([mine, other], axis=0)
        for n in range(4):
            cols = slice(512 * n, 512 * n + 512)
            partial = mm(both, w_ref[:, cols])
            own[i, :, cols] = partial[:ROWS]
            cores[i, :, cols] = partial[ROWS:].astype(BF16)
        core_copies.append(send(cores.at[i], corebox.at[i], sc.at[i], rc.at[i], twin))

    def pair_sum(i, cols):
        return own[i, :, cols] + corebox[i, :, cols].astype(F32)

    near, far = slice(0, HALF), slice(HALF, WIDE)
    ring = []
    project(0)
    project(1)
    core_copies[0].wait_recv()
    ring1[0] = pair_sum(0, near).astype(BF16)
    ring.append(send(ring1.at[0], box1.at[0], s1.at[0], r1.at[0], right))
    ring1[1] = pair_sum(0, far).astype(BF16)
    ring.append(send(ring1.at[1], box1.at[1], s1.at[1], r1.at[1], left))
    project(2)
    core_copies[1].wait_recv()
    ring2[0] = pair_sum(1, far).astype(BF16)
    ring.append(send(ring2.at[0], box2.at[0], s2.at[0], r2.at[0], right))
    core_copies[2].wait_recv()
    ring2[1] = pair_sum(2, near).astype(BF16)
    ring.append(send(ring2.at[1], box2.at[1], s2.at[1], r2.at[1], left))
    project(3)
    ring[0].wait_recv()
    ring2[2] = (pair_sum(1, near) + box1[0].astype(F32)).astype(BF16)
    ring.append(send(ring2.at[2], box2.at[2], s2.at[2], r2.at[2], right))
    ring[1].wait_recv()
    ring2[3] = (pair_sum(2, far) + box1[1].astype(F32)).astype(BF16)
    ring.append(send(ring2.at[3], box2.at[3], s2.at[3], r2.at[3], left))
    core_copies[3].wait_recv()
    for copy in ring[2:]:
        copy.wait_recv()
    out_near = (pair_sum(3, near) + box2[2].astype(F32) + box2[1].astype(F32)).astype(BF16)
    out_far = (pair_sum(3, far) + box2[0].astype(F32) + box2[3].astype(F32)).astype(BF16)
    lo_ref[:, near] = out_near
    lo_ref[:, far] = out_far
    new_logit = mm(out_near, router_ref[near]) + mm(out_far, router_ref[far])
    new_logp = new_logit - jnp.log(jnp.sum(jnp.exp(new_logit), axis=1, keepdims=True))
    div = old_part - jnp.sum(old_prob * new_logp, axis=1, keepdims=True)
    div_ref[...] = jnp.broadcast_to(div, (ROWS, L)).T[0:1, :]

    for copy in firsts + lasts + core_copies + ring:
        copy.wait_send()
    for d in range(1, QUAD):

        @pl.when(zq + d < QUAD)
        def _():
            quad_copy(d).wait_send()

    @pl.when(z == QUAD - 1)
    def _():
        for other in range(QUAD, nz):
            half_copy(other).wait_send()


def layer(nz, *arrays):
    vm = pl.BlockSpec(memory_space=pltpu.VMEM)
    square = (MESH_Y, L, L)
    many = pltpu.VMEM((16, L, L), F32)
    wide = pltpu.VMEM((16, L, 2 * L), F32)
    dma = pltpu.SemaphoreType.DMA
    return pl.pallas_call(
        functools.partial(layer_kernel, nz),
        out_shape=(
            jax.ShapeDtypeStruct((ROWS, WIDE), BF16),
            jax.ShapeDtypeStruct((1, ROWS), F32),
        ),
        in_specs=[pl.BlockSpec(memory_space=pltpu.SMEM), vm] + [pl.BlockSpec(memory_space=pl.ANY)] * 9,
        out_specs=(vm, vm),
        scratch_shapes=[
            pltpu.VMEM((512, 256), BF16),
            pltpu.VMEM((512, 256), BF16),
            pltpu.VMEM((512, 512), BF16),
            pltpu.VMEM((4, 512), F32),
            pltpu.VMEM((4, 512), F32),
            pltpu.VMEM((512, 512), BF16),
            pltpu.VMEM((512, WIDE), BF16),
            pltpu.VMEM((WIDE, 512), BF16),
            pltpu.VMEM((ROWS, 512), jnp.int32),
            pltpu.VMEM((4, 32, L), F32),
            pltpu.VMEM((4, L, L), F32),
            many, many, many, many, wide, wide,
            pltpu.VMEM((MESH_Y, PACK, 2 * L), BF16),
            pltpu.VMEM((MESH_Y, PACK, 2 * L), BF16),
            pltpu.VMEM((MESH_Y - 1, L, 2 * L), F32),
            pltpu.VMEM((PACK, 2 * L), BF16),
            pltpu.VMEM((QUAD, PACK, 2 * L), BF16),
            pltpu.VMEM((L, 2 * L), F32),
            pltpu.VMEM((2, L, L), BF16),
            pltpu.VMEM((L, L), F32),
            pltpu.VMEM(square, BF16),
            pltpu.VMEM(square, BF16),
            pltpu.VMEM((L, 512), BF16),
            pltpu.VMEM((4, ROWS, WIDE), F32),
            pltpu.VMEM((4, ROWS, WIDE), BF16),
            pltpu.VMEM((4, ROWS, WIDE), BF16),
            pltpu.VMEM((2, ROWS, HALF), BF16),
            pltpu.VMEM((2, ROWS, HALF), BF16),
            pltpu.VMEM((4, ROWS, HALF), BF16),
            pltpu.VMEM((4, ROWS, HALF), BF16),
            dma((9,)),
            dma((3,)), dma((3,)), dma((3,)), dma((3,)),
            dma((max(nz - QUAD, 1),)), dma((1,)),
            dma((3,)), dma((3,)),
            dma((4,)), dma((4,)), dma((2,)), dma((2,)), dma((4,)), dma((4,)),
        ],
        compiler_params=pltpu.CompilerParams(
            collective_id=0, has_side_effects=True, vmem_limit_bytes=56 * 1024 * 1024
        ),
    )(*arrays)


def solution(mesh):
    nz = mesh.shape["ctx"] // MESH_Y

    def local(
        queries, key_vec, values, out_gate, beta_logit, decay_gate, decay_exp,
        norm_gain, out_weight, router_weight, old_scores,
    ):
        layer_out, div = layer(
            nz, decay_exp, norm_gain.reshape(1, L), queries, key_vec, values, beta_logit, decay_gate,
            out_gate, out_weight, router_weight, old_scores,
        )
        return layer_out, div.reshape(ROWS)

    placed = (
        P("ctx", "head"), P("ctx", "head"), P("ctx", "head"), P("ctx", "head"), P("head", "ctx"),
        P("head", "ctx"), P("head"), P(), P("head", None), P(), P(("ctx", "head"), None),
    )
    return jax.shard_map(
        local,
        mesh=mesh,
        in_specs=placed,
        out_specs=(P(("ctx", "head"), None), P(("ctx", "head"))),
        check_vma=False,
    )
```

```python
import jax
import jax.numpy as jnp
from jax import lax
from jax.experimental import pallas as pl
from jax.experimental.pallas import tpu as pltpu
from jax.sharding import PartitionSpec as P

F32 = jnp.float32
BF16 = jnp.bfloat16
L = 128
EPS = 1e-6


def mm(a, b):
    return jnp.dot(a, b, preferred_element_type=F32)


def split(x):
    hi = x.astype(BF16)
    return hi, (x - hi.astype(F32)).astype(BF16)


def mm_wide(a, b):
    ah, al = split(a)
    bh, bl = split(b)
    row = jnp.concatenate([bh, bl], axis=1)
    r = mm(jnp.concatenate([ah, al], axis=1), jnp.concatenate([row, row], axis=0))
    n = b.shape[1]
    return r[:, :n] + r[:, n:]


def mm_rows(a, b):
    n, wide = a.shape[0], b.shape[1]
    r = mm(jnp.concatenate(split(a), axis=0), jnp.concatenate(split(b), axis=1))
    return r[:n, :wide] + (r[:n, wide:] + r[n:, :wide])


def mm_three(a, b):
    ah, al = split(a)
    bh, bl = split(b)
    return mm(jnp.concatenate([ah, al, ah], axis=1), jnp.concatenate([bh, bh, bl], axis=0))


def mm_exact_right(a, b16):
    ah, al = split(a)
    return mm(jnp.concatenate([ah, al], axis=1), jnp.concatenate([b16, b16], axis=0))


def odd_rows(x, s):
    if s == 64:
        return x[64:]
    return jnp.concatenate([x[i : i + s] for i in range(s, L, 2 * s)], axis=0)


def weave(even, odd, s):
    parts = []
    for n, i in enumerate(range(0, L, 2 * s)):
        parts += [even[i : i + s], odd[n * s : (n + 1) * s]]
    return jnp.concatenate(parts, axis=0)


def unit_lower_inverse(systems):
    lane16 = lax.broadcasted_iota(jnp.int32, (16, L), 1)
    row16 = lax.broadcasted_iota(jnp.int32, (16, L), 0)
    place = lane16 // 16
    bands = []
    for a in systems:
        band = jnp.zeros((16, L), F32)
        for b in range(L // 16):
            band = jnp.where(place == b, a[16 * b : 16 * b + 16], band)
        bands.append(band)
    start = jnp.where(lane16 % 16 == row16, 1.0, 0.0).astype(F32)
    solved = [start for _ in systems]
    for m in range(15):
        index = place * 16 + m
        spread = [jnp.take_along_axis(band, index, axis=1) for band in bands]
        solved = [r - s * r[m : m + 1] for r, s in zip(solved, spread)]
    row = lax.broadcasted_iota(jnp.int32, (L, L), 0)
    lane = lax.broadcasted_iota(jnp.int32, (L, L), 1)
    same = row // 16 == lane // 16
    inverses = [jnp.where(same, jnp.concatenate([r] * (L // 16), axis=0), 0.0) for r in solved]
    for s in (16, 32, 64):
        below = odd_rows(row // s, s) == odd_rows(lane // s, s) + 1
        zeros = jnp.zeros((L, L), F32)
        lower = [mm_rows(jnp.where(below, odd_rows(a, s), 0.0), t) for a, t in zip(systems, inverses)]
        full = [weave(zeros, y, s) for y in lower]
        odd = [odd_rows(t, s) for t in inverses]
        change = [mm_rows(o, f) for o, f in zip(odd, full)]
        inverses = [weave(t, o - c, s) for t, o, c in zip(inverses, odd, change)]
    return inverses


ROWS = 64
WIDE = 2048
HALF = WIDE // 2
MESH_X = 4
MESH_Y = 4
QUAD = 4
PACK = L + 16


def to_ctx(ctx):
    return {"ctx": ctx}


def to_head(head):
    return {"head": head}


def signal(semaphore, device):
    pl.semaphore_signal(semaphore, inc=1, device_id=device, device_id_type=pl.DeviceIdType.MESH)


def remote(src, dst, send_sem, recv_sem, device):
    return pltpu.make_async_remote_copy(
        src_ref=src, dst_ref=dst, send_sem=send_sem, recv_sem=recv_sem,
        device_id=device, device_id_type=pl.DeviceIdType.MESH,
    )


def iotas():
    return lax.broadcasted_iota(jnp.int32, (L, L), 0), lax.broadcasted_iota(jnp.int32, (L, L), 1)


def decay_tables(de_ref, bl_ref, dg_ref, rows_s, cols_s):
    row = lax.broadcasted_iota(jnp.int32, (8, 512), 0)
    lane = lax.broadcasted_iota(jnp.int32, (8, 512), 1) % L
    exponent = jnp.zeros((8, 512), jnp.int32)
    for h in range(4):
        exponent = jnp.where(row % 4 == h, de_ref[h], exponent)
    rate = jnp.exp2(exponent.astype(F32)) / 16384.0
    gate = jnp.concatenate([dg_ref[...]] * 2, axis=0)
    beta = jax.nn.sigmoid(jnp.concatenate([bl_ref[...]] * 2, axis=0))
    cum = -rate * gate
    for s in (1, 2, 4, 8, 16, 32, 64):
        cum = cum + jnp.where(lane >= s, pltpu.roll(cum, s, 1), 0.0)
    growth = jnp.exp(cum)
    for b in range(4):
        tokens = slice(L * b, L * b + L)
        now = cum[:, tokens]
        last = jnp.broadcast_to(now[:, L - 1 : L], (8, L))
        parts = [now, beta[:, tokens], growth[:, tokens]]
        rows_s[b] = jnp.concatenate(parts + [jnp.exp(last)], axis=0)
        padding = [jnp.zeros((L - 32, L), F32)]
        cols_s[b] = jnp.concatenate(parts + [jnp.exp(last - now)] + padding, axis=0).T


def solve_blocks(blocks, q_ref, k_ref, v_ref, rows_s, cols_s, t1_s, fade_s, b_s, d_s):
    row, lane = iotas()
    eye = jnp.where(row == lane, 1.0, 0.0).astype(F32)
    tokens = [pl.ds(pl.multiple_of(b * L, L), L) for b in blocks]
    rows = [rows_s[b] for b in blocks]
    columns = [cols_s[b] for b in blocks]
    places = [(n, kh) for n in range(len(blocks)) for kh in range(2)]
    keys = [k_ref[tokens[n], L * kh : L * kh + L] for n, kh in places]
    keys_t = [key.T for key in keys]
    norms = [
        lax.rsqrt(jnp.sum(key.astype(F32) * key.astype(F32), axis=1, keepdims=True) + EPS) for key in keys
    ]
    grams = [mm(key, key_t) for key, key_t in zip(keys, keys_t)]
    key_rows = []
    for n, b in enumerate(blocks):
        table = jnp.where(lane == 0, norms[2 * n], jnp.where(lane == 1, norms[2 * n + 1], 0.0))
        key_rows.append(table.T)
        rows_s[b, 28:30] = key_rows[n][:2]
    spots = [(n, h) for n in range(len(blocks)) for h in range(4)]
    systems = []
    for n, h in spots:
        kh = h // 2
        fade = jnp.exp(jnp.minimum(columns[n][:, h : h + 1] - rows[n][h : h + 1], 0.0))
        fade = fade * key_rows[n][kh : kh + 1]
        fade_s[4 * blocks[n] + h] = fade
        scaled = grams[2 * n + kh] * (norms[2 * n + kh] * columns[n][:, 8 + h : 9 + h])
        systems.append(jnp.where(row > lane, scaled * fade, 0.0))
    inverses = unit_lower_inverse(systems)
    t1s = [t * rows[n][8 + h : 9 + h] for t, (n, h) in zip(inverses, spots)]
    reaches = [rows[n][16 + h : 17 + h] * key_rows[n][h // 2 : h // 2 + 1] for n, h in spots]
    for (n, h), t1, reach in zip(spots, t1s, reaches):
        t1_s[4 * blocks[n] + h] = t1
        rows_s[blocks[n], 4 + h : 5 + h] = reach
    written = [mm_exact_right(t1, v_ref[tokens[n], L * h : L * h + L]) for t1, (n, h) in zip(t1s, spots)]
    widened = [
        mm_exact_right(t1 * reach, keys[2 * n + h // 2]) for t1, reach, (n, h) in zip(t1s, reaches, spots)
    ]
    changes = []
    for (n, h), u, w in zip(spots, written, widened):
        rem = columns[n][:, 24 + h : 25 + h] * norms[2 * n + h // 2]
        wh, wl = split(jnp.concatenate([u * rem, w * rem], axis=1))
        kt = keys_t[2 * n + h // 2]
        changes.append(mm(jnp.concatenate([kt, kt], axis=1), jnp.concatenate([wh, wl], axis=0)))
    for (n, h), change in zip(spots, changes):
        d_s[4 * blocks[n] + h] = change[:, :L]
        b_s[4 * blocks[n] + h] = eye * rows[n][24 + h : 25 + h] - change[:, L:]


def output_block(b, q_ref, k_ref, v_ref, rows_s, cols_s, t1_s, fade_s, state_s, out_s):
    row, lane = iotas()
    tokens = pl.ds(pl.multiple_of(b * L, L), L)
    rows, columns = rows_s[b], cols_s[b]
    zero = jnp.zeros((L, L), F32)
    keys, queries, scales, grams = [], [], [], []
    for kh in range(2):
        key = k_ref[tokens, L * kh : L * kh + L]
        query = q_ref[tokens, L * kh : L * kh + L]
        query32 = query.astype(F32)
        scales.append(lax.rsqrt(jnp.sum(query32 * query32, axis=1, keepdims=True) + EPS) * (L**-0.5))
        grams.append(mm(query, key.T))
        keys.append(key)
        queries.append(query32)
    scores = [
        jnp.where(row >= lane, grams[h // 2] * scales[h // 2] * fade_s[4 * b + h], 0.0) for h in range(4)
    ]
    reads = [mm_wide(score, t1_s[4 * b + h]) for h, score in enumerate(scores)]
    from_values = [mm_exact_right(r, v_ref[tokens, L * h : L * h + L]) for h, r in enumerate(reads)]
    from_keys = [mm_exact_right(r * rows[4 + h : 5 + h], keys[h // 2]) for h, r in enumerate(reads)]
    for h in range(4):
        lead = queries[h // 2] * (columns[:, 16 + h : 17 + h] * scales[h // 2]) - from_keys[h]
        out_s[4 * b + h] = mm_three(lead, state_s[4 * b + h]) + jnp.concatenate([from_values[h], zero], axis=1)


def pack(state):
    row, lane = iotas()
    kept = state.astype(BF16)
    lost = state[:, L:] - kept[:, L:].astype(F32)
    lost = jnp.sum(jnp.where(row == lane, lost, 0.0), axis=0, keepdims=True)
    lost = jnp.broadcast_to(jnp.concatenate([jnp.zeros((1, L), F32), lost], axis=1), (PACK - L, 2 * L))
    return jnp.concatenate([kept, lost.astype(BF16)], axis=0)


def lost_diagonal(packed):
    row, lane = iotas()
    return jnp.where(row == lane, packed[L : L + 1, L:].astype(F32), 0.0)


def unpack(packed):
    state = packed[:L].astype(F32)
    return jnp.concatenate([state[:, :L], state[:, L:] + lost_diagonal(packed)], axis=1)


def after(packed, state):
    m = packed[:L, L:]
    hi, lo = split(state)
    lhs = jnp.concatenate([m, lost_diagonal(packed).astype(BF16), m], axis=1)
    moved = mm(lhs, jnp.concatenate([hi, hi, lo], axis=0))
    return moved + jnp.concatenate([packed[:L, :L].astype(F32), jnp.zeros((L, L), F32)], axis=1)


def after_state(packed, state):
    m = packed[:L, L:]
    hi, lo = split(state)
    lhs = jnp.concatenate([m, lost_diagonal(packed).astype(BF16), m], axis=1)
    return mm(lhs, jnp.concatenate([hi, hi, lo], axis=0)) + packed[:L, :L].astype(F32)


def before(state, packed):
    hi, lo = split(state[:, L:])
    lost = jnp.concatenate([jnp.zeros((L, L), F32), lost_diagonal(packed)], axis=1).astype(BF16)
    moved = mm(
        jnp.concatenate([hi, lo, hi], axis=1), jnp.concatenate([packed[:L], packed[:L], lost], axis=0)
    )
    return moved + jnp.concatenate([state[:, :L], jnp.zeros((L, L), F32)], axis=1)


def layer_kernel(
    de_hbm, gain_hbm, q_hbm, k_hbm, v_hbm, bl_hbm, dg_hbm, gate_hbm, w_hbm, router_hbm, old_hbm,
    lo_ref, div_ref,
    de_ref, gain_ref, q_ref, k_ref, v_ref, bl_ref, dg_ref, gate_ref, w_ref, w2_ref, router_ref, old_ref,
    rows_s, cols_s, t1_s, fade_s, b_s, d_s, state_s, out_s,
    packs, gath, prefix, total, zbox, acc, first_half, start, outbox, landed,
    normed, nbox, own, ring1, box1, ring2, box2,
    load, ys, yr, zs, zr, hs, hr, ls, lr, ws, wr, sc, rc, s1, r1, s2, r2,
):
    ctx = lax.axis_index("ctx")
    z, y = ctx // MESH_Y, lax.rem(ctx, MESH_Y)
    quad, zq = z // QUAD, lax.rem(z, QUAD)
    head = lax.axis_index("head")
    x, c = head // 2, lax.rem(head, 2)
    in_group = [to_ctx(z * MESH_Y + lax.rem(y + d, MESH_Y)) for d in range(1, MESH_Y)]
    right = to_head(lax.rem(x + 1, MESH_X) * 2 + c)
    left = to_head(lax.rem(x + MESH_X - 1, MESH_X) * 2 + c)
    twin = to_head(x * 2 + 1 - c)

    def at_z(other):
        return to_ctx(other * MESH_Y + y)

    loads = [
        pltpu.make_async_copy(src, dst, load.at[i])
        for i, (src, dst) in enumerate(
            (
                (de_hbm, de_ref), (bl_hbm, bl_ref), (dg_hbm, dg_ref), (k_hbm, k_ref), (v_hbm, v_ref),
                (q_hbm, q_ref), (w_hbm, w_ref), (gate_hbm, gate_ref), (gain_hbm, gain_ref),
                (router_hbm, router_ref), (old_hbm, old_ref),
            )
        )
    ]
    for copy in loads:
        copy.start()

    barrier = pltpu.get_barrier_semaphore()
    for device in in_group + [right, left, twin]:
        signal(barrier, device)
    for d in range(1, QUAD):
        signal(barrier, at_z(quad * QUAD + lax.rem(zq + d, QUAD)))
    serves = ((QUAD - 1, (QUAD, QUAD + 1)), (0, (2 * QUAD - 1, 2 * QUAD - 2)))
    for end, served in serves:

        @pl.when(z == end)
        def _():
            for other in served:
                signal(barrier, at_z(other))

        for other in served:

            @pl.when(z == other)
            def _():
                signal(barrier, at_z(end))

    for copy in loads[:3]:
        copy.wait()
    decay_tables(de_ref, bl_ref, dg_ref, rows_s, cols_s)
    for copy in loads[3:5]:
        copy.wait()
    solve_blocks(range(4), q_ref, k_ref, v_ref, rows_s, cols_s, t1_s, fade_s, b_s, d_s)

    row, lane = iotas()
    zero = jnp.zeros((L, L), F32)
    eye = jnp.where(row == lane, 1.0, 0.0).astype(F32)
    states = []
    for h in range(4):
        state_s[h] = jnp.concatenate([zero, eye], axis=1)
        states.append(jnp.concatenate([d_s[h], b_s[h]], axis=1))
    for b in range(1, 4):
        for h in range(4):
            state_s[4 * b + h] = states[h]
        states = [
            mm_three(b_s[4 * b + h], states[h]) + jnp.concatenate([d_s[4 * b + h], zero], axis=1)
            for h in range(4)
        ]
    for h, packed in enumerate([pack(state) for state in states]):
        packs[h] = packed

    peers = MESH_Y - 1 + 3 + QUAD - 1

    @pl.when(jnp.logical_or(z == 0, z == QUAD - 1))
    def _():
        pl.semaphore_wait(barrier, peers + 2)

    @pl.when(jnp.logical_and(z > 0, z < QUAD - 1))
    def _():
        pl.semaphore_wait(barrier, peers)

    @pl.when(z >= QUAD)
    def _():
        pl.semaphore_wait(barrier, peers + 1)

    firsts = [
        remote(packs.at[lax.rem(y + d, MESH_Y)], gath.at[y], ys.at[d - 1], yr.at[d - 1], in_group[d - 1])
        for d in range(1, MESH_Y)
    ]
    for copy in firsts:
        copy.start()
    gath[y] = packs[y]
    loads[6].wait()
    weights = remote(w_ref, w2_ref, ws.at[0], wr.at[0], twin)
    weights.start()
    loads[5].wait()

    def output(b, carry):
        output_block(b, q_ref, k_ref, v_ref, rows_s, cols_s, t1_s, fade_s, state_s, out_s)
        return carry

    lax.fori_loop(0, 4, output, 0)

    for copy in firsts:
        copy.wait_recv()
    state = unpack(gath[0])
    for j in range(1, MESH_Y):
        prefix[j - 1] = state
        state = after(gath[j], state)
    total[...] = pack(state)

    def up_copy(d):
        device = at_z(quad * QUAD + lax.rem(zq + d, QUAD))
        return remote(total, zbox.at[zq], zs.at[d - 1], zr.at[d - 1], device)

    def down_copy(d):
        return remote(total, zbox.at[zq], zs.at[QUAD - 1], zr.at[QUAD - 2 + d], at_z(0))

    for d in range(1, QUAD):

        @pl.when(zq + d < QUAD)
        def _():
            up_copy(d).start()

        @pl.when(z == d)
        def _():
            down_copy(d).start()

    for copy in loads[7:]:
        copy.wait()
    old_logit = old_ref[...].astype(F32) / 1024.0
    old_logp = old_logit - jnp.log(jnp.sum(jnp.exp(old_logit), axis=1, keepdims=True))
    old_prob = jnp.exp(old_logp)
    old_part = jnp.sum(old_prob * old_logp, axis=1, keepdims=True)

    acc[...] = jnp.concatenate([zero, eye], axis=1)
    for d in range(1, QUAD):

        @pl.when(zq - d >= 0)
        def _():
            up_copy(d).wait_recv()
            acc[...] = unpack(zbox[zq - 1]) if d == 1 else before(acc[...], zbox[zq - d])

    def half_copy(i, other):
        return remote(first_half.at[0], first_half.at[1], hs.at[i], hr.at[0], at_z(other))

    @pl.when(z == QUAD - 1)
    def _():
        ended = state[:, :L] + mm_three(state[:, L:], acc[:, :L])
        first_half[0] = ended.astype(BF16)
        for i, other in enumerate(serves[0][1]):
            half_copy(i, other).start()

    @pl.when(z == 0)
    def _():
        ended = state[:, :L]
        for d in range(1, QUAD):
            down_copy(d).wait_recv()
            ended = after_state(zbox[d], ended)
        first_half[0] = ended.astype(BF16)
        for i, other in enumerate(serves[1][1]):
            half_copy(i, other).start()

    start[...] = acc[:, :L]

    @pl.when(z >= QUAD)
    def _():
        half_copy(0, QUAD).wait_recv()
        start[...] = acc[:, :L] + mm_exact_right(acc[:, L:], first_half[1])

    incoming = start[...]
    outbox[0] = incoming.astype(BF16)
    moved = mm_three(jnp.concatenate([prefix[j, :, L:] for j in range(MESH_Y - 1)], axis=0), incoming)
    for j in range(1, MESH_Y):
        outbox[j] = (prefix[j - 1, :, :L] + moved[L * (j - 1) : L * j]).astype(BF16)
    lasts = [
        remote(outbox.at[lax.rem(y + d, MESH_Y)], landed.at[y], ls.at[d - 1], lr.at[d - 1], in_group[d - 1])
        for d in range(1, MESH_Y)
    ]
    for copy in lasts:
        copy.start()
    landed[y] = outbox[y]
    weights.wait_recv()
    for copy in lasts:
        copy.wait_recv()

    order = [lax.rem(x + d, MESH_X) for d in (2, 1, 3, 0)]

    def send(src, dst, ssem, rsem, device):
        copy = remote(src, dst, ssem, rsem, device)
        copy.start()
        return copy

    def norm(i):
        rows = pl.ds(pl.multiple_of(order[i] * L, L), L)
        outs = [out_s[4 * order[i] + h] for h in range(4)]
        attended = [o[:, :L] + mm_exact_right(o[:, L:], landed[h]) for h, o in enumerate(outs)]
        scales = [lax.rsqrt(jnp.mean(a * a, axis=1, keepdims=True) + EPS) for a in attended]
        gates = [gate_ref[rows, L * h : L * h + L].astype(F32) for h in range(4)]
        parts = [
            (a * s * gain_ref[...] * (g / (1.0 + jnp.exp(-g)))).astype(BF16)
            for a, s, g in zip(attended, scales, gates)
        ]
        normed[i] = jnp.concatenate(parts, axis=1)
        rows = pl.ds(pl.multiple_of((1 - c) * ROWS, ROWS), ROWS)
        return send(normed.at[i, rows], nbox.at[i], sc.at[i], rc.at[i], twin)

    def mine(i):
        return normed[i, pl.ds(pl.multiple_of(c * ROWS, ROWS), ROWS), :]

    near, far = slice(0, HALF), slice(HALF, WIDE)
    swaps = [norm(i) for i in range(4)]
    ring = []
    swaps[0].wait_recv()
    ring1[0] = (mm(mine(0), w_ref[:, near]) + mm(nbox[0], w2_ref[:, near])).astype(BF16)
    ring.append(send(ring1.at[0], box1.at[0], s1.at[0], r1.at[0], right))
    ring1[1] = (mm(mine(0), w_ref[:, far]) + mm(nbox[0], w2_ref[:, far])).astype(BF16)
    ring.append(send(ring1.at[1], box1.at[1], s1.at[1], r1.at[1], left))
    for swap in swaps[1:]:
        swap.wait_recv()
    my_rows = jnp.concatenate([mine(1), mine(2), mine(3)], axis=0)
    twin_rows = jnp.concatenate([nbox[1], nbox[2], nbox[3]], axis=0)
    own[:, far] = mm(my_rows, w_ref[:, far]) + mm(twin_rows, w2_ref[:, far])
    ring2[0] = own[0:ROWS, far].astype(BF16)
    ring.append(send(ring2.at[0], box2.at[0], s2.at[0], r2.at[0], right))
    own[:, near] = mm(my_rows, w_ref[:, near]) + mm(twin_rows, w2_ref[:, near])
    ring2[1] = own[ROWS : 2 * ROWS, near].astype(BF16)
    ring.append(send(ring2.at[1], box2.at[1], s2.at[1], r2.at[1], left))
    ring[0].wait_recv()
    ring2[2] = (own[0:ROWS, near] + box1[0].astype(F32)).astype(BF16)
    ring.append(send(ring2.at[2], box2.at[2], s2.at[2], r2.at[2], right))
    ring[1].wait_recv()
    ring2[3] = (own[ROWS : 2 * ROWS, far] + box1[1].astype(F32)).astype(BF16)
    ring.append(send(ring2.at[3], box2.at[3], s2.at[3], r2.at[3], left))
    for copy in ring[2:4]:
        copy.wait_recv()
    sum_far = own[2 * ROWS :, far] + box2[0].astype(F32)
    sum_near = own[2 * ROWS :, near] + box2[1].astype(F32)
    ring[4].wait_recv()
    out_near = (sum_near + box2[2].astype(F32)).astype(BF16)
    lo_ref[:, near] = out_near
    new_logit = mm(out_near, router_ref[near])
    ring[5].wait_recv()
    out_far = (sum_far + box2[3].astype(F32)).astype(BF16)
    lo_ref[:, far] = out_far
    new_logit = new_logit + mm(out_far, router_ref[far])
    new_logp = new_logit - jnp.log(jnp.sum(jnp.exp(new_logit), axis=1, keepdims=True))
    div = old_part - jnp.sum(old_prob * new_logp, axis=1, keepdims=True)
    div_ref[...] = jnp.broadcast_to(div, (ROWS, L)).T[0:1, :]

    for copy in firsts + lasts + swaps + ring + [weights]:
        copy.wait_send()
    for d in range(1, QUAD):

        @pl.when(zq + d < QUAD)
        def _():
            up_copy(d).wait_send()

        @pl.when(z == d)
        def _():
            down_copy(d).wait_send()

    for end, served in serves:

        @pl.when(z == end)
        def _():
            for i, other in enumerate(served):
                half_copy(i, other).wait_send()


def layer(*arrays):
    vm = pl.BlockSpec(memory_space=pltpu.VMEM)
    square = (MESH_Y, L, L)
    many = pltpu.VMEM((16, L, L), F32)
    wide = pltpu.VMEM((16, L, 2 * L), F32)
    dma = pltpu.SemaphoreType.DMA
    return pl.pallas_call(
        layer_kernel,
        out_shape=(
            jax.ShapeDtypeStruct((ROWS, WIDE), BF16),
            jax.ShapeDtypeStruct((1, ROWS), F32),
        ),
        in_specs=[pl.BlockSpec(memory_space=pltpu.HBM)] * 11,
        out_specs=(vm, vm),
        scratch_shapes=[
            pltpu.SMEM((4,), jnp.int32),
            pltpu.VMEM((1, L), F32),
            pltpu.VMEM((512, 256), BF16),
            pltpu.VMEM((512, 256), BF16),
            pltpu.VMEM((512, 512), BF16),
            pltpu.VMEM((4, 512), F32),
            pltpu.VMEM((4, 512), F32),
            pltpu.VMEM((512, 512), BF16),
            pltpu.VMEM((512, WIDE), BF16),
            pltpu.VMEM((512, WIDE), BF16),
            pltpu.VMEM((WIDE, 512), BF16),
            pltpu.VMEM((ROWS, 512), jnp.int32),
            pltpu.VMEM((4, 32, L), F32),
            pltpu.VMEM((4, L, L), F32),
            many, many, many, many, wide, wide,
            pltpu.VMEM((MESH_Y, PACK, 2 * L), BF16),
            pltpu.VMEM((MESH_Y, PACK, 2 * L), BF16),
            pltpu.VMEM((MESH_Y - 1, L, 2 * L), F32),
            pltpu.VMEM((PACK, 2 * L), BF16),
            pltpu.VMEM((QUAD, PACK, 2 * L), BF16),
            pltpu.VMEM((L, 2 * L), F32),
            pltpu.VMEM((2, L, L), BF16),
            pltpu.VMEM((L, L), F32),
            pltpu.VMEM(square, BF16),
            pltpu.VMEM(square, BF16),
            pltpu.VMEM((4, L, 512), BF16),
            pltpu.VMEM((4, ROWS, 512), BF16),
            pltpu.VMEM((3 * ROWS, WIDE), F32),
            pltpu.VMEM((2, ROWS, HALF), BF16),
            pltpu.VMEM((2, ROWS, HALF), BF16),
            pltpu.VMEM((4, ROWS, HALF), BF16),
            pltpu.VMEM((4, ROWS, HALF), BF16),
            dma((11,)),
            dma((3,)), dma((3,)),
            dma((QUAD,)), dma((2 * QUAD - 2,)),
            dma((2,)), dma((1,)),
            dma((3,)), dma((3,)),
            dma((1,)), dma((1,)),
            dma((4,)), dma((4,)), dma((2,)), dma((2,)), dma((4,)), dma((4,)),
        ],
        compiler_params=pltpu.CompilerParams(
            collective_id=0, has_side_effects=True, vmem_limit_bytes=36 * 1024 * 1024
        ),
    )(*arrays)


def solution(mesh):
    def local(
        queries, key_vec, values, out_gate, beta_logit, decay_gate, decay_exp,
        norm_gain, out_weight, router_weight, old_scores,
    ):
        arrays = (
            decay_exp, norm_gain.reshape(1, L), queries, key_vec, values, beta_logit, decay_gate,
            out_gate, out_weight, router_weight, old_scores,
        )
        layer_out, div = layer(*(pltpu.with_memory_space_constraint(a, pltpu.HBM) for a in arrays))
        return layer_out, div.reshape(ROWS)

    placed = (
        P("ctx", "head"), P("ctx", "head"), P("ctx", "head"), P("ctx", "head"), P("head", "ctx"),
        P("head", "ctx"), P("head"), P(), P("head", None), P(), P(("ctx", "head"), None),
    )
    return jax.shard_map(
        local,
        mesh=mesh,
        in_specs=placed,
        out_specs=(P(("ctx", "head"), None), P(("ctx", "head"))),
        check_vma=False,
    )
```

```python
import jax
import jax.numpy as jnp
from jax import lax
from jax.experimental import pallas as pl
from jax.experimental.pallas import tpu as pltpu
from jax.sharding import PartitionSpec as P

F32 = jnp.float32
BF16 = jnp.bfloat16
L = 128
EPS = 1e-6


def mm(a, b):
    return jnp.dot(a, b, preferred_element_type=F32)


def split(x):
    hi = x.astype(BF16)
    return hi, (x - hi.astype(F32)).astype(BF16)


def mm_wide(a, b):
    ah, al = split(a)
    bh, bl = split(b)
    row = jnp.concatenate([bh, bl], axis=1)
    r = mm(jnp.concatenate([ah, al], axis=1), jnp.concatenate([row, row], axis=0))
    n = b.shape[1]
    return r[:, :n] + r[:, n:]


def mm_rows(a, b):
    n, wide = a.shape[0], b.shape[1]
    r = mm(jnp.concatenate(split(a), axis=0), jnp.concatenate(split(b), axis=1))
    return r[:n, :wide] + (r[:n, wide:] + r[n:, :wide])


def mm_three(a, b):
    ah, al = split(a)
    bh, bl = split(b)
    return mm(jnp.concatenate([ah, al, ah], axis=1), jnp.concatenate([bh, bh, bl], axis=0))


def mm_exact_right(a, b16):
    ah, al = split(a)
    return mm(jnp.concatenate([ah, al], axis=1), jnp.concatenate([b16, b16], axis=0))


def odd_rows(x, s):
    if s == 64:
        return x[64:]
    return jnp.concatenate([x[i : i + s] for i in range(s, L, 2 * s)], axis=0)


def weave(even, odd, s):
    parts = []
    for n, i in enumerate(range(0, L, 2 * s)):
        parts += [even[i : i + s], odd[n * s : (n + 1) * s]]
    return jnp.concatenate(parts, axis=0)


def unit_lower_inverse(systems):
    lane16 = lax.broadcasted_iota(jnp.int32, (16, L), 1)
    row16 = lax.broadcasted_iota(jnp.int32, (16, L), 0)
    place = lane16 // 16
    bands = []
    for a in systems:
        band = jnp.zeros((16, L), F32)
        for b in range(L // 16):
            band = jnp.where(place == b, a[16 * b : 16 * b + 16], band)
        bands.append(band)
    start = jnp.where(lane16 % 16 == row16, 1.0, 0.0).astype(F32)
    solved = [start for _ in systems]
    for m in range(15):
        index = place * 16 + m
        spread = [jnp.take_along_axis(band, index, axis=1) for band in bands]
        solved = [r - s * r[m : m + 1] for r, s in zip(solved, spread)]
    row = lax.broadcasted_iota(jnp.int32, (L, L), 0)
    lane = lax.broadcasted_iota(jnp.int32, (L, L), 1)
    same = row // 16 == lane // 16
    inverses = [jnp.where(same, jnp.concatenate([r] * (L // 16), axis=0), 0.0) for r in solved]
    for s in (16, 32, 64):
        below = odd_rows(row // s, s) == odd_rows(lane // s, s) + 1
        zeros = jnp.zeros((L, L), F32)
        lower = [mm_rows(jnp.where(below, odd_rows(a, s), 0.0), t) for a, t in zip(systems, inverses)]
        full = [weave(zeros, y, s) for y in lower]
        odd = [odd_rows(t, s) for t in inverses]
        change = [mm_rows(o, f) for o, f in zip(odd, full)]
        inverses = [weave(t, o - c, s) for t, o, c in zip(inverses, odd, change)]
    return inverses


ROWS = 64
WIDE = 2048
HALF = WIDE // 2
QUARTER = WIDE // 4
MESH_X = 4
MESH_Y = 4
QUAD = 4
PACK = L + 16


def to_ctx(ctx):
    return {"ctx": ctx}


def to_head(head):
    return {"head": head}


def signal(semaphore, device):
    pl.semaphore_signal(semaphore, inc=1, device_id=device, device_id_type=pl.DeviceIdType.MESH)


def remote(src, dst, send_sem, recv_sem, device):
    return pltpu.make_async_remote_copy(
        src_ref=src, dst_ref=dst, send_sem=send_sem, recv_sem=recv_sem,
        device_id=device, device_id_type=pl.DeviceIdType.MESH,
    )


def iotas():
    return lax.broadcasted_iota(jnp.int32, (L, L), 0), lax.broadcasted_iota(jnp.int32, (L, L), 1)


def decay_tables(de_ref, bl_ref, dg_ref, rows_s, cols_s):
    row = lax.broadcasted_iota(jnp.int32, (8, 512), 0)
    lane = lax.broadcasted_iota(jnp.int32, (8, 512), 1) % L
    exponent = jnp.zeros((8, 512), jnp.int32)
    for h in range(4):
        exponent = jnp.where(row % 4 == h, de_ref[h], exponent)
    rate = jnp.exp2(exponent.astype(F32)) / 16384.0
    gate = jnp.concatenate([dg_ref[...]] * 2, axis=0)
    beta = jax.nn.sigmoid(jnp.concatenate([bl_ref[...]] * 2, axis=0))
    cum = -rate * gate
    for s in (1, 2, 4, 8, 16, 32, 64):
        cum = cum + jnp.where(lane >= s, pltpu.roll(cum, s, 1), 0.0)
    growth = jnp.exp(cum)
    for b in range(4):
        tokens = slice(L * b, L * b + L)
        now = cum[:, tokens]
        last = jnp.broadcast_to(now[:, L - 1 : L], (8, L))
        parts = [now, beta[:, tokens], growth[:, tokens]]
        rows_s[b] = jnp.concatenate(parts + [jnp.exp(last)], axis=0)
        padding = [jnp.zeros((L - 32, L), F32)]
        cols_s[b] = jnp.concatenate(parts + [jnp.exp(last - now)] + padding, axis=0).T


def solve_blocks(blocks, k_ref, v_ref, rows_s, cols_s, t1_s, fade_s, b_s, d_s, values_ready):
    row, lane = iotas()
    eye = jnp.where(row == lane, 1.0, 0.0).astype(F32)
    tokens = [pl.ds(pl.multiple_of(b * L, L), L) for b in blocks]
    rows = [rows_s[b] for b in blocks]
    columns = [cols_s[b] for b in blocks]
    places = [(n, kh) for n in range(len(blocks)) for kh in range(2)]
    keys = [k_ref[tokens[n], L * kh : L * kh + L] for n, kh in places]
    keys_t = [key.T for key in keys]
    norms = [
        lax.rsqrt(jnp.sum(key.astype(F32) * key.astype(F32), axis=1, keepdims=True) + EPS) for key in keys
    ]
    grams = [mm(key, key_t) for key, key_t in zip(keys, keys_t)]
    key_rows = []
    for n, b in enumerate(blocks):
        table = jnp.where(lane == 0, norms[2 * n], jnp.where(lane == 1, norms[2 * n + 1], 0.0))
        key_rows.append(table.T)
        rows_s[b, 28:30] = key_rows[n][:2]
    spots = [(n, h) for n in range(len(blocks)) for h in range(4)]
    systems = []
    for n, h in spots:
        kh = h // 2
        fade = jnp.exp(jnp.minimum(columns[n][:, h : h + 1] - rows[n][h : h + 1], 0.0))
        fade = fade * key_rows[n][kh : kh + 1]
        fade_s[4 * blocks[n] + h] = fade
        scaled = grams[2 * n + kh] * (norms[2 * n + kh] * columns[n][:, 8 + h : 9 + h])
        systems.append(jnp.where(row > lane, scaled * fade, 0.0))
    inverses = unit_lower_inverse(systems)
    t1s = [t * rows[n][8 + h : 9 + h] for t, (n, h) in zip(inverses, spots)]
    reaches = [rows[n][16 + h : 17 + h] * key_rows[n][h // 2 : h // 2 + 1] for n, h in spots]
    for (n, h), t1, reach in zip(spots, t1s, reaches):
        t1_s[4 * blocks[n] + h] = t1
        rows_s[blocks[n], 4 + h : 5 + h] = reach
    values_ready()
    written = [mm_exact_right(t1, v_ref[tokens[n], L * h : L * h + L]) for t1, (n, h) in zip(t1s, spots)]
    widened = [
        mm_exact_right(t1 * reach, keys[2 * n + h // 2]) for t1, reach, (n, h) in zip(t1s, reaches, spots)
    ]
    changes = []
    for (n, h), u, w in zip(spots, written, widened):
        rem = columns[n][:, 24 + h : 25 + h] * norms[2 * n + h // 2]
        wh, wl = split(jnp.concatenate([u * rem, w * rem], axis=1))
        kt = keys_t[2 * n + h // 2]
        changes.append(mm(jnp.concatenate([kt, kt], axis=1), jnp.concatenate([wh, wl], axis=0)))
    for (n, h), change in zip(spots, changes):
        d_s[4 * blocks[n] + h] = change[:, :L]
        b_s[4 * blocks[n] + h] = eye * rows[n][24 + h : 25 + h] - change[:, L:]


def output_block(b, q_ref, k_ref, v_ref, rows_s, cols_s, t1_s, fade_s, state_s, out_s, map_s):
    row, lane = iotas()
    tokens = pl.ds(pl.multiple_of(b * L, L), L)
    rows, columns = rows_s[b], cols_s[b]
    keys, queries, scales, grams = [], [], [], []
    for kh in range(2):
        key = k_ref[tokens, L * kh : L * kh + L]
        query = q_ref[tokens, L * kh : L * kh + L]
        query32 = query.astype(F32)
        scales.append(lax.rsqrt(jnp.sum(query32 * query32, axis=1, keepdims=True) + EPS) * (L**-0.5))
        grams.append(mm(query, key.T))
        keys.append(key)
        queries.append(query32)
    scores = [
        jnp.where(row >= lane, grams[h // 2] * scales[h // 2] * fade_s[4 * b + h], 0.0) for h in range(4)
    ]
    reads = [mm_wide(score, t1_s[4 * b + h]) for h, score in enumerate(scores)]
    from_values = [mm_exact_right(r, v_ref[tokens, L * h : L * h + L]) for h, r in enumerate(reads)]
    from_keys = [mm_exact_right(r * rows[4 + h : 5 + h], keys[h // 2]) for h, r in enumerate(reads)]
    for h in range(4):
        lead = queries[h // 2] * (columns[:, 16 + h : 17 + h] * scales[h // 2]) - from_keys[h]
        both = mm_three(lead, state_s[4 * b + h])
        out_s[4 * b + h] = both[:, :L] + from_values[h]
        map_s[4 * b + h] = jnp.concatenate(split(both[:, L:]), axis=1)


def pack(state):
    row, lane = iotas()
    kept = state.astype(BF16)
    lost = state[:, L:] - kept[:, L:].astype(F32)
    lost = jnp.sum(jnp.where(row == lane, lost, 0.0), axis=0, keepdims=True)
    lost = jnp.broadcast_to(jnp.concatenate([jnp.zeros((1, L), F32), lost], axis=1), (PACK - L, 2 * L))
    return jnp.concatenate([kept, lost.astype(BF16)], axis=0)


def lost_diagonal(packed):
    row, lane = iotas()
    return jnp.where(row == lane, packed[L : L + 1, L:].astype(F32), 0.0)


def unpack(packed):
    state = packed[:L].astype(F32)
    return jnp.concatenate([state[:, :L], state[:, L:] + lost_diagonal(packed)], axis=1)


def after(packed, state):
    m = packed[:L, L:]
    hi, lo = split(state)
    lhs = jnp.concatenate([m, lost_diagonal(packed).astype(BF16), m], axis=1)
    moved = mm(lhs, jnp.concatenate([hi, hi, lo], axis=0))
    return moved + jnp.concatenate([packed[:L, :L].astype(F32), jnp.zeros((L, L), F32)], axis=1)


def after_state(packed, state):
    m = packed[:L, L:]
    hi, lo = split(state)
    lhs = jnp.concatenate([m, lost_diagonal(packed).astype(BF16), m], axis=1)
    return mm(lhs, jnp.concatenate([hi, hi, lo], axis=0)) + packed[:L, :L].astype(F32)


def before(state, packed):
    hi, lo = split(state[:, L:])
    lost = jnp.concatenate([jnp.zeros((L, L), F32), lost_diagonal(packed)], axis=1).astype(BF16)
    moved = mm(
        jnp.concatenate([hi, lo, hi], axis=1), jnp.concatenate([packed[:L], packed[:L], lost], axis=0)
    )
    return moved + jnp.concatenate([state[:, :L], jnp.zeros((L, L), F32)], axis=1)


def layer_kernel(
    de_hbm, gain_hbm, q_hbm, k_hbm, v_hbm, bl_hbm, dg_hbm, gate_hbm, w_hbm, router_hbm, old_hbm,
    lo_ref, div_ref,
    de_ref, gain_ref, q_ref, k_ref, v_ref, bl_ref, dg_ref, gate_ref, w_ref, w2_ref, router_ref, old_ref,
    rows_s, cols_s, t1_s, fade_s, b_s, d_s, state_s, out_s, map_s,
    packs, gath, prefix, total, zbox, acc, first_half, starts, outbox, landed,
    gate_s, normed, nbox, ahead, own, ring1, box1, ring2, box2, ring3, box3,
    load, ys, yr, zs, zr, hs, hr, ls, lr, ws, wr, sc, rc, s1, r1, s2, r2, s3, r3,
):
    ctx = lax.axis_index("ctx")
    z, y = ctx // MESH_Y, lax.rem(ctx, MESH_Y)
    quad, zq = z // QUAD, lax.rem(z, QUAD)
    head = lax.axis_index("head")
    x, c = head // 2, lax.rem(head, 2)
    in_group = [to_ctx(z * MESH_Y + lax.rem(y + d, MESH_Y)) for d in range(1, MESH_Y)]
    right = to_head(lax.rem(x + 1, MESH_X) * 2 + c)
    left = to_head(lax.rem(x + MESH_X - 1, MESH_X) * 2 + c)
    twin = to_head(x * 2 + 1 - c)

    def at_z(other):
        return to_ctx(other * MESH_Y + y)

    loads = [
        pltpu.make_async_copy(src, dst, load.at[i])
        for i, (src, dst) in enumerate(
            (
                (de_hbm, de_ref), (bl_hbm, bl_ref), (dg_hbm, dg_ref), (k_hbm, k_ref), (v_hbm, v_ref),
                (q_hbm, q_ref), (w_hbm, w_ref), (gate_hbm, gate_ref), (gain_hbm, gain_ref),
                (router_hbm, router_ref), (old_hbm, old_ref),
            )
        )
    ]
    for copy in loads[:6]:
        copy.start()

    barrier = pltpu.get_barrier_semaphore()
    for device in in_group + [right, left, twin]:
        signal(barrier, device)
    for d in range(1, QUAD):
        signal(barrier, at_z(quad * QUAD + lax.rem(zq + d, QUAD)))
    serves = ((QUAD - 1, (QUAD, QUAD + 1)), (0, (2 * QUAD - 1, 2 * QUAD - 2)))
    for end, served in serves:

        @pl.when(z == end)
        def _():
            for other in served:
                signal(barrier, at_z(other))

        for other in served:

            @pl.when(z == other)
            def _():
                signal(barrier, at_z(end))

    for copy in loads[:3]:
        copy.wait()
    decay_tables(de_ref, bl_ref, dg_ref, rows_s, cols_s)
    loads[3].wait()
    for copy in loads[6:]:
        copy.start()
    solve_blocks(range(4), k_ref, v_ref, rows_s, cols_s, t1_s, fade_s, b_s, d_s, loads[4].wait)

    row, lane = iotas()
    zero = jnp.zeros((L, L), F32)
    eye = jnp.where(row == lane, 1.0, 0.0).astype(F32)
    states = []
    for h in range(4):
        state_s[h] = jnp.concatenate([zero, eye], axis=1)
        states.append(jnp.concatenate([d_s[h], b_s[h]], axis=1))
    for b in range(1, 4):
        for h in range(4):
            state_s[4 * b + h] = states[h]
        states = [
            mm_three(b_s[4 * b + h], states[h]) + jnp.concatenate([d_s[4 * b + h], zero], axis=1)
            for h in range(4)
        ]
    for h, packed in enumerate([pack(state) for state in states]):
        packs[h] = packed

    peers = MESH_Y - 1 + 3 + QUAD - 1

    @pl.when(jnp.logical_or(z == 0, z == QUAD - 1))
    def _():
        pl.semaphore_wait(barrier, peers + 2)

    @pl.when(jnp.logical_and(z > 0, z < QUAD - 1))
    def _():
        pl.semaphore_wait(barrier, peers)

    @pl.when(z >= QUAD)
    def _():
        pl.semaphore_wait(barrier, peers + 1)

    firsts = [
        remote(packs.at[lax.rem(y + d, MESH_Y)], gath.at[y], ys.at[d - 1], yr.at[d - 1], in_group[d - 1])
        for d in range(1, MESH_Y)
    ]
    for i in (1, 0, 2):
        firsts[i].start()
    gath[y] = packs[y]
    loads[6].wait()
    weights = remote(w_ref, w2_ref, ws.at[0], wr.at[0], twin)
    weights.start()
    loads[5].wait()

    def output(b, carry):
        output_block(b, q_ref, k_ref, v_ref, rows_s, cols_s, t1_s, fade_s, state_s, out_s, map_s)
        return carry

    lax.fori_loop(0, 4, output, 0)

    for copy in firsts:
        copy.wait_recv()
    prefix[0] = unpack(gath[0])
    prefix[1] = after(gath[1], prefix[0])
    upper = after(gath[3], unpack(gath[2]))
    state = mm_three(upper[:, L:], prefix[1]) + jnp.concatenate([upper[:, :L], zero], axis=1)
    total[...] = pack(state)

    def up_copy(d):
        device = at_z(quad * QUAD + lax.rem(zq + d, QUAD))
        return remote(total, zbox.at[zq], zs.at[d - 1], zr.at[d - 1], device)

    def down_copy(d):
        return remote(total, zbox.at[zq], zs.at[QUAD - 1], zr.at[QUAD - 2 + d], at_z(0))

    for d in range(QUAD - 1, 0, -1):

        @pl.when(zq + d < QUAD)
        def _():
            up_copy(d).start()

        @pl.when(z == d)
        def _():
            down_copy(d).start()

    prefix[2] = after(gath[2], prefix[1])
    for copy in loads[7:]:
        copy.wait()
    gain = jnp.concatenate([gain_ref[...]] * 4, axis=1)
    for b in range(4):
        gate = gate_ref[L * b : L * b + L, :].astype(F32)
        gate_s[L * b : L * b + L, :] = gain * (gate / (1.0 + jnp.exp(-gate)))
    old_logit = old_ref[...].astype(F32) / 1024.0
    old_logp = old_logit - jnp.log(jnp.sum(jnp.exp(old_logit), axis=1, keepdims=True))
    old_prob = jnp.exp(old_logp)
    old_part = jnp.sum(old_prob * old_logp, axis=1, keepdims=True)

    def half_copy(i, other):
        return remote(first_half.at[0], first_half.at[1], hs.at[i], hr.at[0], at_z(other))

    @pl.when(z == QUAD - 1)
    def _():
        reach = state
        for d in range(1, QUAD - 1):
            up_copy(d).wait_recv()
            reach = before(reach, zbox[QUAD - 1 - d])
        up_copy(QUAD - 1).wait_recv()
        first_half[0] = (reach[:, :L] + mm_exact_right(reach[:, L:], zbox[0, :L, :L])).astype(BF16)
        for i, other in enumerate(serves[0][1]):
            half_copy(i, other).start()

    acc[...] = jnp.concatenate([zero, eye], axis=1)
    for d in range(1, QUAD):

        @pl.when(zq - d >= 0)
        def _():
            @pl.when(z != QUAD - 1)
            def _():
                up_copy(d).wait_recv()

            acc[...] = unpack(zbox[zq - 1]) if d == 1 else before(acc[...], zbox[zq - d])

    starts[0:L] = acc[...]
    moved = mm_three(jnp.concatenate([prefix[j, :, L:] for j in range(MESH_Y - 1)], axis=0), acc[...])
    for j in range(1, MESH_Y):
        rows = slice(L * j, L * j + L)
        starts[rows, :L] = moved[L * (j - 1) : L * j, :L] + prefix[j - 1, :, :L]
        starts[rows, L:] = moved[L * (j - 1) : L * j, L:]

    @pl.when(z >= QUAD)
    def _():
        half_copy(0, QUAD).wait_recv()
        starts[:, :L] = starts[:, :L] + mm_exact_right(starts[:, L:], first_half[1])

    for j in range(MESH_Y):
        outbox[j] = starts[L * j : L * j + L, :L].astype(BF16)
    lasts = [
        remote(outbox.at[lax.rem(y + d, MESH_Y)], landed.at[y], ls.at[d - 1], lr.at[d - 1], in_group[d - 1])
        for d in range(1, MESH_Y)
    ]
    for i in (1, 0, 2):
        lasts[i].start()
    landed[y] = outbox[y]

    @pl.when(z == 0)
    def _():
        ended = state[:, :L]
        for d in range(1, QUAD):
            down_copy(d).wait_recv()
            ended = after_state(zbox[d], ended)
        first_half[0] = ended.astype(BF16)
        for i, other in enumerate(serves[1][1]):
            half_copy(i, other).start()

    weights.wait_recv()
    for copy in lasts:
        copy.wait_recv()

    order = [lax.rem(x + d, MESH_X) for d in (2, 1, 3, 0)]

    def send(src, dst, ssem, rsem, device):
        copy = remote(src, dst, ssem, rsem, device)
        copy.start()
        return copy

    def norm(i):
        rows = pl.ds(pl.multiple_of(order[i] * L, L), L)
        attended = [
            out_s[4 * order[i] + h] + mm(map_s[4 * order[i] + h], landed_twice[h]) for h in range(4)
        ]
        scales = [lax.rsqrt(jnp.mean(a * a, axis=1, keepdims=True) + EPS) for a in attended]
        parts = [
            (a * s * gate_s[rows, L * h : L * h + L]).astype(BF16)
            for h, (a, s) in enumerate(zip(attended, scales))
        ]
        normed[i] = jnp.concatenate(parts, axis=1)
        rows = pl.ds(pl.multiple_of((1 - c) * ROWS, ROWS), ROWS)
        return send(normed.at[i, rows], nbox.at[i], sc.at[i], rc.at[i], twin)

    def mine(i):
        return normed[i, pl.ds(pl.multiple_of(c * ROWS, ROWS), ROWS), :]

    landed_twice = [jnp.concatenate([landed[h], landed[h]], axis=0) for h in range(4)]
    near, far = slice(0, HALF), slice(HALF, WIDE)
    quarters = [slice(QUARTER * n, QUARTER * n + QUARTER) for n in range(4)]
    swaps = [norm(0)]
    for cols in quarters:
        ahead[:, cols] = mm(mine(0), w_ref[:, cols])
    swaps += [norm(i) for i in range(1, 4)]
    swaps[0].wait_recv()
    first = [None] * 4
    for n in (0, 2, 1, 3):
        ring1[n] = (ahead[:, quarters[n]] + mm(nbox[0], w2_ref[:, quarters[n]])).astype(BF16)
        first[n] = send(ring1.at[n], box1.at[n], s1.at[n], r1.at[n], right if n < 2 else left)
    for swap in swaps[1:]:
        swap.wait_recv()
    my_rows = jnp.concatenate([mine(1), mine(2), mine(3)], axis=0)
    twin_rows = jnp.concatenate([nbox[1], nbox[2], nbox[3]], axis=0)
    own[:, far] = mm(my_rows, w_ref[:, far]) + mm(twin_rows, w2_ref[:, far])
    ring2[0] = own[0:ROWS, far].astype(BF16)
    plain = [send(ring2.at[0], box2.at[0], s2.at[0], r2.at[0], right)]
    own[:, near] = mm(my_rows, w_ref[:, near]) + mm(twin_rows, w2_ref[:, near])
    ring2[1] = own[ROWS : 2 * ROWS, near].astype(BF16)
    plain.append(send(ring2.at[1], box2.at[1], s2.at[1], r2.at[1], left))
    second = [None] * 4
    for n in (0, 2, 1, 3):
        first[n].wait_recv()
        rows = slice(0, ROWS) if n < 2 else slice(ROWS, 2 * ROWS)
        ring3[n] = (own[rows, quarters[n]] + box1[n].astype(F32)).astype(BF16)
        second[n] = send(ring3.at[n], box3.at[n], s3.at[n], r3.at[n], right if n < 2 else left)
    for copy in plain:
        copy.wait_recv()
    own[2 * ROWS :, far] = own[2 * ROWS :, far] + box2[0].astype(F32)
    own[2 * ROWS :, near] = own[2 * ROWS :, near] + box2[1].astype(F32)
    new_logit = jnp.zeros((ROWS, 512), F32)
    for n in (0, 2, 1, 3):
        second[n].wait_recv()
        done = (own[2 * ROWS :, quarters[n]] + box3[n].astype(F32)).astype(BF16)
        lo_ref[:, quarters[n]] = done
        new_logit = new_logit + mm(done, router_ref[quarters[n]])
    new_logp = new_logit - jnp.log(jnp.sum(jnp.exp(new_logit), axis=1, keepdims=True))
    div = old_part - jnp.sum(old_prob * new_logp, axis=1, keepdims=True)
    div_ref[...] = jnp.broadcast_to(div, (ROWS, L)).T[0:1, :]

    for copy in firsts + lasts + swaps + first + plain + second + [weights]:
        copy.wait_send()
    for d in range(1, QUAD):

        @pl.when(zq + d < QUAD)
        def _():
            up_copy(d).wait_send()

        @pl.when(z == d)
        def _():
            down_copy(d).wait_send()

    for end, served in serves:

        @pl.when(z == end)
        def _():
            for i, other in enumerate(served):
                half_copy(i, other).wait_send()


def layer(*arrays):
    vm = pl.BlockSpec(memory_space=pltpu.VMEM)
    square = (MESH_Y, L, L)
    many = pltpu.VMEM((16, L, L), F32)
    wide = pltpu.VMEM((16, L, 2 * L), F32)
    dma = pltpu.SemaphoreType.DMA
    return pl.pallas_call(
        layer_kernel,
        out_shape=(
            jax.ShapeDtypeStruct((ROWS, WIDE), BF16),
            jax.ShapeDtypeStruct((1, ROWS), F32),
        ),
        in_specs=[pl.BlockSpec(memory_space=pltpu.HBM)] * 11,
        out_specs=(vm, vm),
        scratch_shapes=[
            pltpu.SMEM((4,), jnp.int32),
            pltpu.VMEM((1, L), F32),
            pltpu.VMEM((512, 256), BF16),
            pltpu.VMEM((512, 256), BF16),
            pltpu.VMEM((512, 512), BF16),
            pltpu.VMEM((4, 512), F32),
            pltpu.VMEM((4, 512), F32),
            pltpu.VMEM((512, 512), BF16),
            pltpu.VMEM((512, WIDE), BF16),
            pltpu.VMEM((512, WIDE), BF16),
            pltpu.VMEM((WIDE, 512), BF16),
            pltpu.VMEM((ROWS, 512), jnp.int32),
            pltpu.VMEM((4, 32, L), F32),
            pltpu.VMEM((4, L, L), F32),
            many, many, many, many, wide, many,
            pltpu.VMEM((16, L, 2 * L), BF16),
            pltpu.VMEM((MESH_Y, PACK, 2 * L), BF16),
            pltpu.VMEM((MESH_Y, PACK, 2 * L), BF16),
            pltpu.VMEM((MESH_Y - 1, L, 2 * L), F32),
            pltpu.VMEM((PACK, 2 * L), BF16),
            pltpu.VMEM((QUAD, PACK, 2 * L), BF16),
            pltpu.VMEM((L, 2 * L), F32),
            pltpu.VMEM((2, L, L), BF16),
            pltpu.VMEM((MESH_Y * L, 2 * L), F32),
            pltpu.VMEM(square, BF16),
            pltpu.VMEM(square, BF16),
            pltpu.VMEM((512, 512), F32),
            pltpu.VMEM((4, L, 512), BF16),
            pltpu.VMEM((4, ROWS, 512), BF16),
            pltpu.VMEM((ROWS, WIDE), F32),
            pltpu.VMEM((3 * ROWS, WIDE), F32),
            pltpu.VMEM((4, ROWS, QUARTER), BF16),
            pltpu.VMEM((4, ROWS, QUARTER), BF16),
            pltpu.VMEM((2, ROWS, HALF), BF16),
            pltpu.VMEM((2, ROWS, HALF), BF16),
            pltpu.VMEM((4, ROWS, QUARTER), BF16),
            pltpu.VMEM((4, ROWS, QUARTER), BF16),
            dma((11,)),
            dma((3,)), dma((3,)),
            dma((QUAD,)), dma((2 * QUAD - 2,)),
            dma((2,)), dma((1,)),
            dma((3,)), dma((3,)),
            dma((1,)), dma((1,)),
            dma((4,)), dma((4,)), dma((4,)), dma((4,)), dma((2,)), dma((2,)), dma((4,)), dma((4,)),
        ],
        compiler_params=pltpu.CompilerParams(
            collective_id=0, has_side_effects=True, vmem_limit_bytes=36 * 1024 * 1024
        ),
    )(*arrays)


def solution(mesh):
    def local(
        queries, key_vec, values, out_gate, beta_logit, decay_gate, decay_exp,
        norm_gain, out_weight, router_weight, old_scores,
    ):
        arrays = (
            decay_exp, norm_gain.reshape(1, L), queries, key_vec, values, beta_logit, decay_gate,
            out_gate, out_weight, router_weight, old_scores,
        )
        layer_out, div = layer(*(pltpu.with_memory_space_constraint(a, pltpu.HBM) for a in arrays))
        return layer_out, div.reshape(ROWS)

    placed = (
        P("ctx", "head"), P("ctx", "head"), P("ctx", "head"), P("ctx", "head"), P("head", "ctx"),
        P("head", "ctx"), P("head"), P(), P("head", None), P(), P(("ctx", "head"), None),
    )
    return jax.shard_map(
        local,
        mesh=mesh,
        in_specs=placed,
        out_specs=(P(("ctx", "head"), None), P(("ctx", "head"))),
        check_vma=False,
    )
```

```python
import jax
import jax.numpy as jnp
from jax import lax
from jax.experimental import pallas as pl
from jax.experimental.pallas import tpu as pltpu
from jax.sharding import PartitionSpec as P

F32 = jnp.float32
BF16 = jnp.bfloat16
L = 128
EPS = 1e-6


def mm(a, b):
    return jnp.dot(a, b, preferred_element_type=F32)


def split(x):
    hi = x.astype(BF16)
    return hi, (x - hi.astype(F32)).astype(BF16)


def mm_wide(a, b):
    ah, al = split(a)
    bh, bl = split(b)
    row = jnp.concatenate([bh, bl], axis=1)
    r = mm(jnp.concatenate([ah, al], axis=1), jnp.concatenate([row, row], axis=0))
    n = b.shape[1]
    return r[:, :n] + r[:, n:]


def four_products(a, b):
    row = jnp.concatenate(b, axis=1)
    r = mm(jnp.concatenate(a, axis=1), jnp.concatenate([row, row], axis=0))
    return r[:, :L] + r[:, L:]


def mm_three(a, b):
    ah, al = split(a)
    bh, bl = split(b)
    return mm(jnp.concatenate([ah, al, ah], axis=1), jnp.concatenate([bh, bh, bl], axis=0))


def mm_exact_right(a, b16):
    ah, al = split(a)
    return mm(jnp.concatenate([ah, al], axis=1), jnp.concatenate([b16, b16], axis=0))


def odd_rows(x, s):
    if s == 64:
        return x[64:]
    return jnp.concatenate([x[i : i + s] for i in range(s, L, 2 * s)], axis=0)


def even_rows(x, s):
    return jnp.concatenate([x[i : i + s] for i in range(0, L, 2 * s)], axis=0)


def interleave(even, odd, s):
    parts = []
    for i in range(0, L // 2, s):
        parts += [even[i : i + s], odd[i : i + s]]
    return jnp.concatenate(parts, axis=0)


def weave(even, odd, s):
    parts = []
    for n, i in enumerate(range(0, L, 2 * s)):
        parts += [even[i : i + s], odd[n * s : (n + 1) * s]]
    return jnp.concatenate(parts, axis=0)


def unit_lower_inverse(systems):
    lane16 = lax.broadcasted_iota(jnp.int32, (16, L), 1)
    row16 = lax.broadcasted_iota(jnp.int32, (16, L), 0)
    place = lane16 // 16
    bands = []
    for a in systems:
        band = jnp.zeros((16, L), F32)
        for b in range(L // 16):
            band = jnp.where(place == b, a[16 * b : 16 * b + 16], band)
        bands.append(band)
    start = jnp.where(lane16 % 16 == row16, 1.0, 0.0).astype(F32)
    solved = [start for _ in systems]
    for m in range(15):
        index = place * 16 + m
        spread = [jnp.take_along_axis(band, index, axis=1) for band in bands]
        solved = [r - s * r[m : m + 1] for r, s in zip(solved, spread)]
    row = lax.broadcasted_iota(jnp.int32, (L, L), 0)
    lane = lax.broadcasted_iota(jnp.int32, (L, L), 1)
    same = row // 16 == lane // 16
    inverses = [jnp.where(same, jnp.concatenate([r] * (L // 16), axis=0), 0.0) for r in solved]
    halves = [split(t) for t in inverses]
    twos = range(0, len(systems), 2)
    for s in (16, 32, 64):
        below = odd_rows(row // s, s) == odd_rows(lane // s, s) + 1
        lower = []
        for n in twos:
            one, two = (jnp.where(below, odd_rows(a, s), 0.0) for a in systems[n : n + 2])
            left = split(jnp.concatenate([one, pltpu.roll(two, s, 1)], axis=0))
            right = [interleave(even_rows(p, s), even_rows(q, s), s) for p, q in zip(halves[n], halves[n + 1])]
            lower.append(four_products(left, right))
        change = []
        for n, y in zip(twos, lower):
            one, two = (odd_rows(t, s) for t in inverses[n : n + 2])
            left = split(jnp.concatenate([one, pltpu.roll(two, L - s, 1)], axis=0))
            right = [interleave(p[L // 2 :], p[: L // 2], s) for p in split(y)]
            change.append(four_products(left, right))
        fresh = []
        for n, c in zip(twos, change):
            fresh += [odd_rows(inverses[n], s) - c[: L // 2], odd_rows(inverses[n + 1], s) - c[L // 2 :]]
        inverses = [weave(t, f, s) for t, f in zip(inverses, fresh)]
        if s < 64:
            halves = [[weave(p, q, s) for p, q in zip(half, split(f))] for half, f in zip(halves, fresh)]
    return inverses


ROWS = 64
WIDE = 2048
HALF = WIDE // 2
QUARTER = WIDE // 4
MESH_X = 4
MESH_Y = 4
QUAD = 4
PACK = L + 16


def to_ctx(ctx):
    return {"ctx": ctx}


def to_head(head):
    return {"head": head}


def signal(semaphore, device):
    pl.semaphore_signal(semaphore, inc=1, device_id=device, device_id_type=pl.DeviceIdType.MESH)


def remote(src, dst, send_sem, recv_sem, device):
    return pltpu.make_async_remote_copy(
        src_ref=src, dst_ref=dst, send_sem=send_sem, recv_sem=recv_sem,
        device_id=device, device_id_type=pl.DeviceIdType.MESH,
    )


def iotas():
    return lax.broadcasted_iota(jnp.int32, (L, L), 0), lax.broadcasted_iota(jnp.int32, (L, L), 1)


def decay_tables(de_ref, bl_ref, dg_ref, rows_s, cols_s):
    row = lax.broadcasted_iota(jnp.int32, (8, 512), 0)
    lane = lax.broadcasted_iota(jnp.int32, (8, 512), 1) % L
    exponent = jnp.zeros((8, 512), jnp.int32)
    for h in range(4):
        exponent = jnp.where(row % 4 == h, de_ref[h], exponent)
    rate = jnp.exp2(exponent.astype(F32)) / 16384.0
    gate = jnp.concatenate([dg_ref[...]] * 2, axis=0)
    beta = jax.nn.sigmoid(jnp.concatenate([bl_ref[...]] * 2, axis=0))
    cum = -rate * gate
    for s in (1, 2, 4, 8, 16, 32, 64):
        cum = cum + jnp.where(lane >= s, pltpu.roll(cum, s, 1), 0.0)
    growth = jnp.exp(cum)
    for b in range(4):
        tokens = slice(L * b, L * b + L)
        now = cum[:, tokens]
        last = jnp.broadcast_to(now[:, L - 1 : L], (8, L))
        parts = [now, beta[:, tokens], growth[:, tokens]]
        rows_s[b] = jnp.concatenate(parts + [jnp.exp(last)], axis=0)
        padding = [jnp.zeros((L - 32, L), F32)]
        cols_s[b] = jnp.concatenate(parts + [jnp.exp(last - now)] + padding, axis=0).T


def solve_blocks(blocks, k_ref, v_ref, rows_s, cols_s, t1_s, fade_s, b_s, d_s, values_ready):
    row, lane = iotas()
    eye = jnp.where(row == lane, 1.0, 0.0).astype(F32)
    tokens = [pl.ds(pl.multiple_of(b * L, L), L) for b in blocks]
    rows = [rows_s[b] for b in blocks]
    columns = [cols_s[b] for b in blocks]
    places = [(n, kh) for n in range(len(blocks)) for kh in range(2)]
    keys = [k_ref[tokens[n], L * kh : L * kh + L] for n, kh in places]
    keys_t = [key.T for key in keys]
    norms = [
        lax.rsqrt(jnp.sum(key.astype(F32) * key.astype(F32), axis=1, keepdims=True) + EPS) for key in keys
    ]
    grams = [mm(key, key_t) for key, key_t in zip(keys, keys_t)]
    key_rows = []
    for n, b in enumerate(blocks):
        table = jnp.where(lane == 0, norms[2 * n], jnp.where(lane == 1, norms[2 * n + 1], 0.0))
        key_rows.append(table.T)
        rows_s[b, 28:30] = key_rows[n][:2]
    spots = [(n, h) for n in range(len(blocks)) for h in range(4)]
    systems = []
    for n, h in spots:
        kh = h // 2
        fade = jnp.exp(jnp.minimum(columns[n][:, h : h + 1] - rows[n][h : h + 1], 0.0))
        fade = fade * key_rows[n][kh : kh + 1]
        fade_s[4 * blocks[n] + h] = fade
        scaled = grams[2 * n + kh] * (norms[2 * n + kh] * columns[n][:, 8 + h : 9 + h])
        systems.append(jnp.where(row > lane, scaled * fade, 0.0))
    inverses = unit_lower_inverse(systems)
    t1s = [t * rows[n][8 + h : 9 + h] for t, (n, h) in zip(inverses, spots)]
    reaches = [rows[n][16 + h : 17 + h] * key_rows[n][h // 2 : h // 2 + 1] for n, h in spots]
    for (n, h), t1, reach in zip(spots, t1s, reaches):
        t1_s[4 * blocks[n] + h] = t1
        rows_s[blocks[n], 4 + h : 5 + h] = reach
    values_ready()
    written = [mm_exact_right(t1, v_ref[tokens[n], L * h : L * h + L]) for t1, (n, h) in zip(t1s, spots)]
    widened = [
        mm_exact_right(t1 * reach, keys[2 * n + h // 2]) for t1, reach, (n, h) in zip(t1s, reaches, spots)
    ]
    changes = []
    for (n, h), u, w in zip(spots, written, widened):
        rem = columns[n][:, 24 + h : 25 + h] * norms[2 * n + h // 2]
        wh, wl = split(jnp.concatenate([u * rem, w * rem], axis=1))
        kt = keys_t[2 * n + h // 2]
        changes.append(mm(jnp.concatenate([kt, kt], axis=1), jnp.concatenate([wh, wl], axis=0)))
    for (n, h), change in zip(spots, changes):
        d_s[4 * blocks[n] + h] = change[:, :L]
        b_s[4 * blocks[n] + h] = eye * rows[n][24 + h : 25 + h] - change[:, L:]


def output_block(b, q_ref, k_ref, v_ref, rows_s, cols_s, t1_s, fade_s, state_s, out_s, map_s):
    row, lane = iotas()
    tokens = pl.ds(pl.multiple_of(b * L, L), L)
    rows, columns = rows_s[b], cols_s[b]
    keys, queries, scales, grams = [], [], [], []
    for kh in range(2):
        key = k_ref[tokens, L * kh : L * kh + L]
        query = q_ref[tokens, L * kh : L * kh + L]
        query32 = query.astype(F32)
        scales.append(lax.rsqrt(jnp.sum(query32 * query32, axis=1, keepdims=True) + EPS) * (L**-0.5))
        grams.append(mm(query, key.T))
        keys.append(key)
        queries.append(query32)
    scores = [
        jnp.where(row >= lane, grams[h // 2] * scales[h // 2] * fade_s[4 * b + h], 0.0) for h in range(4)
    ]
    reads = [mm_wide(score, t1_s[4 * b + h]) for h, score in enumerate(scores)]
    from_values = [mm_exact_right(r, v_ref[tokens, L * h : L * h + L]) for h, r in enumerate(reads)]
    from_keys = [mm_exact_right(r * rows[4 + h : 5 + h], keys[h // 2]) for h, r in enumerate(reads)]
    for h in range(4):
        lead = queries[h // 2] * (columns[:, 16 + h : 17 + h] * scales[h // 2]) - from_keys[h]
        both = mm_three(lead, state_s[4 * b + h])
        out_s[4 * b + h] = both[:, :L] + from_values[h]
        map_s[4 * b + h] = jnp.concatenate(split(both[:, L:]), axis=1)


def pack(state):
    row, lane = iotas()
    kept = state.astype(BF16)
    lost = state[:, L:] - kept[:, L:].astype(F32)
    lost = jnp.sum(jnp.where(row == lane, lost, 0.0), axis=0, keepdims=True)
    lost = jnp.broadcast_to(jnp.concatenate([jnp.zeros((1, L), F32), lost], axis=1), (PACK - L, 2 * L))
    return jnp.concatenate([kept, lost.astype(BF16)], axis=0)


def lost_diagonal(packed):
    row, lane = iotas()
    return jnp.where(row == lane, packed[L : L + 1, L:].astype(F32), 0.0)


def unpack(packed):
    state = packed[:L].astype(F32)
    return jnp.concatenate([state[:, :L], state[:, L:] + lost_diagonal(packed)], axis=1)


def after(packed, state):
    m = packed[:L, L:]
    hi, lo = split(state)
    lhs = jnp.concatenate([m, lost_diagonal(packed).astype(BF16), m], axis=1)
    moved = mm(lhs, jnp.concatenate([hi, hi, lo], axis=0))
    return moved + jnp.concatenate([packed[:L, :L].astype(F32), jnp.zeros((L, L), F32)], axis=1)


def after_state(packed, state):
    m = packed[:L, L:]
    hi, lo = split(state)
    lhs = jnp.concatenate([m, lost_diagonal(packed).astype(BF16), m], axis=1)
    return mm(lhs, jnp.concatenate([hi, hi, lo], axis=0)) + packed[:L, :L].astype(F32)


def before(state, packed):
    hi, lo = split(state[:, L:])
    lost = jnp.concatenate([jnp.zeros((L, L), F32), lost_diagonal(packed)], axis=1).astype(BF16)
    moved = mm(
        jnp.concatenate([hi, lo, hi], axis=1), jnp.concatenate([packed[:L], packed[:L], lost], axis=0)
    )
    return moved + jnp.concatenate([state[:, :L], jnp.zeros((L, L), F32)], axis=1)


def layer_kernel(
    de_hbm, gain_hbm, q_hbm, k_hbm, v_hbm, bl_hbm, dg_hbm, gate_hbm, w_hbm, router_hbm, old_hbm,
    lo_ref, logit_ref, prob_ref, part_ref,
    de_ref, gain_ref, q_ref, k_ref, v_ref, bl_ref, dg_ref, gate_ref, w_ref, w2_ref, router_ref, old_ref,
    rows_s, cols_s, t1_s, fade_s, b_s, d_s, state_s, out_s, map_s,
    packs, gath, prefix, total, zbox, acc, first_half, starts, outbox, landed,
    gate_s, normed, nbox, ahead, own, ring1, box1, ring2, box2, ring3, box3,
    load, ys, yr, zs, zr, hs, hr, ls, lr, ws, wr, sc, rc, s1, r1, s2, r2, s3, r3,
):
    ctx = lax.axis_index("ctx")
    z, y = ctx // MESH_Y, lax.rem(ctx, MESH_Y)
    quad, zq = z // QUAD, lax.rem(z, QUAD)
    head = lax.axis_index("head")
    x, c = head // 2, lax.rem(head, 2)
    in_group = [to_ctx(z * MESH_Y + lax.rem(y + d, MESH_Y)) for d in range(1, MESH_Y)]
    right = to_head(lax.rem(x + 1, MESH_X) * 2 + c)
    left = to_head(lax.rem(x + MESH_X - 1, MESH_X) * 2 + c)
    twin = to_head(x * 2 + 1 - c)

    def at_z(other):
        return to_ctx(other * MESH_Y + y)

    loads = [
        pltpu.make_async_copy(src, dst, load.at[i])
        for i, (src, dst) in enumerate(
            (
                (de_hbm, de_ref), (bl_hbm, bl_ref), (dg_hbm, dg_ref), (k_hbm, k_ref), (v_hbm, v_ref),
                (q_hbm, q_ref), (w_hbm, w_ref), (gate_hbm, gate_ref), (gain_hbm, gain_ref),
                (router_hbm, router_ref), (old_hbm, old_ref),
            )
        )
    ]
    for copy in loads[:6]:
        copy.start()

    zbox[0] = jnp.zeros((PACK, 2 * L), BF16)
    barrier = pltpu.get_barrier_semaphore()
    for device in in_group + [right, left, twin]:
        signal(barrier, device)
    for d in range(1, QUAD):
        signal(barrier, at_z(quad * QUAD + lax.rem(zq + d, QUAD)))
    serves = ((QUAD - 1, (QUAD, QUAD + 1)), (0, (2 * QUAD - 1, 2 * QUAD - 2)))
    for end, served in serves:

        @pl.when(z == end)
        def _():
            for other in served:
                signal(barrier, at_z(other))

        for other in served:

            @pl.when(z == other)
            def _():
                signal(barrier, at_z(end))

    for copy in loads[:3]:
        copy.wait()
    decay_tables(de_ref, bl_ref, dg_ref, rows_s, cols_s)
    loads[3].wait()
    for copy in loads[6:]:
        copy.start()
    solve_blocks(range(4), k_ref, v_ref, rows_s, cols_s, t1_s, fade_s, b_s, d_s, loads[4].wait)

    row, lane = iotas()
    zero = jnp.zeros((L, L), F32)
    eye = jnp.where(row == lane, 1.0, 0.0).astype(F32)
    states = []
    for h in range(4):
        state_s[h] = jnp.concatenate([zero, eye], axis=1)
        states.append(jnp.concatenate([d_s[h], b_s[h]], axis=1))
    for b in range(1, 4):
        for h in range(4):
            state_s[4 * b + h] = states[h]
        states = [
            mm_three(b_s[4 * b + h], states[h]) + jnp.concatenate([d_s[4 * b + h], zero], axis=1)
            for h in range(4)
        ]
    for h, packed in enumerate([pack(state) for state in states]):
        packs[h] = packed

    peers = MESH_Y - 1 + 3 + QUAD - 1

    @pl.when(jnp.logical_or(z == 0, z == QUAD - 1))
    def _():
        pl.semaphore_wait(barrier, peers + 2)

    @pl.when(jnp.logical_and(z > 0, z < QUAD - 1))
    def _():
        pl.semaphore_wait(barrier, peers)

    @pl.when(z >= QUAD)
    def _():
        pl.semaphore_wait(barrier, peers + 1)

    firsts = [
        remote(packs.at[lax.rem(y + d, MESH_Y)], gath.at[y], ys.at[d - 1], yr.at[d - 1], in_group[d - 1])
        for d in range(1, MESH_Y)
    ]
    for i in (1, 0, 2):
        firsts[i].start()
    gath[y] = packs[y]
    loads[6].wait()
    weights = remote(w_ref, w2_ref, ws.at[0], wr.at[0], twin)
    weights.start()
    loads[5].wait()

    def output(b, carry):
        output_block(b, q_ref, k_ref, v_ref, rows_s, cols_s, t1_s, fade_s, state_s, out_s, map_s)
        return carry

    lax.fori_loop(0, 4, output, 0)

    for copy in firsts:
        copy.wait_recv()
    prefix[0] = unpack(gath[0])
    prefix[1] = after(gath[1], prefix[0])
    upper = after(gath[3], unpack(gath[2]))
    state = mm_three(upper[:, L:], prefix[1]) + jnp.concatenate([upper[:, :L], zero], axis=1)
    total[...] = pack(state)

    def up_copy(d):
        device = at_z(quad * QUAD + lax.rem(zq + d, QUAD))
        return remote(total, zbox.at[zq], zs.at[d - 1], zr.at[d - 1], device)

    def first_copy(d):
        part = (pl.ds(0, L), pl.ds(0, L))
        return remote(total.at[part], zbox.at[(0, *part)], zs.at[d - 1], zr.at[d - 1], at_z(d))

    def down_copy(d):
        return remote(total, zbox.at[zq], zs.at[QUAD - 1], zr.at[QUAD - 2 + d], at_z(0))

    for d in range(QUAD - 1, 0, -1):

        @pl.when(z == 0)
        def _():
            first_copy(d).start()

        @pl.when(jnp.logical_and(z > 0, zq + d < QUAD))
        def _():
            up_copy(d).start()

        @pl.when(z == d)
        def _():
            down_copy(d).start()

    prefix[2] = after(gath[2], prefix[1])
    for copy in loads[7:]:
        copy.wait()
    gain = jnp.concatenate([gain_ref[...]] * 4, axis=1)
    for b in range(4):
        gate = gate_ref[L * b : L * b + L, :].astype(F32)
        gate_s[L * b : L * b + L, :] = gain * (gate / (1.0 + jnp.exp(-gate)))
    old_logit = old_ref[...].astype(F32) / 1024.0
    old_logp = old_logit - jnp.log(jnp.sum(jnp.exp(old_logit), axis=1, keepdims=True))
    old_prob = jnp.exp(old_logp)
    prob_ref[...] = old_prob
    part_ref[...] = jnp.broadcast_to(jnp.sum(old_prob * old_logp, axis=1, keepdims=True), (ROWS, L))

    def half_copy(i, other):
        return remote(first_half.at[0], first_half.at[1], hs.at[i], hr.at[0], at_z(other))

    @pl.when(z == QUAD - 1)
    def _():
        reach = state
        for d in range(1, QUAD - 1):
            up_copy(d).wait_recv()
            reach = before(reach, zbox[QUAD - 1 - d])
        first_copy(QUAD - 1).wait_recv()
        first_half[0] = (reach[:, :L] + mm_exact_right(reach[:, L:], zbox[0, :L, :L])).astype(BF16)
        for i, other in enumerate(serves[0][1]):
            half_copy(i, other).start()

    acc[...] = jnp.concatenate([zero, eye], axis=1)
    for d in range(1, QUAD):

        @pl.when(zq - d >= 0)
        def _():
            @pl.when(jnp.logical_and(z == d, d < QUAD - 1))
            def _():
                first_copy(d).wait_recv()

            @pl.when(jnp.logical_and(z != QUAD - 1, z != d))
            def _():
                up_copy(d).wait_recv()

            acc[...] = unpack(zbox[zq - 1]) if d == 1 else before(acc[...], zbox[zq - d])

    starts[0:L] = acc[...]
    moved = mm_three(jnp.concatenate([prefix[j, :, L:] for j in range(MESH_Y - 1)], axis=0), acc[...])
    for j in range(1, MESH_Y):
        rows = slice(L * j, L * j + L)
        starts[rows, :L] = moved[L * (j - 1) : L * j, :L] + prefix[j - 1, :, :L]
        starts[rows, L:] = moved[L * (j - 1) : L * j, L:]

    @pl.when(z >= QUAD)
    def _():
        half_copy(0, QUAD).wait_recv()
        starts[:, :L] = starts[:, :L] + mm_exact_right(starts[:, L:], first_half[1])

    for j in range(MESH_Y):
        outbox[j] = starts[L * j : L * j + L, :L].astype(BF16)
    lasts = [
        remote(outbox.at[lax.rem(y + d, MESH_Y)], landed.at[y], ls.at[d - 1], lr.at[d - 1], in_group[d - 1])
        for d in range(1, MESH_Y)
    ]
    for i in (1, 0, 2):
        lasts[i].start()
    landed[y] = outbox[y]

    @pl.when(z == 0)
    def _():
        ended = state[:, :L]
        for d in range(1, QUAD):
            down_copy(d).wait_recv()
            ended = after_state(zbox[d], ended)
        first_half[0] = ended.astype(BF16)
        for i, other in enumerate(serves[1][1]):
            half_copy(i, other).start()

    weights.wait_recv()
    for copy in lasts:
        copy.wait_recv()

    order = [lax.rem(x + d, MESH_X) for d in (2, 1, 3, 0)]

    def send(src, dst, ssem, rsem, device):
        copy = remote(src, dst, ssem, rsem, device)
        copy.start()
        return copy

    def norm(i):
        rows = pl.ds(pl.multiple_of(order[i] * L, L), L)
        attended = [
            out_s[4 * order[i] + h] + mm(map_s[4 * order[i] + h], landed_twice[h]) for h in range(4)
        ]
        scales = [lax.rsqrt(jnp.mean(a * a, axis=1, keepdims=True) + EPS) for a in attended]
        parts = [
            (a * s * gate_s[rows, L * h : L * h + L]).astype(BF16)
            for h, (a, s) in enumerate(zip(attended, scales))
        ]
        normed[i] = jnp.concatenate(parts, axis=1)
        rows = pl.ds(pl.multiple_of((1 - c) * ROWS, ROWS), ROWS)
        return send(normed.at[i, rows], nbox.at[i], sc.at[i], rc.at[i], twin)

    def mine(i):
        return normed[i, pl.ds(pl.multiple_of(c * ROWS, ROWS), ROWS), :]

    landed_twice = [jnp.concatenate([landed[h], landed[h]], axis=0) for h in range(4)]
    near, far = slice(0, HALF), slice(HALF, WIDE)
    quarters = [slice(QUARTER * n, QUARTER * n + QUARTER) for n in range(4)]
    swaps = [norm(0)]
    swaps[0].wait_recv()
    first = [None] * 4
    for n in (0, 2, 1, 3):
        ring1[n] = (mm(mine(0), w_ref[:, quarters[n]]) + mm(nbox[0], w2_ref[:, quarters[n]])).astype(BF16)
        first[n] = send(ring1.at[n], box1.at[n], s1.at[n], r1.at[n], right if n < 2 else left)
    swaps += [norm(i) for i in range(1, 4)]
    for swap in swaps[1:]:
        swap.wait_recv()
    my_rows = jnp.concatenate([mine(1), mine(2), mine(3)], axis=0)
    twin_rows = jnp.concatenate([nbox[1], nbox[2], nbox[3]], axis=0)
    own[:, far] = mm(my_rows, w_ref[:, far]) + mm(twin_rows, w2_ref[:, far])
    ring2[0] = own[0:ROWS, far].astype(BF16)
    plain = [send(ring2.at[0], box2.at[0], s2.at[0], r2.at[0], right)]
    own[:, near] = mm(my_rows, w_ref[:, near]) + mm(twin_rows, w2_ref[:, near])
    ring2[1] = own[ROWS : 2 * ROWS, near].astype(BF16)
    plain.append(send(ring2.at[1], box2.at[1], s2.at[1], r2.at[1], left))
    second = [None] * 4
    for n in (0, 2, 1, 3):
        first[n].wait_recv()
        rows = slice(0, ROWS) if n < 2 else slice(ROWS, 2 * ROWS)
        ring3[n] = (own[rows, quarters[n]] + box1[n].astype(F32)).astype(BF16)
        second[n] = send(ring3.at[n], box3.at[n], s3.at[n], r3.at[n], right if n < 2 else left)
    for copy in plain:
        copy.wait_recv()
    own[2 * ROWS :, far] = own[2 * ROWS :, far] + box2[0].astype(F32)
    own[2 * ROWS :, near] = own[2 * ROWS :, near] + box2[1].astype(F32)
    new_logit = jnp.zeros((ROWS, 512), F32)
    for n in (0, 2, 1, 3):
        second[n].wait_recv()
        done = (own[2 * ROWS :, quarters[n]] + box3[n].astype(F32)).astype(BF16)
        lo_ref[:, quarters[n]] = done
        new_logit = new_logit + mm(done, router_ref[quarters[n]])
    logit_ref[...] = new_logit

    for copy in firsts + lasts + swaps + first + plain + second + [weights]:
        copy.wait_send()
    for d in range(1, QUAD):

        @pl.when(z == 0)
        def _():
            first_copy(d).wait_send()

        @pl.when(jnp.logical_and(z > 0, zq + d < QUAD))
        def _():
            up_copy(d).wait_send()

        @pl.when(z == d)
        def _():
            down_copy(d).wait_send()

    for end, served in serves:

        @pl.when(z == end)
        def _():
            for i, other in enumerate(served):
                half_copy(i, other).wait_send()


def layer(*arrays):
    vm = pl.BlockSpec(memory_space=pltpu.VMEM)
    square = (MESH_Y, L, L)
    many = pltpu.VMEM((16, L, L), F32)
    wide = pltpu.VMEM((16, L, 2 * L), F32)
    dma = pltpu.SemaphoreType.DMA
    return pl.pallas_call(
        layer_kernel,
        out_shape=(
            jax.ShapeDtypeStruct((ROWS, WIDE), BF16),
            jax.ShapeDtypeStruct((ROWS, 512), F32),
            jax.ShapeDtypeStruct((ROWS, 512), F32),
            jax.ShapeDtypeStruct((ROWS, L), F32),
        ),
        in_specs=[pl.BlockSpec(memory_space=pltpu.HBM)] * 11,
        out_specs=(vm,) * 4,
        scratch_shapes=[
            pltpu.SMEM((4,), jnp.int32),
            pltpu.VMEM((1, L), F32),
            pltpu.VMEM((512, 256), BF16),
            pltpu.VMEM((512, 256), BF16),
            pltpu.VMEM((512, 512), BF16),
            pltpu.VMEM((4, 512), F32),
            pltpu.VMEM((4, 512), F32),
            pltpu.VMEM((512, 512), BF16),
            pltpu.VMEM((512, WIDE), BF16),
            pltpu.VMEM((512, WIDE), BF16),
            pltpu.VMEM((WIDE, 512), BF16),
            pltpu.VMEM((ROWS, 512), jnp.int32),
            pltpu.VMEM((4, 32, L), F32),
            pltpu.VMEM((4, L, L), F32),
            many, many, many, many, wide, many,
            pltpu.VMEM((16, L, 2 * L), BF16),
            pltpu.VMEM((MESH_Y, PACK, 2 * L), BF16),
            pltpu.VMEM((MESH_Y, PACK, 2 * L), BF16),
            pltpu.VMEM((MESH_Y - 1, L, 2 * L), F32),
            pltpu.VMEM((PACK, 2 * L), BF16),
            pltpu.VMEM((QUAD, PACK, 2 * L), BF16),
            pltpu.VMEM((L, 2 * L), F32),
            pltpu.VMEM((2, L, L), BF16),
            pltpu.VMEM((MESH_Y * L, 2 * L), F32),
            pltpu.VMEM(square, BF16),
            pltpu.VMEM(square, BF16),
            pltpu.VMEM((512, 512), F32),
            pltpu.VMEM((4, L, 512), BF16),
            pltpu.VMEM((4, ROWS, 512), BF16),
            pltpu.VMEM((ROWS, WIDE), F32),
            pltpu.VMEM((3 * ROWS, WIDE), F32),
            pltpu.VMEM((4, ROWS, QUARTER), BF16),
            pltpu.VMEM((4, ROWS, QUARTER), BF16),
            pltpu.VMEM((2, ROWS, HALF), BF16),
            pltpu.VMEM((2, ROWS, HALF), BF16),
            pltpu.VMEM((4, ROWS, QUARTER), BF16),
            pltpu.VMEM((4, ROWS, QUARTER), BF16),
            dma((11,)),
            dma((3,)), dma((3,)),
            dma((QUAD,)), dma((2 * QUAD - 2,)),
            dma((2,)), dma((1,)),
            dma((3,)), dma((3,)),
            dma((1,)), dma((1,)),
            dma((4,)), dma((4,)), dma((4,)), dma((4,)), dma((2,)), dma((2,)), dma((4,)), dma((4,)),
        ],
        compiler_params=pltpu.CompilerParams(
            collective_id=0, has_side_effects=True, vmem_limit_bytes=36 * 1024 * 1024
        ),
    )(*arrays)


def close_kernel(lo_ref, logit_ref, prob_ref, part_ref, lo_hbm, div_hbm, div_ref, out):
    copies = [pltpu.make_async_copy(lo_ref, lo_hbm, out.at[0]), pltpu.make_async_copy(div_ref, div_hbm, out.at[1])]
    copies[0].start()
    new_logit = logit_ref[...]
    new_logp = new_logit - jnp.log(jnp.sum(jnp.exp(new_logit), axis=1, keepdims=True))
    div = part_ref[:, 0:1] - jnp.sum(prob_ref[...] * new_logp, axis=1, keepdims=True)
    div_ref[...] = jnp.broadcast_to(div, (ROWS, L)).T[0:1, :]
    copies[1].start()
    for copy in copies:
        copy.wait()


def close(*arrays):
    vm, hbm = pl.BlockSpec(memory_space=pltpu.VMEM), pl.BlockSpec(memory_space=pltpu.HBM)
    return pl.pallas_call(
        close_kernel,
        out_shape=(
            jax.ShapeDtypeStruct((ROWS, WIDE), BF16),
            jax.ShapeDtypeStruct((1, ROWS), F32),
        ),
        in_specs=[vm] * 4,
        out_specs=(hbm, hbm),
        scratch_shapes=[pltpu.VMEM((1, ROWS), F32), pltpu.SemaphoreType.DMA((2,))],
        compiler_params=pltpu.CompilerParams(vmem_limit_bytes=36 * 1024 * 1024),
    )(*arrays)


def solution(mesh):
    def local(
        queries, key_vec, values, out_gate, beta_logit, decay_gate, decay_exp,
        norm_gain, out_weight, router_weight, old_scores,
    ):
        arrays = (
            decay_exp, norm_gain.reshape(1, L), queries, key_vec, values, beta_logit, decay_gate,
            out_gate, out_weight, router_weight, old_scores,
        )
        layer_out, div = close(*layer(*(pltpu.with_memory_space_constraint(a, pltpu.HBM) for a in arrays)))
        return layer_out, div.reshape(ROWS)

    placed = (
        P("ctx", "head"), P("ctx", "head"), P("ctx", "head"), P("ctx", "head"), P("head", "ctx"),
        P("head", "ctx"), P("head"), P(), P("head", None), P(), P(("ctx", "head"), None),
    )
    return jax.shard_map(
        local,
        mesh=mesh,
        in_specs=placed,
        out_specs=(P(("ctx", "head"), None), P(("ctx", "head"))),
        check_vma=False,
    )
```

```python
import jax
import jax.numpy as jnp
from jax import lax
from jax.experimental import pallas as pl
from jax.experimental.pallas import tpu as pltpu
from jax.sharding import PartitionSpec as P

F32 = jnp.float32
BF16 = jnp.bfloat16
L = 128
EPS = 1e-6


def mm(a, b):
    return jnp.dot(a, b, preferred_element_type=F32)


def split(x):
    hi = x.astype(BF16)
    return hi, (x - hi.astype(F32)).astype(BF16)


def mm_wide(a, b):
    ah, al = split(a)
    bh, bl = split(b)
    row = jnp.concatenate([bh, bl], axis=1)
    r = mm(jnp.concatenate([ah, al], axis=1), jnp.concatenate([row, row], axis=0))
    n = b.shape[1]
    return r[:, :n] + r[:, n:]


def four_products(a, b):
    row = jnp.concatenate(b, axis=1)
    r = mm(jnp.concatenate(a, axis=1), jnp.concatenate([row, row], axis=0))
    return r[:, :L] + r[:, L:]


def mm_three(a, b):
    ah, al = split(a)
    bh, bl = split(b)
    return mm(jnp.concatenate([ah, al, ah], axis=1), jnp.concatenate([bh, bh, bl], axis=0))


def mm_exact_right(a, b16):
    ah, al = split(a)
    return mm(jnp.concatenate([ah, al], axis=1), jnp.concatenate([b16, b16], axis=0))


def odd_rows(x, s):
    if s == 64:
        return x[64:]
    return jnp.concatenate([x[i : i + s] for i in range(s, L, 2 * s)], axis=0)


def even_rows(x, s):
    return jnp.concatenate([x[i : i + s] for i in range(0, L, 2 * s)], axis=0)


def interleave(even, odd, s):
    parts = []
    for i in range(0, L // 2, s):
        parts += [even[i : i + s], odd[i : i + s]]
    return jnp.concatenate(parts, axis=0)


def weave(even, odd, s):
    parts = []
    for n, i in enumerate(range(0, L, 2 * s)):
        parts += [even[i : i + s], odd[n * s : (n + 1) * s]]
    return jnp.concatenate(parts, axis=0)


def unit_lower_inverse(systems):
    lane8 = lax.broadcasted_iota(jnp.int32, (8, L), 1)
    row8 = lax.broadcasted_iota(jnp.int32, (8, L), 0)
    place = lane8 // 8
    bands = []
    for a in systems:
        band = jnp.zeros((8, L), F32)
        for b in range(L // 8):
            band = jnp.where(place == b, a[8 * b : 8 * b + 8], band)
        bands.append(band)
    start = jnp.where(lane8 % 8 == row8, 1.0, 0.0).astype(F32)
    solved = [start for _ in systems]
    for m in range(7):
        index = place * 8 + m
        spread = [jnp.take_along_axis(band, index, axis=1) for band in bands]
        solved = [r - s * r[m : m + 1] for r, s in zip(solved, spread)]
    row = lax.broadcasted_iota(jnp.int32, (L, L), 0)
    lane = lax.broadcasted_iota(jnp.int32, (L, L), 1)
    same = row // 8 == lane // 8
    inverses = [jnp.where(same, jnp.concatenate([r] * (L // 8), axis=0), 0.0) for r in solved]
    halves = [[t] for t in inverses]
    twos = range(0, len(systems), 2)
    for s in (8, 16, 32, 64):
        below = odd_rows(row // s, s) == odd_rows(lane // s, s) + 1
        lower = []
        for n in twos:
            one, two = (jnp.where(below, odd_rows(a, s), 0.0) for a in systems[n : n + 2])
            left = split(jnp.concatenate([one, pltpu.roll(two, s, 1)], axis=0))
            right = [interleave(even_rows(p, s), even_rows(q, s), s) for p, q in zip(halves[n], halves[n + 1])]
            lower.append(four_products(left, right if s > 8 else split(right[0])))
        change = []
        for n, y in zip(twos, lower):
            one, two = (odd_rows(t, s) for t in inverses[n : n + 2])
            left = split(jnp.concatenate([one, pltpu.roll(two, L - s, 1)], axis=0))
            if s > 8:
                right = [interleave(p[L // 2 :], p[: L // 2], s) for p in split(y)]
            else:
                right = split(interleave(y[L // 2 :], y[: L // 2], s))
            change.append(four_products(left, right))
        fresh = []
        for n, c in zip(twos, change):
            fresh += [odd_rows(inverses[n], s) - c[: L // 2], odd_rows(inverses[n + 1], s) - c[L // 2 :]]
        inverses = [weave(t, f, s) for t, f in zip(inverses, fresh)]
        if s == 8:
            halves = [split(t) for t in inverses]
        elif s < 64:
            halves = [[weave(p, q, s) for p, q in zip(half, split(f))] for half, f in zip(halves, fresh)]
    return inverses


ROWS = 64
WIDE = 2048
HALF = WIDE // 2
QUARTER = WIDE // 4
MESH_X = 4
MESH_Y = 4
QUAD = 4
PACK = L + 16


def to_ctx(ctx):
    return {"ctx": ctx}


def to_head(head):
    return {"head": head}


def signal(semaphore, device):
    pl.semaphore_signal(semaphore, inc=1, device_id=device, device_id_type=pl.DeviceIdType.MESH)


def remote(src, dst, send_sem, recv_sem, device):
    return pltpu.make_async_remote_copy(
        src_ref=src, dst_ref=dst, send_sem=send_sem, recv_sem=recv_sem,
        device_id=device, device_id_type=pl.DeviceIdType.MESH,
    )


def iotas():
    return lax.broadcasted_iota(jnp.int32, (L, L), 0), lax.broadcasted_iota(jnp.int32, (L, L), 1)


def decay_tables(de_ref, bl_ref, dg_ref, rows_s, cols_s):
    row = lax.broadcasted_iota(jnp.int32, (8, 512), 0)
    lane = lax.broadcasted_iota(jnp.int32, (8, 512), 1) % L
    exponent = jnp.zeros((8, 512), jnp.int32)
    for h in range(4):
        exponent = jnp.where(row % 4 == h, de_ref[h], exponent)
    rate = jnp.exp2(exponent.astype(F32)) / 16384.0
    gate = jnp.concatenate([dg_ref[...]] * 2, axis=0)
    beta = jax.nn.sigmoid(jnp.concatenate([bl_ref[...]] * 2, axis=0))
    cum = -rate * gate
    for s in (1, 2, 4, 8, 16, 32, 64):
        cum = cum + jnp.where(lane >= s, pltpu.roll(cum, s, 1), 0.0)
    growth = jnp.exp(cum)
    for b in range(4):
        tokens = slice(L * b, L * b + L)
        now = cum[:, tokens]
        last = jnp.broadcast_to(now[:, L - 1 : L], (8, L))
        parts = [now, beta[:, tokens], growth[:, tokens]]
        rows_s[b] = jnp.concatenate(parts + [jnp.exp(last)], axis=0)
        padding = [jnp.zeros((L - 32, L), F32)]
        cols_s[b] = jnp.concatenate(parts + [jnp.exp(last - now)] + padding, axis=0).T


def solve_blocks(blocks, k_ref, v_ref, rows_s, cols_s, t1_s, fade_s, b_s, d_s, values_ready):
    row, lane = iotas()
    eye = jnp.where(row == lane, 1.0, 0.0).astype(F32)
    tokens = [pl.ds(pl.multiple_of(b * L, L), L) for b in blocks]
    rows = [rows_s[b] for b in blocks]
    columns = [cols_s[b] for b in blocks]
    places = [(n, kh) for n in range(len(blocks)) for kh in range(2)]
    keys = [k_ref[tokens[n], L * kh : L * kh + L] for n, kh in places]
    keys_t = [key.T for key in keys]
    norms = [
        lax.rsqrt(jnp.sum(key.astype(F32) * key.astype(F32), axis=1, keepdims=True) + EPS) for key in keys
    ]
    grams = [mm(key, key_t) for key, key_t in zip(keys, keys_t)]
    key_rows = []
    for n, b in enumerate(blocks):
        table = jnp.where(lane == 0, norms[2 * n], jnp.where(lane == 1, norms[2 * n + 1], 0.0))
        key_rows.append(table.T)
        rows_s[b, 28:30] = key_rows[n][:2]
    spots = [(n, h) for n in range(len(blocks)) for h in range(4)]
    systems = []
    for n, h in spots:
        kh = h // 2
        fade = jnp.exp(jnp.minimum(columns[n][:, h : h + 1] - rows[n][h : h + 1], 0.0))
        fade = fade * key_rows[n][kh : kh + 1]
        fade_s[4 * blocks[n] + h] = fade
        scaled = grams[2 * n + kh] * (norms[2 * n + kh] * columns[n][:, 8 + h : 9 + h])
        systems.append(jnp.where(row > lane, scaled * fade, 0.0))
    inverses = unit_lower_inverse(systems)
    t1s = [t * rows[n][8 + h : 9 + h] for t, (n, h) in zip(inverses, spots)]
    reaches = [rows[n][16 + h : 17 + h] * key_rows[n][h // 2 : h // 2 + 1] for n, h in spots]
    for (n, h), t1, reach in zip(spots, t1s, reaches):
        t1_s[4 * blocks[n] + h] = t1
        rows_s[blocks[n], 4 + h : 5 + h] = reach
    values_ready()
    written = [mm_exact_right(t1, v_ref[tokens[n], L * h : L * h + L]) for t1, (n, h) in zip(t1s, spots)]
    widened = [
        mm_exact_right(t1 * reach, keys[2 * n + h // 2]) for t1, reach, (n, h) in zip(t1s, reaches, spots)
    ]
    changes = []
    for (n, h), u, w in zip(spots, written, widened):
        rem = columns[n][:, 24 + h : 25 + h] * norms[2 * n + h // 2]
        wh, wl = split(jnp.concatenate([u * rem, w * rem], axis=1))
        kt = keys_t[2 * n + h // 2]
        changes.append(mm(jnp.concatenate([kt, kt], axis=1), jnp.concatenate([wh, wl], axis=0)))
    for (n, h), change in zip(spots, changes):
        d_s[4 * blocks[n] + h] = change[:, :L]
        b_s[4 * blocks[n] + h] = eye * rows[n][24 + h : 25 + h] - change[:, L:]


def output_block(b, q_ref, k_ref, v_ref, rows_s, cols_s, t1_s, fade_s, state_s, out_s, map_s):
    row, lane = iotas()
    tokens = pl.ds(pl.multiple_of(b * L, L), L)
    rows, columns = rows_s[b], cols_s[b]
    keys, queries, scales, grams = [], [], [], []
    for kh in range(2):
        key = k_ref[tokens, L * kh : L * kh + L]
        query = q_ref[tokens, L * kh : L * kh + L]
        query32 = query.astype(F32)
        scales.append(lax.rsqrt(jnp.sum(query32 * query32, axis=1, keepdims=True) + EPS) * (L**-0.5))
        grams.append(mm(query, key.T))
        keys.append(key)
        queries.append(query32)
    scores = [
        jnp.where(row >= lane, grams[h // 2] * scales[h // 2] * fade_s[4 * b + h], 0.0) for h in range(4)
    ]
    reads = [mm_wide(score, t1_s[4 * b + h]) for h, score in enumerate(scores)]
    from_values = [mm_exact_right(r, v_ref[tokens, L * h : L * h + L]) for h, r in enumerate(reads)]
    from_keys = [mm_exact_right(r * rows[4 + h : 5 + h], keys[h // 2]) for h, r in enumerate(reads)]
    for h in range(4):
        lead = queries[h // 2] * (columns[:, 16 + h : 17 + h] * scales[h // 2]) - from_keys[h]
        both = mm_three(lead, state_s[4 * b + h])
        out_s[4 * b + h] = both[:, :L] + from_values[h]
        map_s[4 * b + h] = jnp.concatenate(split(both[:, L:]), axis=1)


def pack(state):
    row, lane = iotas()
    kept = state.astype(BF16)
    lost = state[:, L:] - kept[:, L:].astype(F32)
    lost = jnp.sum(jnp.where(row == lane, lost, 0.0), axis=0, keepdims=True)
    lost = jnp.broadcast_to(jnp.concatenate([jnp.zeros((1, L), F32), lost], axis=1), (PACK - L, 2 * L))
    return jnp.concatenate([kept, lost.astype(BF16)], axis=0)


def lost_diagonal(packed):
    row, lane = iotas()
    return jnp.where(row == lane, packed[L : L + 1, L:].astype(F32), 0.0)


def unpack(packed):
    state = packed[:L].astype(F32)
    return jnp.concatenate([state[:, :L], state[:, L:] + lost_diagonal(packed)], axis=1)


def after(packed, state):
    m = packed[:L, L:]
    hi, lo = split(state)
    lhs = jnp.concatenate([m, lost_diagonal(packed).astype(BF16), m], axis=1)
    moved = mm(lhs, jnp.concatenate([hi, hi, lo], axis=0))
    return moved + jnp.concatenate([packed[:L, :L].astype(F32), jnp.zeros((L, L), F32)], axis=1)


def after_state(packed, state):
    m = packed[:L, L:]
    hi, lo = split(state)
    lhs = jnp.concatenate([m, lost_diagonal(packed).astype(BF16), m], axis=1)
    return mm(lhs, jnp.concatenate([hi, hi, lo], axis=0)) + packed[:L, :L].astype(F32)


def before(state, packed):
    hi, lo = split(state[:, L:])
    lost = jnp.concatenate([jnp.zeros((L, L), F32), lost_diagonal(packed)], axis=1).astype(BF16)
    moved = mm(
        jnp.concatenate([hi, lo, hi], axis=1), jnp.concatenate([packed[:L], packed[:L], lost], axis=0)
    )
    return moved + jnp.concatenate([state[:, :L], jnp.zeros((L, L), F32)], axis=1)


def layer_kernel(
    de_hbm, gain_hbm, q_hbm, k_hbm, v_hbm, bl_hbm, dg_hbm, gate_hbm, w_hbm, router_hbm, old_hbm,
    lo_ref, logit_ref, prob_ref, part_ref,
    de_ref, gain_ref, q_ref, k_ref, v_ref, bl_ref, dg_ref, gate_ref, w_ref, w2_ref, router_ref, old_ref,
    rows_s, cols_s, t1_s, fade_s, b_s, d_s, state_s, out_s, map_s,
    packs, gath, prefix, total, zbox, acc, first_half, starts, maps_s, outbox, landed,
    gate_s, normed, nbox, ahead, own, ring1, box1, ring2, box2, ring3, box3,
    load, ys, yr, zs, zr, hs, hr, ls, lr, ws, wr, sc, rc, s1, r1, s2, r2, s3, r3,
):
    ctx = lax.axis_index("ctx")
    z, y = ctx // MESH_Y, lax.rem(ctx, MESH_Y)
    quad, zq = z // QUAD, lax.rem(z, QUAD)
    head = lax.axis_index("head")
    x, c = head // 2, lax.rem(head, 2)
    in_group = [to_ctx(z * MESH_Y + lax.rem(y + d, MESH_Y)) for d in range(1, MESH_Y)]
    right = to_head(lax.rem(x + 1, MESH_X) * 2 + c)
    left = to_head(lax.rem(x + MESH_X - 1, MESH_X) * 2 + c)
    twin = to_head(x * 2 + 1 - c)

    def at_z(other):
        return to_ctx(other * MESH_Y + y)

    loads = [
        pltpu.make_async_copy(src, dst, load.at[i])
        for i, (src, dst) in enumerate(
            (
                (de_hbm, de_ref), (bl_hbm, bl_ref), (dg_hbm, dg_ref), (k_hbm, k_ref), (v_hbm, v_ref),
                (q_hbm, q_ref), (w_hbm, w_ref), (gate_hbm, gate_ref), (gain_hbm, gain_ref),
                (router_hbm, router_ref), (old_hbm, old_ref),
            )
        )
    ]
    for copy in loads[:6]:
        copy.start()

    zbox[0] = jnp.zeros((PACK, 2 * L), BF16)
    barrier = pltpu.get_barrier_semaphore()
    for device in in_group + [right, left, twin]:
        signal(barrier, device)
    for d in range(1, QUAD):
        signal(barrier, at_z(quad * QUAD + lax.rem(zq + d, QUAD)))
    serves = ((QUAD - 1, (QUAD, QUAD + 1)), (0, (2 * QUAD - 1, 2 * QUAD - 2)))
    for end, served in serves:

        @pl.when(z == end)
        def _():
            for other in served:
                signal(barrier, at_z(other))

        for other in served:

            @pl.when(z == other)
            def _():
                signal(barrier, at_z(end))

    for copy in loads[:3]:
        copy.wait()
    decay_tables(de_ref, bl_ref, dg_ref, rows_s, cols_s)
    loads[3].wait()
    for copy in loads[6:]:
        copy.start()
    solve_blocks(range(4), k_ref, v_ref, rows_s, cols_s, t1_s, fade_s, b_s, d_s, loads[4].wait)

    row, lane = iotas()
    zero = jnp.zeros((L, L), F32)
    eye = jnp.where(row == lane, 1.0, 0.0).astype(F32)

    def step(b, h, state):
        return mm_three(b_s[4 * b + h], state) + jnp.concatenate([d_s[4 * b + h], zero], axis=1)

    early = [jnp.concatenate([d_s[h], b_s[h]], axis=1) for h in range(4)]
    late = [jnp.concatenate([d_s[8 + h], b_s[8 + h]], axis=1) for h in range(4)]
    middle = [step(1, h, early[h]) for h in range(4)]
    late = [step(3, h, late[h]) for h in range(4)]
    states = [
        mm_three(q[:, L:], p) + jnp.concatenate([q[:, :L], zero], axis=1) for p, q in zip(middle, late)
    ]
    for h, packed in enumerate([pack(state) for state in states]):
        packs[h] = packed

    peers = MESH_Y - 1 + 3 + QUAD - 1

    @pl.when(jnp.logical_or(z == 0, z == QUAD - 1))
    def _():
        pl.semaphore_wait(barrier, peers + 2)

    @pl.when(jnp.logical_and(z > 0, z < QUAD - 1))
    def _():
        pl.semaphore_wait(barrier, peers)

    @pl.when(z >= QUAD)
    def _():
        pl.semaphore_wait(barrier, peers + 1)

    firsts = [
        remote(packs.at[lax.rem(y + d, MESH_Y)], gath.at[y], ys.at[d - 1], yr.at[d - 1], in_group[d - 1])
        for d in range(1, MESH_Y)
    ]
    for i in (1, 0, 2):
        firsts[i].start()
    gath[y] = packs[y]
    loads[6].wait()
    weights = remote(w_ref, w2_ref, ws.at[0], wr.at[0], twin)
    weights.start()
    loads[5].wait()

    for h in range(4):
        state_s[h] = jnp.concatenate([zero, eye], axis=1)
        state_s[4 + h] = early[h]
        state_s[8 + h] = middle[h]
        state_s[12 + h] = step(2, h, middle[h])

    def output(b, carry):
        output_block(b, q_ref, k_ref, v_ref, rows_s, cols_s, t1_s, fade_s, state_s, out_s, map_s)
        return carry

    lax.fori_loop(0, 4, output, 0)

    for copy in firsts:
        copy.wait_recv()
    prefix[0] = unpack(gath[0])
    prefix[1] = after(gath[1], prefix[0])
    upper = after(gath[3], unpack(gath[2]))
    state = mm_three(upper[:, L:], prefix[1]) + jnp.concatenate([upper[:, :L], zero], axis=1)
    total[...] = pack(state)

    def up_copy(d):
        device = at_z(quad * QUAD + lax.rem(zq + d, QUAD))
        return remote(total, zbox.at[zq], zs.at[d - 1], zr.at[d - 1], device)

    def first_copy(d):
        part = (pl.ds(0, L), pl.ds(0, L))
        return remote(total.at[part], zbox.at[(0, *part)], zs.at[d - 1], zr.at[d - 1], at_z(d))

    def down_copy(d):
        return remote(total, zbox.at[zq], zs.at[QUAD - 1], zr.at[QUAD - 2 + d], at_z(0))

    for d in range(QUAD - 1, 0, -1):

        @pl.when(z == 0)
        def _():
            first_copy(d).start()

        @pl.when(jnp.logical_and(z > 0, zq + d < QUAD))
        def _():
            up_copy(d).start()

        @pl.when(z == d)
        def _():
            down_copy(d).start()

    prefix[2] = after(gath[2], prefix[1])
    for copy in loads[7:]:
        copy.wait()
    gain = jnp.concatenate([gain_ref[...]] * 4, axis=1)
    for b in range(4):
        gate = gate_ref[L * b : L * b + L, :].astype(F32)
        gate_s[L * b : L * b + L, :] = gain * (gate / (1.0 + jnp.exp(-gate)))
    old_logit = old_ref[...].astype(F32) / 1024.0
    old_logp = old_logit - jnp.log(jnp.sum(jnp.exp(old_logit), axis=1, keepdims=True))
    old_prob = jnp.exp(old_logp)
    prob_ref[...] = old_prob
    part_ref[...] = jnp.broadcast_to(jnp.sum(old_prob * old_logp, axis=1, keepdims=True), (ROWS, L))

    def half_copy(i, other):
        return remote(first_half.at[0], first_half.at[1], hs.at[i], hr.at[0], at_z(other))

    @pl.when(z == QUAD - 1)
    def _():
        reach = state
        for d in range(1, QUAD - 1):
            up_copy(d).wait_recv()
            reach = before(reach, zbox[QUAD - 1 - d])
        first_copy(QUAD - 1).wait_recv()
        first_half[0] = (reach[:, :L] + mm_exact_right(reach[:, L:], zbox[0, :L, :L])).astype(BF16)
        for i, other in enumerate(serves[0][1]):
            half_copy(i, other).start()

    acc[...] = jnp.concatenate([zero, eye], axis=1)
    for d in range(1, QUAD):

        @pl.when(zq - d >= 0)
        def _():
            @pl.when(jnp.logical_and(z == d, d < QUAD - 1))
            def _():
                first_copy(d).wait_recv()

            @pl.when(jnp.logical_and(z != QUAD - 1, z != d))
            def _():
                up_copy(d).wait_recv()

            acc[...] = unpack(zbox[zq - 1]) if d == 1 else before(acc[...], zbox[zq - d])

    starts[0:L] = acc[...]
    moved = mm_three(jnp.concatenate([prefix[j, :, L:] for j in range(MESH_Y - 1)], axis=0), acc[...])
    for j in range(1, MESH_Y):
        rows = slice(L * j, L * j + L)
        starts[rows, :L] = moved[L * (j - 1) : L * j, :L] + prefix[j - 1, :, :L]
        starts[rows, L:] = moved[L * (j - 1) : L * j, L:]

    @pl.when(z < QUAD)
    def _():
        for j in range(MESH_Y):
            outbox[j] = starts[L * j : L * j + L, :L].astype(BF16)

    @pl.when(z >= QUAD)
    def _():
        maps_s[...] = jnp.concatenate(split(starts[:, L:]), axis=1)
        half_copy(0, QUAD).wait_recv()
        ended = jnp.concatenate([first_half[1], first_half[1]], axis=0)
        for j in range(MESH_Y):
            rows = slice(L * j, L * j + L)
            outbox[j] = (starts[rows, :L] + mm(maps_s[rows], ended)).astype(BF16)
    lasts = [
        remote(outbox.at[lax.rem(y + d, MESH_Y)], landed.at[y], ls.at[d - 1], lr.at[d - 1], in_group[d - 1])
        for d in range(1, MESH_Y)
    ]
    for i in (1, 0, 2):
        lasts[i].start()
    landed[y] = outbox[y]

    @pl.when(z == 0)
    def _():
        ended = state[:, :L]
        for d in range(1, QUAD):
            down_copy(d).wait_recv()
            ended = after_state(zbox[d], ended)
        first_half[0] = ended.astype(BF16)
        for i, other in enumerate(serves[1][1]):
            half_copy(i, other).start()

    weights.wait_recv()
    for copy in lasts:
        copy.wait_recv()

    order = [lax.rem(x + d, MESH_X) for d in (2, 1, 3, 0)]

    def send(src, dst, ssem, rsem, device):
        copy = remote(src, dst, ssem, rsem, device)
        copy.start()
        return copy

    def norm(i):
        rows = pl.ds(pl.multiple_of(order[i] * L, L), L)
        attended = [
            out_s[4 * order[i] + h] + mm(map_s[4 * order[i] + h], landed_twice[h]) for h in range(4)
        ]
        scales = [lax.rsqrt(jnp.mean(a * a, axis=1, keepdims=True) + EPS) for a in attended]
        parts = [
            (a * s * gate_s[rows, L * h : L * h + L]).astype(BF16)
            for h, (a, s) in enumerate(zip(attended, scales))
        ]
        normed[i] = jnp.concatenate(parts, axis=1)
        rows = pl.ds(pl.multiple_of((1 - c) * ROWS, ROWS), ROWS)
        return send(normed.at[i, rows], nbox.at[i], sc.at[i], rc.at[i], twin)

    def mine(i):
        return normed[i, pl.ds(pl.multiple_of(c * ROWS, ROWS), ROWS), :]

    landed_twice = [jnp.concatenate([landed[h], landed[h]], axis=0) for h in range(4)]
    near, far = slice(0, HALF), slice(HALF, WIDE)
    quarters = [slice(QUARTER * n, QUARTER * n + QUARTER) for n in range(4)]
    swaps = [norm(0)]
    swaps[0].wait_recv()
    first = [None] * 4
    for n in (0, 2, 1, 3):
        ring1[n] = (mm(mine(0), w_ref[:, quarters[n]]) + mm(nbox[0], w2_ref[:, quarters[n]])).astype(BF16)
        first[n] = send(ring1.at[n], box1.at[n], s1.at[n], r1.at[n], right if n < 2 else left)
    swaps += [norm(i) for i in range(1, 4)]
    for swap in swaps[1:]:
        swap.wait_recv()
    my_rows = jnp.concatenate([mine(1), mine(2), mine(3)], axis=0)
    twin_rows = jnp.concatenate([nbox[1], nbox[2], nbox[3]], axis=0)
    own[:, far] = mm(my_rows, w_ref[:, far]) + mm(twin_rows, w2_ref[:, far])
    ring2[0] = own[0:ROWS, far].astype(BF16)
    plain = [send(ring2.at[0], box2.at[0], s2.at[0], r2.at[0], right)]
    own[:, near] = mm(my_rows, w_ref[:, near]) + mm(twin_rows, w2_ref[:, near])
    ring2[1] = own[ROWS : 2 * ROWS, near].astype(BF16)
    plain.append(send(ring2.at[1], box2.at[1], s2.at[1], r2.at[1], left))
    second = [None] * 4
    for n in (0, 2, 1, 3):
        first[n].wait_recv()
        rows = slice(0, ROWS) if n < 2 else slice(ROWS, 2 * ROWS)
        ring3[n] = (own[rows, quarters[n]] + box1[n].astype(F32)).astype(BF16)
        second[n] = send(ring3.at[n], box3.at[n], s3.at[n], r3.at[n], right if n < 2 else left)
    for copy in plain:
        copy.wait_recv()
    own[2 * ROWS :, far] = own[2 * ROWS :, far] + box2[0].astype(F32)
    own[2 * ROWS :, near] = own[2 * ROWS :, near] + box2[1].astype(F32)
    new_logit = jnp.zeros((ROWS, 512), F32)
    for n in (0, 2, 1, 3):
        second[n].wait_recv()
        done = (own[2 * ROWS :, quarters[n]] + box3[n].astype(F32)).astype(BF16)
        lo_ref[:, quarters[n]] = done
        new_logit = new_logit + mm(done, router_ref[quarters[n]])
    logit_ref[...] = new_logit

    for copy in firsts + lasts + swaps + first + plain + second + [weights]:
        copy.wait_send()
    for d in range(1, QUAD):

        @pl.when(z == 0)
        def _():
            first_copy(d).wait_send()

        @pl.when(jnp.logical_and(z > 0, zq + d < QUAD))
        def _():
            up_copy(d).wait_send()

        @pl.when(z == d)
        def _():
            down_copy(d).wait_send()

    for end, served in serves:

        @pl.when(z == end)
        def _():
            for i, other in enumerate(served):
                half_copy(i, other).wait_send()


def layer(*arrays):
    vm = pl.BlockSpec(memory_space=pltpu.VMEM)
    square = (MESH_Y, L, L)
    many = pltpu.VMEM((16, L, L), F32)
    wide = pltpu.VMEM((16, L, 2 * L), F32)
    dma = pltpu.SemaphoreType.DMA
    return pl.pallas_call(
        layer_kernel,
        out_shape=(
            jax.ShapeDtypeStruct((ROWS, WIDE), BF16),
            jax.ShapeDtypeStruct((ROWS, 512), F32),
            jax.ShapeDtypeStruct((ROWS, 512), F32),
            jax.ShapeDtypeStruct((ROWS, L), F32),
        ),
        in_specs=[pl.BlockSpec(memory_space=pltpu.HBM)] * 11,
        out_specs=(vm,) * 4,
        scratch_shapes=[
            pltpu.SMEM((4,), jnp.int32),
            pltpu.VMEM((1, L), F32),
            pltpu.VMEM((512, 256), BF16),
            pltpu.VMEM((512, 256), BF16),
            pltpu.VMEM((512, 512), BF16),
            pltpu.VMEM((4, 512), F32),
            pltpu.VMEM((4, 512), F32),
            pltpu.VMEM((512, 512), BF16),
            pltpu.VMEM((512, WIDE), BF16),
            pltpu.VMEM((512, WIDE), BF16),
            pltpu.VMEM((WIDE, 512), BF16),
            pltpu.VMEM((ROWS, 512), jnp.int32),
            pltpu.VMEM((4, 32, L), F32),
            pltpu.VMEM((4, L, L), F32),
            many, many, many, many, wide, many,
            pltpu.VMEM((16, L, 2 * L), BF16),
            pltpu.VMEM((MESH_Y, PACK, 2 * L), BF16),
            pltpu.VMEM((MESH_Y, PACK, 2 * L), BF16),
            pltpu.VMEM((MESH_Y - 1, L, 2 * L), F32),
            pltpu.VMEM((PACK, 2 * L), BF16),
            pltpu.VMEM((QUAD, PACK, 2 * L), BF16),
            pltpu.VMEM((L, 2 * L), F32),
            pltpu.VMEM((2, L, L), BF16),
            pltpu.VMEM((MESH_Y * L, 2 * L), F32),
            pltpu.VMEM((MESH_Y * L, 2 * L), BF16),
            pltpu.VMEM(square, BF16),
            pltpu.VMEM(square, BF16),
            pltpu.VMEM((512, 512), F32),
            pltpu.VMEM((4, L, 512), BF16),
            pltpu.VMEM((4, ROWS, 512), BF16),
            pltpu.VMEM((ROWS, WIDE), F32),
            pltpu.VMEM((3 * ROWS, WIDE), F32),
            pltpu.VMEM((4, ROWS, QUARTER), BF16),
            pltpu.VMEM((4, ROWS, QUARTER), BF16),
            pltpu.VMEM((2, ROWS, HALF), BF16),
            pltpu.VMEM((2, ROWS, HALF), BF16),
            pltpu.VMEM((4, ROWS, QUARTER), BF16),
            pltpu.VMEM((4, ROWS, QUARTER), BF16),
            dma((11,)),
            dma((3,)), dma((3,)),
            dma((QUAD,)), dma((2 * QUAD - 2,)),
            dma((2,)), dma((1,)),
            dma((3,)), dma((3,)),
            dma((1,)), dma((1,)),
            dma((4,)), dma((4,)), dma((4,)), dma((4,)), dma((2,)), dma((2,)), dma((4,)), dma((4,)),
        ],
        compiler_params=pltpu.CompilerParams(
            collective_id=0, has_side_effects=True, vmem_limit_bytes=36 * 1024 * 1024
        ),
    )(*arrays)


def close_kernel(lo_ref, logit_ref, prob_ref, part_ref, lo_hbm, div_hbm, div_ref, out):
    copies = [pltpu.make_async_copy(lo_ref, lo_hbm, out.at[0]), pltpu.make_async_copy(div_ref, div_hbm, out.at[1])]
    copies[0].start()
    new_logit = logit_ref[...]
    new_logp = new_logit - jnp.log(jnp.sum(jnp.exp(new_logit), axis=1, keepdims=True))
    div = part_ref[:, 0:1] - jnp.sum(prob_ref[...] * new_logp, axis=1, keepdims=True)
    div_ref[...] = jnp.broadcast_to(div, (ROWS, L)).T[0:1, :]
    copies[1].start()
    for copy in copies:
        copy.wait()


def close(*arrays):
    vm, hbm = pl.BlockSpec(memory_space=pltpu.VMEM), pl.BlockSpec(memory_space=pltpu.HBM)
    return pl.pallas_call(
        close_kernel,
        out_shape=(
            jax.ShapeDtypeStruct((ROWS, WIDE), BF16),
            jax.ShapeDtypeStruct((1, ROWS), F32),
        ),
        in_specs=[vm] * 4,
        out_specs=(hbm, hbm),
        scratch_shapes=[pltpu.VMEM((1, ROWS), F32), pltpu.SemaphoreType.DMA((2,))],
        compiler_params=pltpu.CompilerParams(vmem_limit_bytes=36 * 1024 * 1024),
    )(*arrays)


def solution(mesh):
    def local(
        queries, key_vec, values, out_gate, beta_logit, decay_gate, decay_exp,
        norm_gain, out_weight, router_weight, old_scores,
    ):
        arrays = (
            decay_exp, norm_gain.reshape(1, L), queries, key_vec, values, beta_logit, decay_gate,
            out_gate, out_weight, router_weight, old_scores,
        )
        layer_out, div = close(*layer(*(pltpu.with_memory_space_constraint(a, pltpu.HBM) for a in arrays)))
        return layer_out, div.reshape(ROWS)

    placed = (
        P("ctx", "head"), P("ctx", "head"), P("ctx", "head"), P("ctx", "head"), P("head", "ctx"),
        P("head", "ctx"), P("head"), P(), P("head", None), P(), P(("ctx", "head"), None),
    )
    return jax.shard_map(
        local,
        mesh=mesh,
        in_specs=placed,
        out_specs=(P(("ctx", "head"), None), P(("ctx", "head"))),
        check_vma=False,
    )
```

```python
import jax
import jax.numpy as jnp
from jax import lax
from jax.experimental import pallas as pl
from jax.experimental.pallas import tpu as pltpu
from jax.sharding import PartitionSpec as P

F32 = jnp.float32
BF16 = jnp.bfloat16
L = 128
EPS = 1e-6


def mm(a, b):
    return jnp.dot(a, b, preferred_element_type=F32)


def split(x):
    hi = x.astype(BF16)
    return hi, (x - hi.astype(F32)).astype(BF16)


def mm_wide(a, b):
    ah, al = split(a)
    bh, bl = split(b)
    row = jnp.concatenate([bh, bl], axis=1)
    r = mm(jnp.concatenate([ah, al], axis=1), jnp.concatenate([row, row], axis=0))
    n = b.shape[1]
    return r[:, :n] + r[:, n:]


def four_products(a, b):
    row = jnp.concatenate(b, axis=1)
    r = mm(jnp.concatenate(a, axis=1), jnp.concatenate([row, row], axis=0))
    return r[:, :L] + r[:, L:]


def mm_three(a, b):
    ah, al = split(a)
    bh, bl = split(b)
    return mm(jnp.concatenate([ah, al, ah], axis=1), jnp.concatenate([bh, bh, bl], axis=0))


def mm_exact_right(a, b16):
    ah, al = split(a)
    return mm(jnp.concatenate([ah, al], axis=1), jnp.concatenate([b16, b16], axis=0))


def odd_rows(x, s):
    if s == 64:
        return x[64:]
    return jnp.concatenate([x[i : i + s] for i in range(s, L, 2 * s)], axis=0)


def even_rows(x, s):
    return jnp.concatenate([x[i : i + s] for i in range(0, L, 2 * s)], axis=0)


def interleave(even, odd, s):
    parts = []
    for i in range(0, L // 2, s):
        parts += [even[i : i + s], odd[i : i + s]]
    return jnp.concatenate(parts, axis=0)


def weave(even, odd, s):
    parts = []
    for n, i in enumerate(range(0, L, 2 * s)):
        parts += [even[i : i + s], odd[n * s : (n + 1) * s]]
    return jnp.concatenate(parts, axis=0)


def unit_lower_inverse(systems):
    lane8 = lax.broadcasted_iota(jnp.int32, (8, L), 1)
    row8 = lax.broadcasted_iota(jnp.int32, (8, L), 0)
    place = lane8 // 8
    bands = []
    for a in systems:
        band = jnp.zeros((8, L), F32)
        for b in range(L // 8):
            band = jnp.where(place == b, a[8 * b : 8 * b + 8], band)
        bands.append(band)
    start = jnp.where(lane8 % 8 == row8, 1.0, 0.0).astype(F32)
    solved = [start for _ in systems]
    for m in range(7):
        index = place * 8 + m
        spread = [jnp.take_along_axis(band, index, axis=1) for band in bands]
        solved = [r - s * r[m : m + 1] for r, s in zip(solved, spread)]
    row = lax.broadcasted_iota(jnp.int32, (L, L), 0)
    lane = lax.broadcasted_iota(jnp.int32, (L, L), 1)
    same = row // 8 == lane // 8
    inverses = [jnp.where(same, jnp.concatenate([r] * (L // 8), axis=0), 0.0) for r in solved]
    halves = [[t] for t in inverses]
    twos = range(0, len(systems), 2)
    for s in (8, 16, 32, 64):
        below = odd_rows(row // s, s) == odd_rows(lane // s, s) + 1
        lower = []
        for n in twos:
            one, two = (jnp.where(below, odd_rows(a, s), 0.0) for a in systems[n : n + 2])
            left = split(jnp.concatenate([one, pltpu.roll(two, s, 1)], axis=0))
            right = [interleave(even_rows(p, s), even_rows(q, s), s) for p, q in zip(halves[n], halves[n + 1])]
            lower.append(four_products(left, right if s > 8 else split(right[0])))
        change = []
        for n, y in zip(twos, lower):
            one, two = (odd_rows(t, s) for t in inverses[n : n + 2])
            left = split(jnp.concatenate([one, pltpu.roll(two, L - s, 1)], axis=0))
            if s > 8:
                right = [interleave(p[L // 2 :], p[: L // 2], s) for p in split(y)]
            else:
                right = split(interleave(y[L // 2 :], y[: L // 2], s))
            change.append(four_products(left, right))
        fresh = []
        for n, c in zip(twos, change):
            fresh += [odd_rows(inverses[n], s) - c[: L // 2], odd_rows(inverses[n + 1], s) - c[L // 2 :]]
        inverses = [weave(t, f, s) for t, f in zip(inverses, fresh)]
        if s == 8:
            halves = [split(t) for t in inverses]
        elif s < 64:
            halves = [[weave(p, q, s) for p, q in zip(half, split(f))] for half, f in zip(halves, fresh)]
    return inverses


ROWS = 64
WIDE = 2048
HALF = WIDE // 2
QUARTER = WIDE // 4
MESH_X = 4
MESH_Y = 4
QUAD = 4
PACK = L + 16


def to_ctx(ctx):
    return {"ctx": ctx}


def to_head(head):
    return {"head": head}


def signal(semaphore, device):
    pl.semaphore_signal(semaphore, inc=1, device_id=device, device_id_type=pl.DeviceIdType.MESH)


def remote(src, dst, send_sem, recv_sem, device):
    return pltpu.make_async_remote_copy(
        src_ref=src, dst_ref=dst, send_sem=send_sem, recv_sem=recv_sem,
        device_id=device, device_id_type=pl.DeviceIdType.MESH,
    )


def iotas():
    return lax.broadcasted_iota(jnp.int32, (L, L), 0), lax.broadcasted_iota(jnp.int32, (L, L), 1)


def decay_tables(de_ref, bl_ref, dg_ref, rows_s, cols_s):
    row = lax.broadcasted_iota(jnp.int32, (8, 512), 0)
    lane = lax.broadcasted_iota(jnp.int32, (8, 512), 1) % L
    exponent = jnp.zeros((8, 512), jnp.int32)
    for h in range(4):
        exponent = jnp.where(row % 4 == h, de_ref[h], exponent)
    rate = jnp.exp2(exponent.astype(F32)) / 16384.0
    gate = jnp.concatenate([dg_ref[...]] * 2, axis=0)
    beta = jax.nn.sigmoid(jnp.concatenate([bl_ref[...]] * 2, axis=0))
    cum = -rate * gate
    for s in (1, 2, 4, 8, 16, 32, 64):
        cum = cum + jnp.where(lane >= s, pltpu.roll(cum, s, 1), 0.0)
    growth = jnp.exp(cum)
    for b in range(4):
        tokens = slice(L * b, L * b + L)
        now = cum[:, tokens]
        last = jnp.broadcast_to(now[:, L - 1 : L], (8, L))
        parts = [now, beta[:, tokens], growth[:, tokens]]
        rows_s[b] = jnp.concatenate(parts + [jnp.exp(last)], axis=0)
        padding = [jnp.zeros((L - 32, L), F32)]
        cols_s[b] = jnp.concatenate(parts + [jnp.exp(last - now)] + padding, axis=0).T


def solve_blocks(blocks, k_ref, v_ref, rows_s, cols_s, t1_s, fade_s, b_s, d_s, values_ready):
    row, lane = iotas()
    eye = jnp.where(row == lane, 1.0, 0.0).astype(F32)
    tokens = [pl.ds(pl.multiple_of(b * L, L), L) for b in blocks]
    rows = [rows_s[b] for b in blocks]
    columns = [cols_s[b] for b in blocks]
    places = [(n, kh) for n in range(len(blocks)) for kh in range(2)]
    keys = [k_ref[tokens[n], L * kh : L * kh + L] for n, kh in places]
    keys_t = [key.T for key in keys]
    norms = [
        lax.rsqrt(jnp.sum(key.astype(F32) * key.astype(F32), axis=1, keepdims=True) + EPS) for key in keys
    ]
    grams = [mm(key, key_t) for key, key_t in zip(keys, keys_t)]
    key_rows = []
    for n, b in enumerate(blocks):
        table = jnp.where(lane == 0, norms[2 * n], jnp.where(lane == 1, norms[2 * n + 1], 0.0))
        key_rows.append(table.T)
        rows_s[b, 28:30] = key_rows[n][:2]
    spots = [(n, h) for n in range(len(blocks)) for h in range(4)]
    systems = []
    for n, h in spots:
        kh = h // 2
        fade = jnp.exp(jnp.minimum(columns[n][:, h : h + 1] - rows[n][h : h + 1], 0.0))
        fade = fade * key_rows[n][kh : kh + 1]
        fade_s[4 * blocks[n] + h] = fade
        scaled = grams[2 * n + kh] * (norms[2 * n + kh] * columns[n][:, 8 + h : 9 + h])
        systems.append(jnp.where(row > lane, scaled * fade, 0.0))
    inverses = unit_lower_inverse(systems)
    t1s = [t * rows[n][8 + h : 9 + h] for t, (n, h) in zip(inverses, spots)]
    reaches = [rows[n][16 + h : 17 + h] * key_rows[n][h // 2 : h // 2 + 1] for n, h in spots]
    for (n, h), t1, reach in zip(spots, t1s, reaches):
        t1_s[4 * blocks[n] + h] = t1
        rows_s[blocks[n], 4 + h : 5 + h] = reach
    values_ready()
    written = [mm_exact_right(t1, v_ref[tokens[n], L * h : L * h + L]) for t1, (n, h) in zip(t1s, spots)]
    widened = [
        mm_exact_right(t1 * reach, keys[2 * n + h // 2]) for t1, reach, (n, h) in zip(t1s, reaches, spots)
    ]
    changes = []
    for (n, h), u, w in zip(spots, written, widened):
        rem = columns[n][:, 24 + h : 25 + h] * norms[2 * n + h // 2]
        wh, wl = split(jnp.concatenate([u * rem, w * rem], axis=1))
        kt = keys_t[2 * n + h // 2]
        changes.append(mm(jnp.concatenate([kt, kt], axis=1), jnp.concatenate([wh, wl], axis=0)))
    for (n, h), change in zip(spots, changes):
        d_s[4 * blocks[n] + h] = change[:, :L]
        b_s[4 * blocks[n] + h] = eye * rows[n][24 + h : 25 + h] - change[:, L:]


def output_block(b, q_ref, k_ref, v_ref, rows_s, cols_s, t1_s, fade_s, state_s, out_s, map_s):
    row, lane = iotas()
    tokens = pl.ds(pl.multiple_of(b * L, L), L)
    rows, columns = rows_s[b], cols_s[b]
    keys, queries, scales, grams = [], [], [], []
    for kh in range(2):
        key = k_ref[tokens, L * kh : L * kh + L]
        query = q_ref[tokens, L * kh : L * kh + L]
        query32 = query.astype(F32)
        scales.append(lax.rsqrt(jnp.sum(query32 * query32, axis=1, keepdims=True) + EPS) * (L**-0.5))
        grams.append(mm(query, key.T))
        keys.append(key)
        queries.append(query32)
    scores = [
        jnp.where(row >= lane, grams[h // 2] * scales[h // 2] * fade_s[4 * b + h], 0.0) for h in range(4)
    ]
    reads = [mm_wide(score, t1_s[4 * b + h]) for h, score in enumerate(scores)]
    from_values = [mm_exact_right(r, v_ref[tokens, L * h : L * h + L]) for h, r in enumerate(reads)]
    from_keys = [mm_exact_right(r * rows[4 + h : 5 + h], keys[h // 2]) for h, r in enumerate(reads)]
    for h in range(4):
        lead = queries[h // 2] * (columns[:, 16 + h : 17 + h] * scales[h // 2]) - from_keys[h]
        both = mm_three(lead, state_s[4 * b + h])
        out_s[4 * b + h] = both[:, :L] + from_values[h]
        map_s[4 * b + h] = jnp.concatenate(split(both[:, L:]), axis=1)


def pack(state):
    row, lane = iotas()
    kept = state.astype(BF16)
    lost = state[:, L:] - kept[:, L:].astype(F32)
    lost = jnp.sum(jnp.where(row == lane, lost, 0.0), axis=0, keepdims=True)
    lost = jnp.broadcast_to(jnp.concatenate([jnp.zeros((1, L), F32), lost], axis=1), (PACK - L, 2 * L))
    return jnp.concatenate([kept, lost.astype(BF16)], axis=0)


def lost_diagonal(packed):
    row, lane = iotas()
    return jnp.where(row == lane, packed[L : L + 1, L:].astype(F32), 0.0)


def unpack(packed):
    state = packed[:L].astype(F32)
    return jnp.concatenate([state[:, :L], state[:, L:] + lost_diagonal(packed)], axis=1)


def after(packed, state):
    m = packed[:L, L:]
    hi, lo = split(state)
    lhs = jnp.concatenate([m, lost_diagonal(packed).astype(BF16), m], axis=1)
    moved = mm(lhs, jnp.concatenate([hi, hi, lo], axis=0))
    return moved + jnp.concatenate([packed[:L, :L].astype(F32), jnp.zeros((L, L), F32)], axis=1)


def after_state(packed, state):
    m = packed[:L, L:]
    hi, lo = split(state)
    lhs = jnp.concatenate([m, lost_diagonal(packed).astype(BF16), m], axis=1)
    return mm(lhs, jnp.concatenate([hi, hi, lo], axis=0)) + packed[:L, :L].astype(F32)


def before(state, packed):
    hi, lo = split(state[:, L:])
    lost = jnp.concatenate([jnp.zeros((L, L), F32), lost_diagonal(packed)], axis=1).astype(BF16)
    moved = mm(
        jnp.concatenate([hi, lo, hi], axis=1), jnp.concatenate([packed[:L], packed[:L], lost], axis=0)
    )
    return moved + jnp.concatenate([state[:, :L], jnp.zeros((L, L), F32)], axis=1)


def layer_kernel(
    de_hbm, gain_hbm, q_hbm, k_hbm, v_hbm, bl_hbm, dg_hbm, gate_hbm, w_hbm, router_hbm, old_hbm,
    lo_ref, logit_ref, prob_ref, part_ref,
    de_ref, gain_ref, q_ref, k_ref, v_ref, bl_ref, dg_ref, gate_ref, w_ref, w2_ref, router_ref, old_ref,
    rows_s, cols_s, t1_s, fade_s, b_s, d_s, state_s, out_s, map_s,
    packs, gath, prefix, total, zbox, acc, first_half, starts, maps_s, outbox, landed,
    gate_s, normed, nbox, ahead, own, ring1, box1, ring2, box2, ring3, box3,
    load, ys, yr, zs, zr, hs, hr, ls, lr, ws, wr, sc, rc, s1, r1, s2, r2, s3, r3,
):
    ctx = lax.axis_index("ctx")
    z, y = ctx // MESH_Y, lax.rem(ctx, MESH_Y)
    quad, zq = z // QUAD, lax.rem(z, QUAD)
    head = lax.axis_index("head")
    x, c = head // 2, lax.rem(head, 2)
    in_group = [to_ctx(z * MESH_Y + lax.rem(y + d, MESH_Y)) for d in range(1, MESH_Y)]
    right = to_head(lax.rem(x + 1, MESH_X) * 2 + c)
    left = to_head(lax.rem(x + MESH_X - 1, MESH_X) * 2 + c)
    twin = to_head(x * 2 + 1 - c)

    def at_z(other):
        return to_ctx(other * MESH_Y + y)

    loads = [
        pltpu.make_async_copy(src, dst, load.at[i])
        for i, (src, dst) in enumerate(
            (
                (de_hbm, de_ref), (bl_hbm, bl_ref), (dg_hbm, dg_ref), (k_hbm, k_ref), (v_hbm, v_ref),
                (q_hbm, q_ref), (w_hbm, w_ref), (gate_hbm, gate_ref), (gain_hbm, gain_ref),
                (router_hbm, router_ref), (old_hbm, old_ref),
            )
        )
    ]
    for copy in loads[:6]:
        copy.start()

    zbox[0] = jnp.zeros((PACK, 2 * L), BF16)
    barrier = pltpu.get_barrier_semaphore()
    for device in in_group + [right, left, twin]:
        signal(barrier, device)
    for d in range(1, QUAD):
        signal(barrier, at_z(quad * QUAD + lax.rem(zq + d, QUAD)))
    serves = ((QUAD - 1, (QUAD, QUAD + 1)), (0, (2 * QUAD - 1, 2 * QUAD - 2)))
    for end, served in serves:

        @pl.when(z == end)
        def _():
            for other in served:
                signal(barrier, at_z(other))

        for other in served:

            @pl.when(z == other)
            def _():
                signal(barrier, at_z(end))

    for copy in loads[:3]:
        copy.wait()
    decay_tables(de_ref, bl_ref, dg_ref, rows_s, cols_s)
    loads[3].wait()
    for copy in loads[6:]:
        copy.start()
    solve_blocks(range(4), k_ref, v_ref, rows_s, cols_s, t1_s, fade_s, b_s, d_s, loads[4].wait)

    row, lane = iotas()
    zero = jnp.zeros((L, L), F32)
    eye = jnp.where(row == lane, 1.0, 0.0).astype(F32)

    def step(b, h, state):
        return mm_three(b_s[4 * b + h], state) + jnp.concatenate([d_s[4 * b + h], zero], axis=1)

    early = [jnp.concatenate([d_s[h], b_s[h]], axis=1) for h in range(4)]
    late = [jnp.concatenate([d_s[8 + h], b_s[8 + h]], axis=1) for h in range(4)]
    middle = [step(1, h, early[h]) for h in range(4)]
    late = [step(3, h, late[h]) for h in range(4)]
    states = [
        mm_three(q[:, L:], p) + jnp.concatenate([q[:, :L], zero], axis=1) for p, q in zip(middle, late)
    ]
    for h, packed in enumerate([pack(state) for state in states]):
        packs[h] = packed

    peers = MESH_Y - 1 + 3 + QUAD - 1

    @pl.when(jnp.logical_or(z == 0, z == QUAD - 1))
    def _():
        pl.semaphore_wait(barrier, peers + 2)

    @pl.when(jnp.logical_and(z > 0, z < QUAD - 1))
    def _():
        pl.semaphore_wait(barrier, peers)

    @pl.when(z >= QUAD)
    def _():
        pl.semaphore_wait(barrier, peers + 1)

    firsts = [
        remote(packs.at[lax.rem(y + d, MESH_Y)], gath.at[y], ys.at[d - 1], yr.at[d - 1], in_group[d - 1])
        for d in range(1, MESH_Y)
    ]
    for i in (1, 0, 2):
        firsts[i].start()
    gath[y] = packs[y]
    loads[6].wait()
    weights = remote(w_ref, w2_ref, ws.at[0], wr.at[0], twin)
    weights.start()
    loads[5].wait()

    for h in range(4):
        state_s[h] = jnp.concatenate([zero, eye], axis=1)
        state_s[4 + h] = early[h]
        state_s[8 + h] = middle[h]
        state_s[12 + h] = step(2, h, middle[h])

    def output(b, carry):
        output_block(b, q_ref, k_ref, v_ref, rows_s, cols_s, t1_s, fade_s, state_s, out_s, map_s)
        return carry

    lax.fori_loop(0, 4, output, 0)

    for copy in firsts:
        copy.wait_recv()
    prefix[0] = unpack(gath[0])
    prefix[1] = after(gath[1], prefix[0])
    upper = after(gath[3], unpack(gath[2]))
    state = mm_three(upper[:, L:], prefix[1]) + jnp.concatenate([upper[:, :L], zero], axis=1)
    total[...] = pack(state)

    def up_copy(d):
        device = at_z(quad * QUAD + lax.rem(zq + d, QUAD))
        return remote(total, zbox.at[zq], zs.at[d - 1], zr.at[d - 1], device)

    def first_copy(d):
        part = (pl.ds(0, L), pl.ds(0, L))
        return remote(total.at[part], zbox.at[(0, *part)], zs.at[d - 1], zr.at[d - 1], at_z(d))

    def down_copy(d):
        return remote(total, zbox.at[zq], zs.at[QUAD - 1], zr.at[QUAD - 2 + d], at_z(0))

    for d in range(1, QUAD):

        @pl.when(z == 0)
        def _():
            first_copy(d).start()

        @pl.when(jnp.logical_and(z > 0, zq + d < QUAD))
        def _():
            up_copy(d).start()

        @pl.when(z == d)
        def _():
            down_copy(d).start()

    prefix[2] = after(gath[2], prefix[1])
    for copy in loads[7:]:
        copy.wait()
    gain = jnp.concatenate([gain_ref[...]] * 4, axis=1)
    for b in range(4):
        gate = gate_ref[L * b : L * b + L, :].astype(F32)
        gate_s[L * b : L * b + L, :] = gain * (gate / (1.0 + jnp.exp(-gate)))
    old_logit = old_ref[...].astype(F32) / 1024.0
    old_logp = old_logit - jnp.log(jnp.sum(jnp.exp(old_logit), axis=1, keepdims=True))
    old_prob = jnp.exp(old_logp)
    prob_ref[...] = old_prob
    part_ref[...] = jnp.broadcast_to(jnp.sum(old_prob * old_logp, axis=1, keepdims=True), (ROWS, L))

    def half_copy(i, other):
        return remote(first_half.at[0], first_half.at[1], hs.at[i], hr.at[0], at_z(other))

    @pl.when(z == QUAD - 1)
    def _():
        reach = state
        for d in range(1, QUAD - 1):
            up_copy(d).wait_recv()
            reach = before(reach, zbox[QUAD - 1 - d])
        first_copy(QUAD - 1).wait_recv()
        first_half[0] = (reach[:, :L] + mm_exact_right(reach[:, L:], zbox[0, :L, :L])).astype(BF16)
        for i, other in enumerate(serves[0][1]):
            half_copy(i, other).start()

    acc[...] = jnp.concatenate([zero, eye], axis=1)
    for d in range(1, QUAD):

        @pl.when(zq - d >= 0)
        def _():
            @pl.when(jnp.logical_and(z == d, d < QUAD - 1))
            def _():
                first_copy(d).wait_recv()

            @pl.when(jnp.logical_and(z != QUAD - 1, z != d))
            def _():
                up_copy(d).wait_recv()

            acc[...] = unpack(zbox[zq - 1]) if d == 1 else before(acc[...], zbox[zq - d])

    starts[0:L] = acc[...]
    moved = mm_three(jnp.concatenate([prefix[j, :, L:] for j in range(MESH_Y - 1)], axis=0), acc[...])
    for j in range(1, MESH_Y):
        rows = slice(L * j, L * j + L)
        starts[rows, :L] = moved[L * (j - 1) : L * j, :L] + prefix[j - 1, :, :L]
        starts[rows, L:] = moved[L * (j - 1) : L * j, L:]

    @pl.when(z < QUAD)
    def _():
        for j in range(MESH_Y):
            outbox[j] = starts[L * j : L * j + L, :L].astype(BF16)

    @pl.when(z >= QUAD)
    def _():
        maps_s[...] = jnp.concatenate(split(starts[:, L:]), axis=1)
        half_copy(0, QUAD).wait_recv()
        ended = jnp.concatenate([first_half[1], first_half[1]], axis=0)
        for j in range(MESH_Y):
            rows = slice(L * j, L * j + L)
            outbox[j] = (starts[rows, :L] + mm(maps_s[rows], ended)).astype(BF16)
    lasts = [
        remote(outbox.at[lax.rem(y + d, MESH_Y)], landed.at[y], ls.at[d - 1], lr.at[d - 1], in_group[d - 1])
        for d in range(1, MESH_Y)
    ]
    for i in (1, 0, 2):
        lasts[i].start()
    landed[y] = outbox[y]

    @pl.when(z == 0)
    def _():
        ended = state[:, :L]
        for d in range(1, QUAD):
            down_copy(d).wait_recv()
            ended = after_state(zbox[d], ended)
        first_half[0] = ended.astype(BF16)
        for i, other in enumerate(serves[1][1]):
            half_copy(i, other).start()

    weights.wait_recv()
    for copy in lasts:
        copy.wait_recv()

    order = [lax.rem(x + d, MESH_X) for d in (2, 1, 3, 0)]

    def send(src, dst, ssem, rsem, device):
        copy = remote(src, dst, ssem, rsem, device)
        copy.start()
        return copy

    def norm(i):
        rows = pl.ds(pl.multiple_of(order[i] * L, L), L)
        attended = [
            out_s[4 * order[i] + h] + mm(map_s[4 * order[i] + h], landed_twice[h]) for h in range(4)
        ]
        scales = [lax.rsqrt(jnp.mean(a * a, axis=1, keepdims=True) + EPS) for a in attended]
        parts = [
            (a * s * gate_s[rows, L * h : L * h + L]).astype(BF16)
            for h, (a, s) in enumerate(zip(attended, scales))
        ]
        normed[i] = jnp.concatenate(parts, axis=1)
        rows = pl.ds(pl.multiple_of((1 - c) * ROWS, ROWS), ROWS)
        return send(normed.at[i, rows], nbox.at[i], sc.at[i], rc.at[i], twin)

    def mine(i):
        return normed[i, pl.ds(pl.multiple_of(c * ROWS, ROWS), ROWS), :]

    landed_twice = [jnp.concatenate([landed[h], landed[h]], axis=0) for h in range(4)]
    near, far = slice(0, HALF), slice(HALF, WIDE)
    quarters = [slice(QUARTER * n, QUARTER * n + QUARTER) for n in range(4)]
    swaps = [norm(0)]
    swaps[0].wait_recv()
    first = [None] * 4
    for n in (0, 2, 1, 3):
        ring1[n] = (mm(mine(0), w_ref[:, quarters[n]]) + mm(nbox[0], w2_ref[:, quarters[n]])).astype(BF16)
        first[n] = send(ring1.at[n], box1.at[n], s1.at[n], r1.at[n], right if n < 2 else left)
    swaps += [norm(i) for i in range(1, 4)]
    for swap in swaps[1:]:
        swap.wait_recv()
    my_rows = jnp.concatenate([mine(1), mine(2), mine(3)], axis=0)
    twin_rows = jnp.concatenate([nbox[1], nbox[2], nbox[3]], axis=0)
    own[:, far] = mm(my_rows, w_ref[:, far]) + mm(twin_rows, w2_ref[:, far])
    ring2[0] = own[0:ROWS, far].astype(BF16)
    plain = [send(ring2.at[0], box2.at[0], s2.at[0], r2.at[0], right)]
    own[:, near] = mm(my_rows, w_ref[:, near]) + mm(twin_rows, w2_ref[:, near])
    ring2[1] = own[ROWS : 2 * ROWS, near].astype(BF16)
    plain.append(send(ring2.at[1], box2.at[1], s2.at[1], r2.at[1], left))
    second = [None] * 4
    for n in (0, 2, 1, 3):
        first[n].wait_recv()
        rows = slice(0, ROWS) if n < 2 else slice(ROWS, 2 * ROWS)
        ring3[n] = (own[rows, quarters[n]] + box1[n].astype(F32)).astype(BF16)
        second[n] = send(ring3.at[n], box3.at[n], s3.at[n], r3.at[n], right if n < 2 else left)
    for copy in plain:
        copy.wait_recv()
    own[2 * ROWS :, far] = own[2 * ROWS :, far] + box2[0].astype(F32)
    own[2 * ROWS :, near] = own[2 * ROWS :, near] + box2[1].astype(F32)
    new_logit = jnp.zeros((ROWS, 512), F32)
    for n in (0, 2, 1, 3):
        second[n].wait_recv()
        done = (own[2 * ROWS :, quarters[n]] + box3[n].astype(F32)).astype(BF16)
        lo_ref[:, quarters[n]] = done
        new_logit = new_logit + mm(done, router_ref[quarters[n]])
    logit_ref[...] = new_logit

    for copy in firsts + lasts + swaps + first + plain + second + [weights]:
        copy.wait_send()
    for d in range(1, QUAD):

        @pl.when(z == 0)
        def _():
            first_copy(d).wait_send()

        @pl.when(jnp.logical_and(z > 0, zq + d < QUAD))
        def _():
            up_copy(d).wait_send()

        @pl.when(z == d)
        def _():
            down_copy(d).wait_send()

    for end, served in serves:

        @pl.when(z == end)
        def _():
            for i, other in enumerate(served):
                half_copy(i, other).wait_send()


def layer(*arrays):
    vm = pl.BlockSpec(memory_space=pltpu.VMEM)
    square = (MESH_Y, L, L)
    many = pltpu.VMEM((16, L, L), F32)
    wide = pltpu.VMEM((16, L, 2 * L), F32)
    dma = pltpu.SemaphoreType.DMA
    return pl.pallas_call(
        layer_kernel,
        out_shape=(
            jax.ShapeDtypeStruct((ROWS, WIDE), BF16),
            jax.ShapeDtypeStruct((ROWS, 512), F32),
            jax.ShapeDtypeStruct((ROWS, 512), F32),
            jax.ShapeDtypeStruct((ROWS, L), F32),
        ),
        in_specs=[pl.BlockSpec(memory_space=pltpu.HBM)] * 11,
        out_specs=(vm,) * 4,
        scratch_shapes=[
            pltpu.SMEM((4,), jnp.int32),
            pltpu.VMEM((1, L), F32),
            pltpu.VMEM((512, 256), BF16),
            pltpu.VMEM((512, 256), BF16),
            pltpu.VMEM((512, 512), BF16),
            pltpu.VMEM((4, 512), F32),
            pltpu.VMEM((4, 512), F32),
            pltpu.VMEM((512, 512), BF16),
            pltpu.VMEM((512, WIDE), BF16),
            pltpu.VMEM((512, WIDE), BF16),
            pltpu.VMEM((WIDE, 512), BF16),
            pltpu.VMEM((ROWS, 512), jnp.int32),
            pltpu.VMEM((4, 32, L), F32),
            pltpu.VMEM((4, L, L), F32),
            many, many, many, many, wide, many,
            pltpu.VMEM((16, L, 2 * L), BF16),
            pltpu.VMEM((MESH_Y, PACK, 2 * L), BF16),
            pltpu.VMEM((MESH_Y, PACK, 2 * L), BF16),
            pltpu.VMEM((MESH_Y - 1, L, 2 * L), F32),
            pltpu.VMEM((PACK, 2 * L), BF16),
            pltpu.VMEM((QUAD, PACK, 2 * L), BF16),
            pltpu.VMEM((L, 2 * L), F32),
            pltpu.VMEM((2, L, L), BF16),
            pltpu.VMEM((MESH_Y * L, 2 * L), F32),
            pltpu.VMEM((MESH_Y * L, 2 * L), BF16),
            pltpu.VMEM(square, BF16),
            pltpu.VMEM(square, BF16),
            pltpu.VMEM((512, 512), F32),
            pltpu.VMEM((4, L, 512), BF16),
            pltpu.VMEM((4, ROWS, 512), BF16),
            pltpu.VMEM((ROWS, WIDE), F32),
            pltpu.VMEM((3 * ROWS, WIDE), F32),
            pltpu.VMEM((4, ROWS, QUARTER), BF16),
            pltpu.VMEM((4, ROWS, QUARTER), BF16),
            pltpu.VMEM((2, ROWS, HALF), BF16),
            pltpu.VMEM((2, ROWS, HALF), BF16),
            pltpu.VMEM((4, ROWS, QUARTER), BF16),
            pltpu.VMEM((4, ROWS, QUARTER), BF16),
            dma((11,)),
            dma((3,)), dma((3,)),
            dma((QUAD,)), dma((2 * QUAD - 2,)),
            dma((2,)), dma((1,)),
            dma((3,)), dma((3,)),
            dma((1,)), dma((1,)),
            dma((4,)), dma((4,)), dma((4,)), dma((4,)), dma((2,)), dma((2,)), dma((4,)), dma((4,)),
        ],
        compiler_params=pltpu.CompilerParams(
            collective_id=0, has_side_effects=True, vmem_limit_bytes=36 * 1024 * 1024
        ),
    )(*arrays)


def close_kernel(lo_ref, logit_ref, prob_ref, part_ref, lo_hbm, div_hbm, div_ref, out):
    copies = [pltpu.make_async_copy(lo_ref, lo_hbm, out.at[0]), pltpu.make_async_copy(div_ref, div_hbm, out.at[1])]
    copies[0].start()
    new_logit = logit_ref[...]
    new_logp = new_logit - jnp.log(jnp.sum(jnp.exp(new_logit), axis=1, keepdims=True))
    div = part_ref[:, 0:1] - jnp.sum(prob_ref[...] * new_logp, axis=1, keepdims=True)
    div_ref[...] = jnp.broadcast_to(div, (ROWS, L)).T[0:1, :]
    copies[1].start()
    for copy in copies:
        copy.wait()


def close(*arrays):
    vm, hbm = pl.BlockSpec(memory_space=pltpu.VMEM), pl.BlockSpec(memory_space=pltpu.HBM)
    return pl.pallas_call(
        close_kernel,
        out_shape=(
            jax.ShapeDtypeStruct((ROWS, WIDE), BF16),
            jax.ShapeDtypeStruct((1, ROWS), F32),
        ),
        in_specs=[vm] * 4,
        out_specs=(hbm, hbm),
        scratch_shapes=[pltpu.VMEM((1, ROWS), F32), pltpu.SemaphoreType.DMA((2,))],
        compiler_params=pltpu.CompilerParams(vmem_limit_bytes=36 * 1024 * 1024),
    )(*arrays)


def solution(mesh):
    def local(
        queries, key_vec, values, out_gate, beta_logit, decay_gate, decay_exp,
        norm_gain, out_weight, router_weight, old_scores,
    ):
        arrays = (
            decay_exp, norm_gain.reshape(1, L), queries, key_vec, values, beta_logit, decay_gate,
            out_gate, out_weight, router_weight, old_scores,
        )
        layer_out, div = close(*layer(*(pltpu.with_memory_space_constraint(a, pltpu.HBM) for a in arrays)))
        return layer_out, div.reshape(ROWS)

    placed = (
        P("ctx", "head"), P("ctx", "head"), P("ctx", "head"), P("ctx", "head"), P("head", "ctx"),
        P("head", "ctx"), P("head"), P(), P("head", None), P(), P(("ctx", "head"), None),
    )
    return jax.shard_map(
        local,
        mesh=mesh,
        in_specs=placed,
        out_specs=(P(("ctx", "head"), None), P(("ctx", "head"))),
        check_vma=False,
    )
```
